128 devices in a mesh: replica: 4 (over y), section: 8 (over x, z_lo), tensor: 4 (over z_hi, core).
Axes of the slice: x: 4, y: 4, z: 4 (z_hi: 2, z_lo: 2; z = z_hi * 2 + z_lo), core: 2. Of those that a mesh axis runs over, the one named last changes fastest.
Arguments:
- inputs: bfloat16 [4, 4, 128, 12288], P('replica', None, 'tensor'), may hold values from -0.375 to 0.375
- cotangent: bfloat16 [4, 4, 128, 12288], P('replica', None, 'tensor'), may hold values from -36 to 36
- micro_counts: int32 [4], replicated, may hold values from 1 to 4
- bounds: int32 [4, 9], replicated, may hold values from 0 to 8, as said below
- holder_down: bfloat16 [4, 8, 2, 64, 12288], P('replica', 'section'), may hold values from -0.25 to 0.25, as said below
- holder_up: bfloat16 [4, 8, 2, 64, 12288], P('replica', 'section'), may hold values from -0.25 to 0.25, as said below
- master_down: float32 [8, 64, 12288], P('section', None, ('replica', 'tensor')), may hold values from -0.25 to 0.25
- master_up: float32 [8, 64, 12288], P('section', None, ('replica', 'tensor')), may hold values from -0.25 to 0.25
- moment_down: float32 [8, 64, 12288], P('section', None, ('replica', 'tensor')), may hold values from -4 to 4
- moment_up: float32 [8, 64, 12288], P('section', None, ('replica', 'tensor')), may hold values from -4 to 4
- second_down: float32 [8, 64, 12288], P('section', None, ('replica', 'tensor')), may hold values from 0.01 to 1
- second_up: float32 [8, 64, 12288], P('section', None, ('replica', 'tensor')), may hold values from 0.01 to 1
Outputs:
- new_holder_down: bfloat16 [4, 8, 2, 64, 12288], P('replica', 'section')
- new_holder_up: bfloat16 [4, 8, 2, 64, 12288], P('replica', 'section')
- new_master_down: float32 [8, 64, 12288], P('section', None, ('replica', 'tensor'))
- new_master_up: float32 [8, 64, 12288], P('section', None, ('replica', 'tensor'))
- new_moment_down: float32 [8, 64, 12288], P('section', None, ('replica', 'tensor'))
- new_moment_up: float32 [8, 64, 12288], P('section', None, ('replica', 'tensor'))
- new_second_down: float32 [8, 64, 12288], P('section', None, ('replica', 'tensor'))
- new_second_up: float32 [8, 64, 12288], P('section', None, ('replica', 'tensor'))
The draws below stay inside these ranges and needn't reach their ends.
Inputs may be any that keep to these rules, and one draw needn't show every extreme that they name: `bounds`: each row starts at 0, never falls and ends at 8; the sections that hold layers come first, 7 to 8 of them and at least one, and their layer counts differ by at most one; a layer l held by section s satisfies s <= l <= s + 1; a section holds at most 2 layers, and some section of replica 0 holds exactly 2. `holder_down`: each used slot holds master_down's layer that lives there by bounds, rounded to bfloat16; unused slots are zeros. `holder_up`: each used slot holds master_up's layer that lives there by bounds, rounded to bfloat16; unused slots are zeros.
All inputs are finite; a program needn't handle non-finite values.
Results may differ from the reference program's by a relative error of at most 0.006.
Values may be sent and summed in bfloat16 or wider, within the bound.
A program may use at most 192 MiB of HBM per device.

```python
import math
import jax
import jax.numpy as jnp
from jax import lax

D = 12288
R = 64
MICRO = 4
LAYERS = 8
MAXL = 2
TOKMB = 128
N_REPLICA = 4
N_SECTION = 8


def layer_bounds(key):
    key = jax.random.fold_in(key, 101)
    first_key, second_key = jax.random.split(key)
    lowest = max(1, N_SECTION - 1)
    dropped = jax.random.randint(first_key, (N_REPLICA,), 0, N_SECTION - lowest + 1)
    used_count = (N_SECTION - dropped).at[0].set(lowest).astype(jnp.int32)
    per_base = LAYERS // used_count
    spare_count = LAYERS - per_base * used_count
    column = jnp.arange(N_SECTION, dtype=jnp.int32)[None, :]
    scores = jax.random.randint(second_key, (N_REPLICA, N_SECTION), 0, 1000) * N_SECTION + column
    scores = scores.at[0, 0].set(-1)
    scores = jnp.where(column < used_count[:, None], scores, 1000 * N_SECTION + N_SECTION)
    ranking = jnp.argsort(jnp.argsort(scores, axis=1, stable=True), axis=1, stable=True)
    extra = (ranking < spare_count[:, None]).astype(jnp.int32)
    per_section = jnp.where(column < used_count[:, None], per_base[:, None] + extra, 0)
    ends = jnp.cumsum(per_section, axis=1).astype(jnp.int32)
    return jnp.concatenate([jnp.zeros((N_REPLICA, 1), jnp.int32), ends], axis=1)


def master_values(key, member):
    key = jax.random.fold_in(key, 200 + member)
    first_key = jax.random.fold_in(key, 0)
    gaussian = jnp.clip(jax.random.normal(first_key, (LAYERS, R, D), jnp.float32), -5.0, 5.0)
    return gaussian * 0.05


def holder_values(key, member):
    master = master_values(key, member)
    bounds = layer_bounds(key)
    slot_ids = jnp.arange(MAXL, dtype=jnp.int32)
    layer_index = bounds[:, :N_SECTION, None] + slot_ids[None, None, :]
    present = layer_index < bounds[:, 1:, None]
    picked = jnp.take(master, jnp.clip(layer_index, 0, LAYERS - 1), axis=0)
    return jnp.where(present[..., None, None], picked, 0.0)


def draw_bounds(key, part):
    return layer_bounds(key)


def draw_master_down(key, part):
    return master_values(key, 1)


def draw_master_up(key, part):
    return master_values(key, 2)


def draw_holder_down(key, part):
    return holder_values(key, 1).astype(jnp.bfloat16)


def draw_holder_up(key, part):
    return holder_values(key, 2).astype(jnp.bfloat16)


def draw_inputs(key, part):
    key = jax.random.fold_in(key, 7)
    subkeys = jax.random.split(key, 3)
    extent = (N_REPLICA, MICRO, TOKMB, D)
    row_scale = jnp.exp(jax.random.uniform(subkeys[1], (N_REPLICA, MICRO, TOKMB, 1), jnp.float32, 0.0, 2.3026))
    column = jnp.exp(jax.random.uniform(subkeys[2], (1, 1, 1, D), jnp.float32, 0.0, 2.3026))
    values_base = jnp.clip(jax.random.normal(subkeys[0], extent, jnp.float32), -6.0, 6.0)
    return (values_base * row_scale * column / 1600.0).astype(jnp.bfloat16)


def touch_ends(array, key, least, high):
    longest = array.shape.index(max(array.shape))
    spots = []
    for shift in (0, 1):
        where = [jax.random.randint(jax.random.fold_in(key, axis), (), 0, length) for axis, length in enumerate(array.shape)]
        where[longest] = (where[longest] + shift) % array.shape[longest]
        spots.append(tuple(where))
    return array.at[spots[0]].set(least).at[spots[1]].set(high)


def block_levels(rng, shape, shards, smallest, top_value):
    def one(position, blocks):
        heights = jax.random.uniform(jax.random.fold_in(jax.random.fold_in(rng, 6), position), (blocks,), jnp.float32, smallest / len(shards), top_value / len(shards))
        return jnp.repeat(jnp.exp(heights), shape[position] // blocks).reshape((-1,) + (1,) * (len(shape) - position - 1))

    factor_of = one(*shards[0])
    for cut in shards[1:]:
        factor_of = factor_of * one(*cut)
    return factor_of


def scatter_about(key, shape, scale, limit, cuts=(), kind=jnp.bfloat16):
    array = scale * jax.random.normal(key, shape, jnp.float32)
    if cuts:
        array = array * block_levels(key, shape, cuts, -0.22, 0.18)
    return jnp.clip(array, -limit, limit).astype(kind)


def setup_inputs(seed: int = 0) -> dict:
    seeds = jax.random.split(jax.random.key(seed), 13)
    inputs = draw_inputs(jax.random.fold_in(seeds[12], 71), 0)
    cotangent = scatter_about(seeds[1], (N_REPLICA, MICRO, TOKMB, D), 6.0, 36.0, ((0, 4), (2, 4)))
    micro_counts = touch_ends(jax.random.randint(seeds[2], (N_REPLICA,), 1, MICRO + 1), jax.random.fold_in(seeds[2], 1), 1, MICRO).astype(jnp.int32)
    bounds = draw_bounds(jax.random.fold_in(seeds[12], 71), 0)
    holder_down = draw_holder_down(jax.random.fold_in(seeds[12], 71), 0)
    holder_up = draw_holder_up(jax.random.fold_in(seeds[12], 71), 0)
    master_down = draw_master_down(jax.random.fold_in(seeds[12], 71), 0)
    master_up = draw_master_up(jax.random.fold_in(seeds[12], 71), 0)
    moment_down = scatter_about(seeds[8], (LAYERS, R, D), 0.3, 4.0, ((0, 8), (2, 16)), jnp.float32)
    moment_up = scatter_about(seeds[9], (LAYERS, R, D), 0.3, 4.0, ((0, 8), (2, 16)), jnp.float32)
    second_down = jnp.clip(jnp.exp(math.log(1.0) - 4.6051702 * jax.random.uniform(seeds[10], (LAYERS, R, D), jnp.float32) ** block_levels(seeds[10], (LAYERS, R, D), ((0, 8), (2, 16)), -0.2, 0.2)), 0.01, 1.0)
    second_up = jnp.clip(jnp.exp(math.log(1.0) - 4.6051702 * jax.random.uniform(seeds[11], (LAYERS, R, D), jnp.float32) ** block_levels(seeds[11], (LAYERS, R, D), ((0, 8), (2, 16)), -0.2, 0.2)), 0.01, 1.0)
    return dict(inputs=inputs, cotangent=cotangent, micro_counts=micro_counts, bounds=bounds, holder_down=holder_down, holder_up=holder_up, master_down=master_down, master_up=master_up, moment_down=moment_down, moment_up=moment_up, second_down=second_down, second_up=second_up)


norm_eps = 1e-06
learn_rate = 0.01
beta_one = 0.9
beta_two = 0.95
decay_rate = 0.1
adam_eps = 1e-08
first_fix = 0.9999734386011124
second_fix = 0.9940794707796659

def layer_forward(hidden, down_w, up_w):
    features = hidden.shape[-1]
    ranks = down_w.shape[0]
    widened = hidden.astype(jnp.float32)
    inverse = lax.rsqrt(lax.optimization_barrier(jnp.mean(widened * widened, axis=-1, keepdims=True)) + norm_eps)
    normed = (widened * inverse).astype(jnp.bfloat16)
    projected = lax.dot_general(normed, down_w, (((1,), (1,)), ((), ())), preferred_element_type=jnp.float32) / math.sqrt(features)
    active = jax.nn.silu(projected).astype(jnp.bfloat16)
    branch = jnp.dot(active, up_w, preferred_element_type=jnp.float32) / math.sqrt(ranks)
    return (widened + branch).astype(jnp.bfloat16)

def layer_backward(hidden, down_w, up_w, incoming):
    features = hidden.shape[-1]
    ranks = down_w.shape[0]
    widened = hidden.astype(jnp.float32)
    inverse = lax.rsqrt(lax.optimization_barrier(jnp.mean(widened * widened, axis=-1, keepdims=True)) + norm_eps)
    normed = (widened * inverse).astype(jnp.bfloat16)
    projected = lax.dot_general(normed, down_w, (((1,), (1,)), ((), ())), preferred_element_type=jnp.float32) / math.sqrt(features)
    active = jax.nn.silu(projected).astype(jnp.bfloat16)
    sigmoid_u = jax.nn.sigmoid(projected)
    d_active = lax.dot_general(incoming, up_w, (((1,), (1,)), ((), ())), preferred_element_type=jnp.float32) / math.sqrt(ranks)
    d_inner = (d_active * sigmoid_u * (1.0 + projected * (1.0 - sigmoid_u))).astype(jnp.bfloat16)
    grad_up = lax.dot_general(active, incoming, (((0,), (0,)), ((), ())), preferred_element_type=jnp.float32) / math.sqrt(ranks)
    grad_down = lax.dot_general(d_inner, normed, (((0,), (0,)), ((), ())), preferred_element_type=jnp.float32) / math.sqrt(features)
    d_normed = jnp.dot(d_inner, down_w, preferred_element_type=jnp.float32) / math.sqrt(features)
    mixed = lax.optimization_barrier(jnp.mean(d_normed * widened, axis=-1, keepdims=True))
    d_wide = incoming.astype(jnp.float32) + inverse * (d_normed - widened * inverse * inverse * mixed)
    return (d_wide.astype(jnp.bfloat16), grad_down, grad_up)

def adam_update(params, moments, seconds, gradient):
    new_moments = beta_one * moments + (1.0 - beta_one) * gradient
    new_seconds = beta_two * seconds + (1.0 - beta_two) * gradient * gradient
    new_params = params - learn_rate * (new_moments / first_fix / (jnp.sqrt(new_seconds / second_fix) + adam_eps) + decay_rate * params)
    return (new_params, new_moments, new_seconds)

def to_holders(params, bounds):
    slot_ids = jnp.arange(MAXL, dtype=jnp.int32)
    layer_at = (bounds[:, :N_SECTION, None] + slot_ids[None, None, :]).astype(jnp.int32)
    present = layer_at < bounds[:, 1:, None]
    picked = params.astype(jnp.bfloat16)[jnp.clip(layer_at, 0, LAYERS - 1)]
    return jnp.where(present[..., None, None], picked, jnp.zeros_like(picked))

def reference(inputs, cotangent, micro_counts, bounds, holder_down, holder_up, master_down, master_up, moment_down, moment_up, second_down, second_up):
    layer_ids = jnp.arange(LAYERS, dtype=jnp.int32)
    grad_down = jnp.zeros((LAYERS, R, D), jnp.float32)
    grad_up = jnp.zeros((LAYERS, R, D), jnp.float32)
    for replica_at in range(N_REPLICA):
        row_bounds = bounds[replica_at]
        section_of = lax.optimization_barrier(jnp.sum((row_bounds[None, 1:] <= layer_ids[:, None]).astype(jnp.int32), axis=1)).astype(jnp.int32)
        slot_of = (layer_ids - row_bounds[section_of]).astype(jnp.int32)
        downs = holder_down[replica_at][section_of, slot_of]
        ups = holder_up[replica_at][section_of, slot_of]
        counted = micro_counts[replica_at]

        def one_micro(carry, item):
            block_in, cot_block, micro_index = item

            def forward_layer(hidden, weights):
                return (layer_forward(hidden, weights[0], weights[1]), hidden)
            _, stored = lax.scan(forward_layer, block_in, (downs, ups))
            starting = jnp.where(micro_index < counted, cot_block, jnp.zeros_like(cot_block))

            def backward_layer(incoming, pieces):
                d_hidden, g_down, g_up = layer_backward(pieces[0], pieces[1], pieces[2], incoming)
                return (d_hidden, (g_down, g_up))
            _, (g_down, g_up) = lax.scan(backward_layer, starting, (stored, downs, ups), reverse=True)
            return ((carry[0] + g_down, carry[1] + g_up), None)
        (grad_down, grad_up), _ = lax.scan(one_micro, (grad_down, grad_up), (inputs[replica_at], cotangent[replica_at], jnp.arange(MICRO, dtype=jnp.int32)))
    new_master_down, new_moment_down, new_second_down = adam_update(master_down, moment_down, second_down, grad_down)
    new_master_up, new_moment_up, new_second_up = adam_update(master_up, moment_up, second_up, grad_up)
    new_holder_down = to_holders(new_master_down, bounds)
    new_holder_up = to_holders(new_master_up, bounds)
    return (new_holder_down, new_holder_up, new_master_down, new_master_up, new_moment_down, new_moment_up, new_second_down, new_second_up)
```

```python
import functools
import math

import jax
import jax.numpy as jnp
from jax import lax
from jax.experimental import pallas as pl
from jax.experimental.pallas import tpu as pltpu
from jax.sharding import PartitionSpec as P

norm_eps = 1e-06
learn_rate = 0.01
beta_one = 0.9
beta_two = 0.95
decay_rate = 0.1
adam_eps = 1e-08
first_fix = 0.9999734386011124
second_fix = 0.9940794707796659
plane = ("replica", "tensor")


def dot_t(left, right):
    return lax.dot_general(
        left, right, (((1,), (1,)), ((), ())), preferred_element_type=jnp.float32
    )


def dot_n(left, right):
    return jnp.dot(left, right, preferred_element_type=jnp.float32)


def layers_kernel(features, tokens_per, meta, z, square, gram, coef, mixing, hb, rate, a_s, w_s, a_all):
    layers, _, tokens, wide = z.shape
    rank = wide // 2
    root = 1.0 / math.sqrt(features)
    section, counted = meta[layers], meta[layers + 1]
    row = lax.broadcasted_iota(jnp.int32, (tokens, 1), 0)
    taken = row < counted * tokens_per

    def picked(kind, layer):
        first = z[layer, kind][:, :rank]
        if layer == 0:
            return first.astype(jnp.float32)
        before = z[layer - 1, kind]
        code = meta[layer]
        other = jnp.where(code == 1, before[:, rank:], before[:, :rank])
        return jnp.where(code == 0, first, other).astype(jnp.float32)

    norm = square[...]
    state = jnp.concatenate([picked(1, l) for l in range(layers)], axis=1)
    a_all[...] = jnp.zeros_like(a_all)
    slopes, inner, rhos = [], [], []
    for l in range(layers):
        at = slice(l * rank, (l + 1) * rank)
        hb[l] = state
        rho = lax.rsqrt(jnp.maximum(norm, 0.0) * (1.0 / features) + norm_eps)
        product = picked(0, l)
        if l:
            product = product + dot_t(a_all[...], gram[l, :rank])
        u = product * (rho * root)
        sigma = jax.nn.sigmoid(u)
        active = (u * sigma * (1.0 / math.sqrt(rank))).astype(jnp.bfloat16)
        a_s[l] = active
        a_all[:, at] = active
        added = dot_n(active, gram[l, rank:])
        wide_a = active.astype(jnp.float32)
        norm = norm + jnp.sum(wide_a * (2.0 * state[:, at] + added[:, at]), axis=1, keepdims=True)
        state = state + added
        slopes.append(sigma * (1.0 + u * (1.0 - sigma)) * (1.0 / math.sqrt(rank)))
        inner.append(u)
        rhos.append(rho)
    back = jnp.concatenate(
        [jnp.where(taken, picked(2, l), 0.0) for l in range(layers)], axis=1
    )
    gamma = jnp.zeros((tokens, 1), jnp.float32)
    for l in reversed(range(layers)):
        at = slice(l * rank, (l + 1) * rank)
        e = back[:, at] * slopes[l]
        rho = rhos[l]
        w = (e * (rho * root)).astype(jnp.bfloat16)
        w_s[l] = w
        rate[l] = gamma
        c = rho * rho * jnp.sum(e * inner[l], axis=1, keepdims=True) * (1.0 / features)
        gamma = gamma + c
        if l:
            back = back + dot_n(w, gram[l, :rank]) - c * hb[l]
    own_w = w_s[section].astype(jnp.float32)
    own_a = a_s[section].astype(jnp.float32)
    own_rate = rate[section]
    nothing = jnp.zeros((tokens, rank), jnp.float32)
    left = jnp.concatenate(
        [
            jnp.concatenate([own_w, -own_rate * own_a], axis=1),
            jnp.concatenate([nothing, jnp.where(taken, own_a, 0.0)], axis=1),
        ],
        axis=0,
    )
    coef[...] = left.T.astype(jnp.bfloat16)
    pair = jnp.concatenate(
        [jnp.concatenate([own_w, nothing], axis=1), jnp.concatenate([nothing, own_a], axis=1)], axis=0
    ).T.astype(jnp.bfloat16)
    for l in range(layers):
        la = a_s[l].astype(jnp.float32)
        top = jnp.concatenate([nothing, jnp.where(l < section, la, 0.0)], axis=1)
        scaled = jnp.where(l <= section, own_rate, rate[l]) * la
        bottom = jnp.concatenate([jnp.where(l > section, w_s[l].astype(jnp.float32), 0.0), -scaled], axis=1)
        rhs = jnp.concatenate([top, bottom], axis=0).astype(jnp.bfloat16)
        mixing[:, l * wide : (l + 1) * wide] = dot_n(pair, rhs)


def run_layers(features, tokens_per, meta, z, square, gram):
    layers, _, tokens, wide = z.shape
    rank = wide // 2
    vmem = pl.BlockSpec(memory_space=pltpu.VMEM)
    return pl.pallas_call(
        functools.partial(layers_kernel, features, tokens_per),
        out_shape=(
            jax.ShapeDtypeStruct((wide, 2 * tokens), jnp.bfloat16),
            jax.ShapeDtypeStruct((wide, layers * wide), jnp.float32),
        ),
        in_specs=[pl.BlockSpec(memory_space=pltpu.SMEM), vmem, vmem, vmem],
        out_specs=(vmem, vmem),
        scratch_shapes=[
            pltpu.VMEM((layers, tokens, layers * rank), jnp.float32),
            pltpu.VMEM((layers, tokens, 1), jnp.float32),
            pltpu.VMEM((layers, tokens, rank), jnp.bfloat16),
            pltpu.VMEM((layers, tokens, rank), jnp.bfloat16),
            pltpu.VMEM((tokens, layers * rank), jnp.bfloat16),
        ],
        compiler_params=pltpu.CompilerParams(vmem_limit_bytes=32 * 2**20),
        name="layers",
    )(meta, z, square, gram)


def on_device(
    inputs, cotangent, micro_counts, bounds, holder_down, holder_up,
    master_down, master_up, moment_down, moment_up, second_down, second_up,
):
    replica_at = lax.axis_index("replica")
    section_at = lax.axis_index("section")
    layers = lax.axis_size("section")
    micros, per, features = inputs.shape[1:]
    slots, rank = holder_down.shape[2:4]
    tokens = micros * per
    first_layers = bounds[replica_at]
    layer_ids = jnp.arange(layers, dtype=jnp.int32)
    here = (first_layers[:-1] == layer_ids) & (first_layers[1:] > layer_ids)
    previous = jnp.concatenate([first_layers[:1], first_layers[:-2]])
    codes = jnp.where(here, 0, jnp.where(previous == layer_ids, 2, 1)).astype(jnp.int32)
    meta = jnp.concatenate([codes, section_at[None].astype(jnp.int32), micro_counts[replica_at][None]])

    hidden = inputs[0].reshape(tokens, features)
    last = cotangent[0].reshape(tokens, features)
    downs = holder_down[0, 0].reshape(slots * rank, features)
    ups = holder_up[0, 0].reshape(slots * rank, features)
    z = jnp.stack([dot_t(hidden, downs), dot_t(hidden, ups), dot_t(last, ups)]).astype(jnp.bfloat16)
    widened = hidden.astype(jnp.float32)
    square = jnp.sum(widened * widened, axis=1, keepdims=True)

    params = jnp.concatenate([master_down[0], master_up[0]], axis=0)
    moments = jnp.concatenate([moment_down[0], moment_up[0]], axis=0)
    seconds = jnp.concatenate([second_down[0], second_up[0]], axis=0)
    rows = lax.all_gather(params.astype(jnp.bfloat16), "section")
    z = lax.all_gather(z, "section")
    ups_rows = rows[:, rank:].reshape(layers * rank, -1)
    part = dot_t(rows[section_at], ups_rows)
    gram = lax.all_gather(lax.psum(part, plane).astype(jnp.bfloat16), "section")
    coef, mixing = run_layers(features, per, meta, z, square, gram)
    grads = dot_n(coef[:, :tokens], hidden) + dot_n(coef[:, tokens:], last)
    gradient = lax.psum_scatter(
        grads.astype(jnp.bfloat16), plane, scatter_dimension=1, tiled=True
    ).astype(jnp.float32)
    mixing = lax.psum(mixing, plane).astype(jnp.bfloat16)
    gradient = gradient + dot_n(mixing, rows.reshape(2 * layers * rank, -1))

    new_moments = beta_one * moments + (1.0 - beta_one) * gradient
    new_seconds = beta_two * seconds + (1.0 - beta_two) * gradient * gradient
    new_params = params - learn_rate * (
        new_moments / first_fix / (jnp.sqrt(new_seconds / second_fix) + adam_eps)
        + decay_rate * params
    )
    share = new_params.astype(jnp.bfloat16)
    after = lax.ppermute(share, "section", [(i, i - 1) for i in range(1, layers)])
    whole = lax.all_gather(jnp.stack([share, after]), plane, axis=2, tiled=True)
    whole = whole.reshape(2, 2, rank, features)
    first, end = first_layers[section_at], first_layers[section_at + 1]
    slot_zero = jnp.where(end > first, jnp.where(first == section_at, whole[0], whole[1]), 0)
    slot_one = jnp.where(end > first + 1, whole[1], 0)
    placed = jnp.stack([slot_zero, slot_one], axis=1)
    return (
        placed[0][None, None], placed[1][None, None],
        new_params[None, :rank], new_params[None, rank:],
        new_moments[None, :rank], new_moments[None, rank:],
        new_seconds[None, :rank], new_seconds[None, rank:],
    )


def solution(mesh):
    owned = P("section", None, ("replica", "tensor"))
    held = P("replica", "section", None, None, None)
    tokens = P("replica", None, "tensor", None)
    return jax.shard_map(
        on_device,
        mesh=mesh,
        in_specs=(tokens, tokens, P(), P(), held, held) + (owned,) * 6,
        out_specs=(held, held) + (owned,) * 6,
        check_vma=False,
    )
```

```python
import functools
import math

import jax
import jax.numpy as jnp
from jax import lax
from jax.experimental import pallas as pl
from jax.experimental.pallas import tpu as pltpu
from jax.sharding import PartitionSpec as P

norm_eps = 1e-06
learn_rate = 0.01
beta_one = 0.9
beta_two = 0.95
decay_rate = 0.1
adam_eps = 1e-08
first_fix = 0.9999734386011124
second_fix = 0.9940794707796659


def dot_t(left, right):
    return lax.dot_general(
        left, right, (((1,), (1,)), ((), ())), preferred_element_type=jnp.float32
    )


def dot_n(left, right):
    return jnp.dot(left, right, preferred_element_type=jnp.float32)


def layers_kernel(features, tokens_per, meta, z, square, gram, coef, mixing, hb, rate, a_s, w_s, a_all):
    layers, _, tokens, wide = z.shape
    rank = wide // 2
    root = 1.0 / math.sqrt(features)
    section, counted = meta[layers], meta[layers + 1]
    row = lax.broadcasted_iota(jnp.int32, (tokens, 1), 0)
    taken = row < counted * tokens_per

    def picked(kind, layer):
        first = z[layer, kind][:, :rank]
        if layer == 0:
            return first.astype(jnp.float32)
        before = z[layer - 1, kind]
        code = meta[layer]
        other = jnp.where(code == 1, before[:, rank:], before[:, :rank])
        return jnp.where(code == 0, first, other).astype(jnp.float32)

    norm = square[...]
    state = jnp.concatenate([picked(1, l) for l in range(layers)], axis=1)
    a_all[...] = jnp.zeros_like(a_all)
    slopes, inner, rhos = [], [], []
    for l in range(layers):
        at = slice(l * rank, (l + 1) * rank)
        hb[l] = state
        rho = lax.rsqrt(jnp.maximum(norm, 0.0) * (1.0 / features) + norm_eps)
        product = picked(0, l)
        if l:
            product = product + dot_t(a_all[...], gram[l, :rank])
        u = product * (rho * root)
        sigma = jax.nn.sigmoid(u)
        active = (u * sigma * (1.0 / math.sqrt(rank))).astype(jnp.bfloat16)
        a_s[l] = active
        a_all[:, at] = active
        added = dot_n(active, gram[l, rank:])
        wide_a = active.astype(jnp.float32)
        norm = norm + jnp.sum(wide_a * (2.0 * state[:, at] + added[:, at]), axis=1, keepdims=True)
        state = state + added
        slopes.append(sigma * (1.0 + u * (1.0 - sigma)) * (1.0 / math.sqrt(rank)))
        inner.append(u)
        rhos.append(rho)
    back = jnp.concatenate(
        [jnp.where(taken, picked(2, l), 0.0) for l in range(layers)], axis=1
    )
    gamma = jnp.zeros((tokens, 1), jnp.float32)
    for l in reversed(range(layers)):
        at = slice(l * rank, (l + 1) * rank)
        e = back[:, at] * slopes[l]
        rho = rhos[l]
        w = (e * (rho * root)).astype(jnp.bfloat16)
        w_s[l] = w
        rate[l] = gamma
        c = rho * rho * jnp.sum(e * inner[l], axis=1, keepdims=True) * (1.0 / features)
        gamma = gamma + c
        if l:
            back = back + dot_n(w, gram[l, :rank]) - c * hb[l]
    own_w = w_s[section].astype(jnp.float32)
    own_a = a_s[section].astype(jnp.float32)
    own_rate = rate[section]
    nothing = jnp.zeros((tokens, rank), jnp.float32)
    left = jnp.concatenate(
        [
            jnp.concatenate([own_w, -own_rate * own_a], axis=1),
            jnp.concatenate([nothing, jnp.where(taken, own_a, 0.0)], axis=1),
        ],
        axis=0,
    )
    coef[...] = left.T.astype(jnp.bfloat16)
    own_left = own_a.T.astype(jnp.bfloat16)
    own_down = own_w.T.astype(jnp.bfloat16)
    before = jnp.concatenate([jnp.where(l < section, a_s[l], jnp.zeros_like(a_s[l])) for l in range(layers)], axis=1)
    beyond = jnp.concatenate([jnp.where(l > section, w_s[l], jnp.zeros_like(w_s[l])) for l in range(layers)], axis=1)
    scaled = jnp.concatenate(
        [
            (jnp.where(l <= section, own_rate, rate[l]) * a_s[l].astype(jnp.float32)).astype(jnp.bfloat16)
            for l in range(layers)
        ],
        axis=1,
    )
    mixing[:rank] = (dot_n(own_down, before) + dot_n(own_left, beyond)).astype(jnp.bfloat16)
    mixing[rank:] = (-dot_n(own_left, scaled)).astype(jnp.bfloat16)


def run_layers(features, tokens_per, meta, z, square, gram):
    layers, _, tokens, wide = z.shape
    rank = wide // 2
    vmem = pl.BlockSpec(memory_space=pltpu.VMEM)
    return pl.pallas_call(
        functools.partial(layers_kernel, features, tokens_per),
        out_shape=(
            jax.ShapeDtypeStruct((wide, 2 * tokens), jnp.bfloat16),
            jax.ShapeDtypeStruct((wide, layers * rank), jnp.bfloat16),
        ),
        in_specs=[pl.BlockSpec(memory_space=pltpu.SMEM), vmem, vmem, vmem],
        out_specs=(vmem, vmem),
        scratch_shapes=[
            pltpu.VMEM((layers, tokens, layers * rank), jnp.float32),
            pltpu.VMEM((layers, tokens, 1), jnp.float32),
            pltpu.VMEM((layers, tokens, rank), jnp.bfloat16),
            pltpu.VMEM((layers, tokens, rank), jnp.bfloat16),
            pltpu.VMEM((tokens, layers * rank), jnp.bfloat16),
        ],
        compiler_params=pltpu.CompilerParams(vmem_limit_bytes=32 * 2**20),
        name="layers",
    )(meta, z, square, gram)


MESH = pl.DeviceIdType.MESH


def place():
    tensor = lax.axis_index("tensor")
    return lax.axis_index("replica"), lax.axis_index("section"), tensor // 2, tensor % 2


def remote(source, target, sems, at, device):
    return pltpu.make_async_remote_copy(
        src_ref=source, dst_ref=target, send_sem=sems[0].at[at], recv_sem=sems[1].at[at],
        device_id=device, device_id_type=MESH,
    )


def greet(devices):
    barrier = pltpu.get_barrier_semaphore()
    for device in devices:
        pl.semaphore_signal(barrier, inc=1, device_id=device, device_id_type=MESH)
    pl.semaphore_wait(barrier, len(devices))


def section_peers(replica, section, chip, core, sections):
    return [(replica, lax.rem(section + d, sections), chip * 2 + core) for d in range(1, sections)]


def plane_peers(replica, section, chip, core, replicas):
    found = []
    for dr in range(replicas):
        for dz in range(2):
            for dc in range(2):
                if dr or dz or dc:
                    there = lax.rem(replica + dr, replicas)
                    tensor = lax.rem(chip + dz, 2) * 2 + lax.rem(core + dc, 2)
                    found.append(((there, section, tensor), there * 4 + tensor))
    return found


def plane_sum(pieces, box, sems, me, peers):
    copies = []
    for i, (device, number) in enumerate(peers):
        copy = remote(pieces.at[number], box.at[me], sems, i, device)
        copy.start()
        copies.append(copy)
    box[me] = pieces[me]
    for copy in copies:
        copy.wait()
    total = box[0].astype(jnp.float32)
    for i in range(1, box.shape[0]):
        total = total + box[i].astype(jnp.float32)
    return total


def cut(value, pieces):
    _, height, width = pieces.shape
    across = value.shape[1] // width
    for i in range(pieces.shape[0]):
        y, x = i // across * height, i % across * width
        pieces[i] = value[y : y + height, x : x + width].astype(pieces.dtype)


def collect_kernel(replicas, sections, mine, z, rows, zs, gram, pieces, box, spread, *sems):
    replica, section, chip, core = place()
    row_sems, z_sems, sum_sems, piece_sems, plane_sems, core_sems = (sems[2 * i : 2 * i + 2] for i in range(6))
    me = replica * 4 + chip * 2 + core
    along = section_peers(replica, section, chip, core, sections)
    peers = plane_peers(replica, section, chip, core, replicas)
    greet(along + [device for device, _ in peers])
    rank = rows.shape[1]
    row_copies, z_copies = [], []
    for i, device in enumerate(along):
        row_copies.append(remote(mine.at[pl.ds(rank, rank)], rows.at[section], row_sems, i, device))
        row_copies[-1].start()
    for i, device in enumerate(along):
        z_copies.append(remote(z, zs.at[section], z_sems, i, device))
        z_copies[-1].start()
    rows[section] = mine[rank:]
    zs[section] = z[...]
    for copy in row_copies:
        copy.wait()
    part = dot_t(mine[...], rows[...].reshape(sections * rank, -1))
    cut(part, pieces)
    total = plane_sum(pieces, box, sum_sems, me, peers)
    spread[me, section] = total.astype(spread.dtype)
    copies = []
    for i, device in enumerate(along):
        copies.append(remote(spread.at[me, section], spread.at[me, section], piece_sems, i, device))
        copies[-1].start()
    for copy in copies:
        copy.wait()
    sibling = (replica, section, chip * 2 + 1 - core)
    same = [(device, number, i) for i, (device, number) in enumerate(peers) if i % 2 == 1]
    copies = []
    for i, (device, number, _) in enumerate(same):
        copies.append(remote(spread.at[me], spread.at[me], plane_sems, i, device))
        copies[-1].start()
    swaps = [remote(spread.at[me], spread.at[me], core_sems, 7, sibling)]
    swaps[0].start()
    for i, copy in enumerate(copies):
        copy.wait_recv()
        dr, dz = (i + 1) // 2, (i + 1) % 2
        source = lax.rem(replica + replicas - dr, replicas) * 4 + lax.rem(chip + dz, 2) * 2 + core
        swaps.append(remote(spread.at[source], spread.at[source], core_sems, i, sibling))
        swaps[-1].start()
    for copy in copies:
        copy.wait_send()
    for copy in swaps:
        copy.wait()
    _, _, height, width = spread.shape
    across = gram.shape[2] // width
    for i in range(spread.shape[0]):
        y, x = i // across * height, i % across * width
        gram[:, y : y + height, x : x + width] = spread[i]
    for copy in z_copies:
        copy.wait()


def dma_pairs(counts):
    return [pltpu.SemaphoreType.DMA((n,)) for n in counts for _ in range(2)]


def collect(mine, z):
    replicas, sections = lax.axis_size("replica"), lax.axis_size("section")
    wide, columns = mine.shape
    rank = wide // 2
    size = replicas * 4
    vmem = pl.BlockSpec(memory_space=pltpu.VMEM)
    height, width = 16, wide * sections * rank // size // 16
    return pl.pallas_call(
        functools.partial(collect_kernel, replicas, sections),
        out_shape=(
            jax.ShapeDtypeStruct((sections, rank, columns), jnp.bfloat16),
            jax.ShapeDtypeStruct((sections,) + z.shape, jnp.bfloat16),
            jax.ShapeDtypeStruct((sections, wide, sections * rank), jnp.bfloat16),
        ),
        in_specs=[vmem, vmem],
        out_specs=(vmem, vmem, vmem),
        scratch_shapes=[
            pltpu.VMEM((size, height, width), jnp.bfloat16),
            pltpu.VMEM((size, height, width), jnp.bfloat16),
            pltpu.VMEM((size, sections, height, width), jnp.bfloat16),
        ] + dma_pairs((sections - 1, sections - 1, size - 1, sections - 1, size // 2 - 1, size // 2)),
        compiler_params=pltpu.CompilerParams(collective_id=1, has_side_effects=True, vmem_limit_bytes=40 * 2**20),
        name="collect",
    )(mine, z)


def reduce_kernel(
    replicas, sections, grads, mixing, mine, out, mixed, rows, half, chips, inbox, pieces, box, spread, *sems
):
    replica, section, chip, core = place()
    half_sems, chip_sems, row_sems, sum_sems, spread_sems = (sems[2 * i : 2 * i + 2] for i in range(5))
    me = replica * 4 + chip * 2 + core
    along = section_peers(replica, section, chip, core, sections)
    peers = plane_peers(replica, section, chip, core, replicas)
    greet(along + [device for device, _ in peers])
    sibling = (replica, section, chip * 2 + 1 - core)
    columns = out.shape[1]
    order = [(2, 1), (2, 0), (1, 1), (3, 1), (1, 0), (3, 0), (0, 1), (0, 0)]
    there = [(lax.rem(replica + dr, replicas), lax.rem(chip + dz, 2)) for dr, dz in order]

    def block(r, z, c):
        return pl.ds(pl.multiple_of((r * 4 + z * 2 + c) * columns, 128), columns)

    halves = []
    for i, (r, z) in enumerate(there):
        halves.append(remote(grads.at[:, block(r, z, 1 - core)], half.at[i], half_sems, i, sibling))
        halves[-1].start()
    cut(mixing[...], pieces)
    small = []
    for i, (device, number) in enumerate(peers):
        small.append(remote(pieces.at[number], box.at[me], sum_sems, i, device))
        small[-1].start()
    box[me] = pieces[me]
    row_copies = []
    for i, device in enumerate(along):
        row_copies.append(remote(mine.at[pl.ds(0, mine.shape[0] // 2)], rows.at[section], row_sems, i, device))
        row_copies[-1].start()
    rows[section] = mine[: mine.shape[0] // 2]
    sends = []
    for i, (r, z) in enumerate(there):
        halves[i].wait()
        chips[i] = (
            grads[:, block(r, z, core)].astype(jnp.float32) + half[i].astype(jnp.float32)
        ).astype(chips.dtype)
        if i < len(there) - 1:
            sends.append(remote(chips.at[i], inbox.at[i], chip_sems, i, (r, section, z * 2 + core)))
            sends[-1].start()
    for copy in small:
        copy.wait()
    total = box[0].astype(jnp.float32)
    for i in range(1, box.shape[0]):
        total = total + box[i].astype(jnp.float32)
    spread[me] = total.astype(spread.dtype)
    small = []
    for i, (device, number) in enumerate(peers):
        small.append(remote(spread.at[me], spread.at[me], spread_sems, i, device))
        small[-1].start()
    out[...] = chips[len(there) - 1].astype(jnp.float32)
    for i, copy in enumerate(sends):
        copy.wait()
        out[...] += inbox[i].astype(jnp.float32)
    for copy in small:
        copy.wait()
    _, height, width = spread.shape
    across = mixed.shape[1] // width
    for i in range(spread.shape[0]):
        y, x = i // across * height, i % across * width
        mixed[y : y + height, x : x + width] = spread[i]
    for copy in row_copies:
        copy.wait()


def reduce(grads, mixing, mine):
    replicas, sections = lax.axis_size("replica"), lax.axis_size("section")
    size = replicas * 4
    wide, columns = mine.shape
    height, width = 16, mixing.size // size // 16
    vmem = pl.BlockSpec(memory_space=pltpu.VMEM)
    block = (size // 2, wide, columns)
    return pl.pallas_call(
        functools.partial(reduce_kernel, replicas, sections),
        out_shape=(
            jax.ShapeDtypeStruct((wide, columns), jnp.float32),
            jax.ShapeDtypeStruct(mixing.shape, jnp.bfloat16),
            jax.ShapeDtypeStruct((sections, wide // 2, columns), jnp.bfloat16),
        ),
        in_specs=[vmem] * 3,
        out_specs=(vmem,) * 3,
        scratch_shapes=[pltpu.VMEM(block, jnp.bfloat16)] * 3 + [pltpu.VMEM((size, height, width), jnp.bfloat16)] * 3
        + dma_pairs((size // 2, size // 2 - 1, sections - 1, size - 1, size - 1)),
        compiler_params=pltpu.CompilerParams(collective_id=2, has_side_effects=True, vmem_limit_bytes=40 * 2**20),
        name="reduce",
    )(grads, mixing, mine)


def publish_kernel(replicas, sections, share, out, shift_send, shift_recv, *sems):
    replica, section, chip, core = place()
    far_sems, core_sems = sems[:2], sems[2:]
    columns = share.shape[1]
    before = lax.rem(section + sections - 1, sections)
    after = lax.rem(section + 1, sections)
    other = 1 - chip
    up, down, across = (lax.rem(replica + d, replicas) for d in (1, replicas - 1, 2))
    tensor = chip * 2 + core
    here = (replica, section, tensor)
    sibling = (replica, section, chip * 2 + 1 - core)
    partner = (replica, section, other * 2 + core)
    above, below = (up, section, tensor), (down, section, tensor)
    greet([(replica, before, tensor), (replica, after, tensor), sibling, partner, above, below])

    def block(window, r, z):
        return out.at[window, :, pl.ds(pl.multiple_of((r * 4 + z * 2 + core) * columns, 128), columns)]

    started = {}
    def send(window, kind, r, z, device):
        copy = remote(block(window, r, z), block(window, r, z), far_sems, window * 7 + kind, device)
        copy.start()
        started[window, kind] = copy

    swaps = []

    def swap(window, r, z):
        number = len(swaps)
        copy = remote(block(window, r, z), block(window, r, z), core_sems, number, sibling)
        copy.start()
        swaps.append(copy)

    own = pl.ds(pl.multiple_of((replica * 4 + tensor) * columns, 128), columns)
    shift = pltpu.make_async_remote_copy(
        src_ref=share, dst_ref=out.at[1, :, own], send_sem=shift_send, recv_sem=shift_recv,
        device_id=(replica, before, tensor), device_id_type=MESH,
    )
    shift.start()
    out[0, :, own] = share[...]
    for window in range(2):
        if window:
            shift.wait()
        send(window, 0, replica, chip, partner)
        send(window, 1, replica, chip, above)
        send(window, 3, replica, chip, below)
        swap(window, replica, chip)
    for window in range(2):
        started[window, 0].wait_recv()
        send(window, 2, replica, other, above)
        send(window, 4, replica, other, below)
        swap(window, replica, other)
    for window in range(2):
        started[window, 1].wait_recv()
        send(window, 5, down, chip, above)
        swap(window, down, chip)
        started[window, 3].wait_recv()
        swap(window, up, chip)
    for window in range(2):
        started[window, 4].wait_recv()
        send(window, 6, up, other, below)
        swap(window, up, other)
        started[window, 2].wait_recv()
        swap(window, down, other)
    for window in range(2):
        started[window, 5].wait_recv()
        swap(window, across, chip)
        started[window, 6].wait_recv()
        swap(window, across, other)
    for copy in started.values():
        copy.wait_send()
    for copy in swaps:
        copy.wait()


def publish(share):
    replicas, sections = lax.axis_size("replica"), lax.axis_size("section")
    wide, columns = share.shape
    vmem = pl.BlockSpec(memory_space=pltpu.VMEM)
    return pl.pallas_call(
        functools.partial(publish_kernel, replicas, sections),
        out_shape=jax.ShapeDtypeStruct((2, wide, columns * replicas * 4), jnp.bfloat16),
        in_specs=[vmem],
        out_specs=vmem,
        scratch_shapes=[pltpu.SemaphoreType.DMA, pltpu.SemaphoreType.DMA] + dma_pairs((14, 16)),
        compiler_params=pltpu.CompilerParams(collective_id=3, has_side_effects=True, vmem_limit_bytes=40 * 2**20),
        name="publish",
    )(share)


def on_device(
    inputs, cotangent, micro_counts, bounds, holder_down, holder_up,
    master_down, master_up, moment_down, moment_up, second_down, second_up,
):
    replica_at = lax.axis_index("replica")
    section_at = lax.axis_index("section")
    layers = lax.axis_size("section")
    micros, per, features = inputs.shape[1:]
    slots, rank = holder_down.shape[2:4]
    tokens = micros * per
    first_layers = bounds[replica_at]
    layer_ids = jnp.arange(layers, dtype=jnp.int32)
    here = (first_layers[:-1] == layer_ids) & (first_layers[1:] > layer_ids)
    previous = jnp.concatenate([first_layers[:1], first_layers[:-2]])
    codes = jnp.where(here, 0, jnp.where(previous == layer_ids, 2, 1)).astype(jnp.int32)
    meta = jnp.concatenate([codes, section_at[None].astype(jnp.int32), micro_counts[replica_at][None]])

    hidden = inputs[0].reshape(tokens, features)
    last = cotangent[0].reshape(tokens, features)
    downs = holder_down[0, 0].reshape(slots * rank, features)
    ups = holder_up[0, 0].reshape(slots * rank, features)
    z = jnp.stack([dot_t(hidden, downs), dot_t(hidden, ups), dot_t(last, ups)]).astype(jnp.bfloat16)
    widened = hidden.astype(jnp.float32)
    square = jnp.sum(widened * widened, axis=1, keepdims=True)

    params = jnp.concatenate([master_down[0], master_up[0]], axis=0)
    moments = jnp.concatenate([moment_down[0], moment_up[0]], axis=0)
    seconds = jnp.concatenate([second_down[0], second_up[0]], axis=0)
    mine = params.astype(jnp.bfloat16)
    ups_rows, z, gram = collect(mine, z)
    coef, mixing = run_layers(features, per, meta, z, square, gram)
    grads = dot_n(coef[:, :tokens], hidden) + dot_n(coef[:, tokens:], last)
    gradient, mixed, downs_rows = reduce(grads.astype(jnp.bfloat16), mixing, mine)
    column_layer = jnp.arange(layers * rank, dtype=jnp.int32)[None] // rank
    crossing = mixed[:rank]
    ups_rows = ups_rows.reshape(layers * rank, -1)
    downs_rows = downs_rows.reshape(layers * rank, -1)
    nothing = jnp.zeros_like(crossing)
    from_ups = jnp.concatenate([jnp.where(column_layer < section_at, crossing, nothing), mixed[rank:]], axis=0)
    from_downs = jnp.concatenate([nothing, jnp.where(column_layer > section_at, crossing, nothing)], axis=0)
    gradient = gradient + dot_n(from_ups, ups_rows) + dot_n(from_downs, downs_rows)

    new_moments = beta_one * moments + (1.0 - beta_one) * gradient
    new_seconds = beta_two * seconds + (1.0 - beta_two) * gradient * gradient
    new_params = params - learn_rate * (
        new_moments / first_fix / (jnp.sqrt(new_seconds / second_fix) + adam_eps)
        + decay_rate * params
    )
    share = new_params.astype(jnp.bfloat16)
    whole = publish(share).reshape(2, 2, rank, features)
    first, end = first_layers[section_at], first_layers[section_at + 1]
    slot_zero = jnp.where(end > first, jnp.where(first == section_at, whole[0], whole[1]), 0)
    slot_one = jnp.where(end > first + 1, whole[1], 0)
    placed = jnp.stack([slot_zero, slot_one], axis=1)
    return (
        placed[0][None, None], placed[1][None, None],
        new_params[None, :rank], new_params[None, rank:],
        new_moments[None, :rank], new_moments[None, rank:],
        new_seconds[None, :rank], new_seconds[None, rank:],
    )


def solution(mesh):
    owned = P("section", None, ("replica", "tensor"))
    held = P("replica", "section", None, None, None)
    tokens = P("replica", None, "tensor", None)
    return jax.shard_map(
        on_device,
        mesh=mesh,
        in_specs=(tokens, tokens, P(), P(), held, held) + (owned,) * 6,
        out_specs=(held, held) + (owned,) * 6,
        check_vma=False,
    )
```

```python
import functools
import math

import jax
import jax.numpy as jnp
from jax import lax
from jax.experimental import pallas as pl
from jax.experimental.pallas import tpu as pltpu
from jax.sharding import PartitionSpec as P

norm_eps = 1e-06
learn_rate = 0.01
beta_one = 0.9
beta_two = 0.95
decay_rate = 0.1
adam_eps = 1e-08
first_fix = 0.9999734386011124
second_fix = 0.9940794707796659


def dot_t(left, right):
    return lax.dot_general(
        left, right, (((1,), (1,)), ((), ())), preferred_element_type=jnp.float32
    )


def dot_n(left, right):
    return jnp.dot(left, right, preferred_element_type=jnp.float32)


MESH = pl.DeviceIdType.MESH


def place():
    tensor = lax.axis_index("tensor")
    return lax.axis_index("replica"), lax.axis_index("section"), tensor // 2, tensor % 2


def remote(source, target, sems, at, device):
    return pltpu.make_async_remote_copy(
        src_ref=source, dst_ref=target, send_sem=sems[0].at[at], recv_sem=sems[1].at[at],
        device_id=device, device_id_type=MESH,
    )


def greet(devices):
    barrier = pltpu.get_barrier_semaphore()
    for device in devices:
        pl.semaphore_signal(barrier, inc=1, device_id=device, device_id_type=MESH)
    pl.semaphore_wait(barrier, len(devices))


def section_peers(replica, section, chip, core, sections):
    return [(replica, lax.rem(section + d, sections), chip * 2 + core) for d in range(1, sections)]


def plane_peers(replica, section, chip, core, replicas):
    found = []
    for dr in range(replicas):
        for dz in range(2):
            for dc in range(2):
                if dr or dz or dc:
                    there = lax.rem(replica + dr, replicas)
                    tensor = lax.rem(chip + dz, 2) * 2 + lax.rem(core + dc, 2)
                    found.append(((there, section, tensor), there * 4 + tensor))
    return found


def piece_sum(box):
    total = box[0].astype(jnp.float32)
    for i in range(1, box.shape[0]):
        total = total + box[i].astype(jnp.float32)
    return total


def cut(value, pieces):
    _, height, width = pieces.shape
    across = value.shape[1] // width
    for i in range(pieces.shape[0]):
        y, x = i // across * height, i % across * width
        pieces[i] = value[y : y + height, x : x + width].astype(pieces.dtype)


def join(spread, whole):
    height, width = spread.shape[-2:]
    across = whole.shape[-1] // width
    for i in range(spread.shape[0]):
        y, x = i // across * height, i % across * width
        whole[..., y : y + height, x : x + width] = spread[i]


def dma_pairs(counts):
    return [pltpu.SemaphoreType.DMA((n,)) for n in counts for _ in range(2)]


def decayed(params, moments, seconds, gradient):
    new_moments = beta_one * moments + (1.0 - beta_one) * gradient
    new_seconds = beta_two * seconds + (1.0 - beta_two) * gradient * gradient
    new_params = params - learn_rate * (
        new_moments / first_fix / (jnp.sqrt(new_seconds / second_fix) + adam_eps)
        + decay_rate * params
    )
    return new_params, new_moments, new_seconds


def run_layers(features, tokens_per, section, counted, codes, z, square, gram, coef, mixing, hb, rate, a_s, w_s, a_all):
    layers, _, tokens, wide = z.shape
    rank = wide // 2
    root = 1.0 / math.sqrt(features)
    row = lax.broadcasted_iota(jnp.int32, (tokens, 1), 0)
    taken = row < counted * tokens_per

    def picked(kind, layer):
        first = z[layer, kind][:, :rank]
        if layer == 0:
            return first.astype(jnp.float32)
        before = z[layer - 1, kind]
        code = codes[layer]
        other = jnp.where(code == 1, before[:, rank:], before[:, :rank])
        return jnp.where(code == 0, first, other).astype(jnp.float32)

    norm = square[...]
    state = jnp.concatenate([picked(1, l) for l in range(layers)], axis=1)
    a_all[...] = jnp.zeros_like(a_all)
    slopes, inner, rhos = [], [], []
    for l in range(layers):
        at = slice(l * rank, (l + 1) * rank)
        hb[l] = state
        rho = lax.rsqrt(jnp.maximum(norm, 0.0) * (1.0 / features) + norm_eps)
        product = picked(0, l)
        if l:
            product = product + dot_t(a_all[...], gram[l, :rank])
        u = product * (rho * root)
        sigma = jax.nn.sigmoid(u)
        active = (u * sigma * (1.0 / math.sqrt(rank))).astype(jnp.bfloat16)
        a_s[l] = active
        a_all[:, at] = active
        added = dot_n(active, gram[l, rank:])
        wide_a = active.astype(jnp.float32)
        norm = norm + jnp.sum(wide_a * (2.0 * state[:, at] + added[:, at]), axis=1, keepdims=True)
        state = state + added
        slopes.append(sigma * (1.0 + u * (1.0 - sigma)) * (1.0 / math.sqrt(rank)))
        inner.append(u)
        rhos.append(rho)
    back = jnp.concatenate(
        [jnp.where(taken, picked(2, l), 0.0) for l in range(layers)], axis=1
    )
    gamma = jnp.zeros((tokens, 1), jnp.float32)
    for l in reversed(range(layers)):
        at = slice(l * rank, (l + 1) * rank)
        e = back[:, at] * slopes[l]
        rho = rhos[l]
        w = (e * (rho * root)).astype(jnp.bfloat16)
        w_s[l] = w
        rate[l] = gamma
        c = rho * rho * jnp.sum(e * inner[l], axis=1, keepdims=True) * (1.0 / features)
        gamma = gamma + c
        if l:
            back = back + dot_n(w, gram[l, :rank]) - c * hb[l]
    own_w = w_s[section].astype(jnp.float32)
    own_a = a_s[section].astype(jnp.float32)
    own_rate = rate[section]
    nothing = jnp.zeros((tokens, rank), jnp.float32)
    left = jnp.concatenate(
        [
            jnp.concatenate([own_w, -own_rate * own_a], axis=1),
            jnp.concatenate([nothing, jnp.where(taken, own_a, 0.0)], axis=1),
        ],
        axis=0,
    )
    coef[...] = left.T.astype(jnp.bfloat16)
    own_left = own_a.T.astype(jnp.bfloat16)
    own_down = own_w.T.astype(jnp.bfloat16)
    before = jnp.concatenate([jnp.where(l < section, a_s[l], jnp.zeros_like(a_s[l])) for l in range(layers)], axis=1)
    beyond = jnp.concatenate([jnp.where(l > section, w_s[l], jnp.zeros_like(w_s[l])) for l in range(layers)], axis=1)
    scaled = jnp.concatenate(
        [
            (jnp.where(l <= section, own_rate, rate[l]) * a_s[l].astype(jnp.float32)).astype(jnp.bfloat16)
            for l in range(layers)
        ],
        axis=1,
    )
    mixing[:rank] = (dot_n(own_down, before) + dot_n(own_left, beyond)).astype(jnp.bfloat16)
    mixing[rank:] = (-dot_n(own_left, scaled)).astype(jnp.bfloat16)


def publish(replicas, sections, share, out, shift_send, shift_recv, far_sems, core_sems):
    replica, section, chip, core = place()
    columns = share.shape[1]
    before = lax.rem(section + sections - 1, sections)
    other = 1 - chip
    up, down, across = (lax.rem(replica + d, replicas) for d in (1, replicas - 1, 2))
    tensor = chip * 2 + core
    sibling = (replica, section, chip * 2 + 1 - core)
    partner = (replica, section, other * 2 + core)
    above, below = (up, section, tensor), (down, section, tensor)
    def block(window, r, z):
        return out.at[window, :, pl.ds(pl.multiple_of((r * 4 + z * 2 + core) * columns, 128), columns)]

    started = {}
    def send(window, kind, r, z, device):
        copy = remote(block(window, r, z), block(window, r, z), far_sems, window * 7 + kind, device)
        copy.start()
        started[window, kind] = copy

    swaps = []

    def swap(window, r, z):
        number = len(swaps)
        copy = remote(block(window, r, z), block(window, r, z), core_sems, number, sibling)
        copy.start()
        swaps.append(copy)

    own = pl.ds(pl.multiple_of((replica * 4 + tensor) * columns, 128), columns)
    shift = pltpu.make_async_remote_copy(
        src_ref=share, dst_ref=out.at[1, :, own], send_sem=shift_send, recv_sem=shift_recv,
        device_id=(replica, before, tensor), device_id_type=MESH,
    )
    shift.start()
    out[0, :, own] = share[...]
    for window in range(2):
        if window:
            shift.wait()
        send(window, 0, replica, chip, partner)
        send(window, 1, replica, chip, above)
        send(window, 3, replica, chip, below)
        swap(window, replica, chip)
    for window in range(2):
        started[window, 0].wait_recv()
        send(window, 2, replica, other, above)
        send(window, 4, replica, other, below)
        swap(window, replica, other)
    for window in range(2):
        started[window, 1].wait_recv()
        send(window, 5, down, chip, above)
        swap(window, down, chip)
        started[window, 3].wait_recv()
        swap(window, up, chip)
    for window in range(2):
        started[window, 4].wait_recv()
        send(window, 6, up, other, below)
        swap(window, up, other)
        started[window, 2].wait_recv()
        swap(window, down, other)
    for window in range(2):
        started[window, 5].wait_recv()
        swap(window, across, chip)
        started[window, 6].wait_recv()
        swap(window, across, other)
    for copy in started.values():
        copy.wait_send()
    for copy in swaps:
        copy.wait()


COUNTS = dict(rows=7, z=7, gram=15, piece=7, plane=7, core=8, downs=7, mix=15, mixed=15, half=8, chip=7, far=14, swap=16)


def step_kernel(
    replicas, sections, tokens_per,
    bounds, counts, hidden_hbm, last_hbm, downs_hbm, ups_hbm,
    master_down, master_up, moment_down, moment_up, second_down, second_up,
    gradient, out,
    hidden, last, weights, mine, z, acc, zs, rows, down_rows, gram, pieces, box, spread,
    coef, mixing, hb, rate, a_s, w_s, a_all, mix_pieces, mix_box, mix_spread,
    parts, half, chips, inbox, share, local, shift_send, shift_recv, *sems,
):
    sem = {name: sems[2 * i : 2 * i + 2] for i, name in enumerate(COUNTS)}
    replica, section, chip, core = place()
    tensor = chip * 2 + core
    me = replica * 4 + tensor
    rank, columns = master_down.shape
    wide = 2 * rank
    tokens, features = hidden.shape
    along = section_peers(replica, section, chip, core, sections)
    peers = plane_peers(replica, section, chip, core, replicas)
    sibling = (replica, section, chip * 2 + 1 - core)

    loads = [
        pltpu.make_async_copy(downs_hbm, weights.at[pl.ds(0, wide)], local.at[0]),
        pltpu.make_async_copy(ups_hbm, weights.at[pl.ds(wide, wide)], local.at[1]),
        pltpu.make_async_copy(hidden_hbm, hidden, local.at[2]),
        pltpu.make_async_copy(last_hbm, last, local.at[3]),
    ]
    for copy in loads:
        copy.start()
    mine[:rank] = master_down[...].astype(mine.dtype)
    mine[rank:] = master_up[...].astype(mine.dtype)
    greet(along + [device for device, _ in peers])

    row_copies = []
    for i, device in enumerate(along):
        row_copies.append(remote(mine.at[pl.ds(rank, rank)], rows.at[section], sem["rows"], i, device))
        row_copies[-1].start()
    rows[section] = mine[rank:]

    for copy in loads:
        copy.wait()
    acc[...] = jnp.zeros_like(acc)
    step = 1024

    @pl.loop(0, features // step)
    def _(i):
        at = pl.ds(pl.multiple_of(i * step, step), step)
        chunk = hidden[:, at]
        acc[:, : 2 * wide] += dot_t(chunk, weights[:, at])
        acc[:, 2 * wide : 3 * wide] += dot_t(last[:, at], weights[wide:, at])
        squares = chunk.astype(jnp.float32)
        squares = squares * squares
        folded = squares[:, :128]
        for j in range(1, step // 128):
            folded = folded + squares[:, j * 128 : (j + 1) * 128]
        acc[:, 3 * wide :] += folded

    for kind in range(3):
        z[kind] = acc[:, kind * wide : (kind + 1) * wide].astype(z.dtype)
    zs[section] = z[...]

    for copy in row_copies:
        copy.wait()
    cut(dot_t(mine[...], rows[...].reshape(sections * rank, columns)), pieces)
    copies = []
    for i, (device, number) in enumerate(peers):
        copies.append(remote(pieces.at[number], box.at[me], sem["gram"], i, device))
        copies[-1].start()
    z_copies = []
    for i, device in enumerate(along):
        z_copies.append(remote(z, zs.at[section], sem["z"], i, device))
        z_copies[-1].start()
    box[me] = pieces[me]
    for copy in copies:
        copy.wait()
    spread[me, section] = piece_sum(box).astype(spread.dtype)
    copies = []
    for i, device in enumerate(along):
        copies.append(remote(spread.at[me, section], spread.at[me, section], sem["piece"], i, device))
        copies[-1].start()
    for copy in copies:
        copy.wait()
    same = [device for i, (device, number) in enumerate(peers) if i % 2 == 1]
    copies = []
    for i, device in enumerate(same):
        copies.append(remote(spread.at[me], spread.at[me], sem["plane"], i, device))
        copies[-1].start()
    swaps = [remote(spread.at[me], spread.at[me], sem["core"], 7, sibling)]
    swaps[0].start()
    for i, copy in enumerate(copies):
        copy.wait_recv()
        dr, dz = (i + 1) // 2, (i + 1) % 2
        source = lax.rem(replica + replicas - dr, replicas) * 4 + lax.rem(chip + dz, 2) * 2 + core
        swaps.append(remote(spread.at[source], spread.at[source], sem["core"], i, sibling))
        swaps[-1].start()
    for copy in copies:
        copy.wait_send()
    for copy in z_copies:
        copy.wait()
    down_copies = []
    for i, device in enumerate(along):
        down_copies.append(remote(mine.at[pl.ds(0, rank)], down_rows.at[section], sem["downs"], i, device))
        down_copies[-1].start()
    down_rows[section] = mine[:rank]
    for copy in swaps:
        copy.wait()
    join(spread, gram)

    codes = [0]
    for l in range(1, sections):
        here = (bounds[replica, l] == l) & (bounds[replica, l + 1] > l)
        codes.append(jnp.where(here, 0, jnp.where(bounds[replica, l - 1] == l, 2, 1)))
    square = jnp.sum(acc[:, 3 * wide :], axis=1, keepdims=True)
    run_layers(
        features, tokens_per, section, counts[replica], codes, zs, square, gram, coef, mixing, hb, rate, a_s, w_s, a_all
    )

    cut(mixing[...], mix_pieces)
    mix_copies = []
    for i, (device, number) in enumerate(peers):
        mix_copies.append(remote(mix_pieces.at[number], mix_box.at[me], sem["mix"], i, device))
        mix_copies[-1].start()
    mix_box[me] = mix_pieces[me]
    order = [(2, 1), (2, 0), (1, 1), (3, 1), (1, 0), (3, 0), (0, 1), (0, 0)]
    there = [(lax.rem(replica + dr, replicas), lax.rem(chip + dz, 2)) for dr, dz in order]

    def block_gradient(r, z_at, c):
        at = pl.ds(pl.multiple_of((r * 4 + z_at * 2 + c) * columns, 128), columns)
        return dot_n(coef[:, :tokens], hidden[:, at]) + dot_n(coef[:, tokens:], last[:, at])

    halves = []
    for i, (r, z_at) in enumerate(there):
        parts[i] = block_gradient(r, z_at, 1 - core).astype(parts.dtype)
        halves.append(remote(parts.at[i], half.at[i], sem["half"], i, sibling))
        halves[-1].start()
    sends = []
    for i, (r, z_at) in enumerate(there):
        added = block_gradient(r, z_at, core)
        halves[i].wait()
        chips[i] = (added + half[i].astype(jnp.float32)).astype(chips.dtype)
        if i < len(there) - 1:
            sends.append(remote(chips.at[i], inbox.at[i], sem["chip"], i, (r, section, z_at * 2 + core)))
            sends[-1].start()
    for copy in mix_copies:
        copy.wait()
    mix_spread[me] = piece_sum(mix_box).astype(mix_spread.dtype)
    mix_copies = []
    for i, (device, number) in enumerate(peers):
        mix_copies.append(remote(mix_spread.at[me], mix_spread.at[me], sem["mixed"], i, device))
        mix_copies[-1].start()
    for copy in mix_copies:
        copy.wait()
    join(mix_spread, mixing)
    for copy in down_copies:
        copy.wait()
    layer_of = lax.broadcasted_iota(jnp.int32, (rank, sections * rank), 1) // rank
    crossing = mixing[:rank]
    nothing = jnp.zeros_like(crossing)
    ups_all = rows[...].reshape(sections * rank, columns)
    downs_all = down_rows[...].reshape(sections * rank, columns)
    gradient[:rank] = dot_n(jnp.where(layer_of < section, crossing, nothing), ups_all)
    gradient[rank:] = dot_n(mixing[rank:], ups_all) + dot_n(
        jnp.where(layer_of > section, crossing, nothing), downs_all
    )
    gradient[...] += chips[len(there) - 1].astype(jnp.float32)
    for i, copy in enumerate(sends):
        copy.wait()
        gradient[...] += inbox[i].astype(jnp.float32)
    share[:rank] = decayed(master_down[...], moment_down[...], second_down[...], gradient[:rank])[0].astype(share.dtype)
    share[rank:] = decayed(master_up[...], moment_up[...], second_up[...], gradient[rank:])[0].astype(share.dtype)
    publish(replicas, sections, share, out, shift_send, shift_recv, sem["far"], sem["swap"])


def run_step(bounds, counts, hidden, last, downs, ups, owned, tokens_per):
    replicas, sections = lax.axis_size("replica"), lax.axis_size("section")
    rank, columns = owned[0].shape
    wide, layers = 2 * rank, sections
    tokens, features = hidden.shape
    size = replicas * 4
    height, width = 16, wide * layers * rank // size // 16
    b16, f32 = jnp.bfloat16, jnp.float32
    smem, hbm, vmem = (pl.BlockSpec(memory_space=m) for m in (pltpu.SMEM, pl.ANY, pltpu.VMEM))
    piece = pltpu.VMEM((size, height, width), b16)
    block = pltpu.VMEM((size // 2, wide, columns), b16)
    return pl.pallas_call(
        functools.partial(step_kernel, replicas, sections, tokens_per),
        out_shape=(
            jax.ShapeDtypeStruct((wide, columns), f32),
            jax.ShapeDtypeStruct((2, wide, columns * size), b16),
        ),
        in_specs=[smem, smem] + [hbm] * 4 + [vmem] * 6,
        out_specs=(vmem, vmem),
        scratch_shapes=[
            pltpu.VMEM((tokens, features), b16),
            pltpu.VMEM((tokens, features), b16),
            pltpu.VMEM((2 * wide, features), b16),
            pltpu.VMEM((wide, columns), b16),
            pltpu.VMEM((3, tokens, wide), b16),
            pltpu.VMEM((tokens, 3 * wide + 128), f32),
            pltpu.VMEM((layers, 3, tokens, wide), b16),
            pltpu.VMEM((layers, rank, columns), b16),
            pltpu.VMEM((layers, rank, columns), b16),
            pltpu.VMEM((layers, wide, layers * rank), b16),
            piece,
            piece,
            pltpu.VMEM((size, sections, height, width), b16),
            pltpu.VMEM((wide, 2 * tokens), b16),
            pltpu.VMEM((wide, layers * rank), b16),
            pltpu.VMEM((layers, tokens, layers * rank), f32),
            pltpu.VMEM((layers, tokens, 1), f32),
            pltpu.VMEM((layers, tokens, rank), b16),
            pltpu.VMEM((layers, tokens, rank), b16),
            pltpu.VMEM((tokens, layers * rank), b16),
            piece,
            piece,
            piece,
            block,
            block,
            block,
            block,
            pltpu.VMEM((wide, columns), b16),
            pltpu.SemaphoreType.DMA((4,)),
            pltpu.SemaphoreType.DMA,
            pltpu.SemaphoreType.DMA,
        ]
        + dma_pairs(COUNTS.values()),
        compiler_params=pltpu.CompilerParams(collective_id=1, has_side_effects=True, vmem_limit_bytes=56 * 2**20),
        name="step",
    )(bounds, counts, hidden, last, downs, ups, *owned)


def on_device(
    inputs, cotangent, micro_counts, bounds, holder_down, holder_up,
    master_down, master_up, moment_down, moment_up, second_down, second_up,
):
    replica_at = lax.axis_index("replica")
    section_at = lax.axis_index("section")
    micros, per, features = inputs.shape[1:]
    slots, rank = holder_down.shape[2:4]
    tokens = micros * per
    first_layers = bounds[replica_at]
    owned = [array[0] for array in (master_down, master_up, moment_down, moment_up, second_down, second_up)]
    gradient, whole = run_step(
        bounds,
        micro_counts,
        inputs[0].reshape(tokens, features),
        cotangent[0].reshape(tokens, features),
        holder_down[0, 0].reshape(slots * rank, features),
        holder_up[0, 0].reshape(slots * rank, features),
        owned,
        per,
    )
    new_down = decayed(owned[0], owned[2], owned[4], gradient[:rank])
    new_up = decayed(owned[1], owned[3], owned[5], gradient[rank:])
    whole = whole.reshape(2, 2, rank, features)
    first, end = first_layers[section_at], first_layers[section_at + 1]
    slot_zero = jnp.where(end > first, jnp.where(first == section_at, whole[0], whole[1]), 0)
    slot_one = jnp.where(end > first + 1, whole[1], 0)
    placed = jnp.stack([slot_zero, slot_one], axis=1)
    news = [array[None] for pair in zip(new_down, new_up) for array in pair]
    return (placed[0][None, None], placed[1][None, None], *news)


def solution(mesh):
    owned = P("section", None, ("replica", "tensor"))
    held = P("replica", "section", None, None, None)
    tokens = P("replica", None, "tensor", None)
    return jax.shard_map(
        on_device,
        mesh=mesh,
        in_specs=(tokens, tokens, P(), P(), held, held) + (owned,) * 6,
        out_specs=(held, held) + (owned,) * 6,
        check_vma=False,
    )
```

```python
import functools
import math

import jax
import jax.numpy as jnp
from jax import lax
from jax.experimental import pallas as pl
from jax.experimental.pallas import tpu as pltpu
from jax.sharding import PartitionSpec as P

norm_eps = 1e-06
learn_rate = 0.01
beta_one = 0.9
beta_two = 0.95
decay_rate = 0.1
adam_eps = 1e-08
first_fix = 0.9999734386011124
second_fix = 0.9940794707796659


def dot_t(left, right):
    return lax.dot_general(
        left, right, (((1,), (1,)), ((), ())), preferred_element_type=jnp.float32
    )


def dot_n(left, right):
    return jnp.dot(left, right, preferred_element_type=jnp.float32)


MESH = pl.DeviceIdType.MESH


def place():
    tensor = lax.axis_index("tensor")
    return lax.axis_index("replica"), lax.axis_index("section"), tensor // 2, tensor % 2


def remote(source, target, sems, at, device):
    return pltpu.make_async_remote_copy(
        src_ref=source, dst_ref=target, send_sem=sems[0].at[at], recv_sem=sems[1].at[at],
        device_id=device, device_id_type=MESH,
    )


def greet(devices):
    barrier = pltpu.get_barrier_semaphore()
    for device in devices:
        pl.semaphore_signal(barrier, inc=1, device_id=device, device_id_type=MESH)
    pl.semaphore_wait(barrier, len(devices))


def section_peers(replica, section, chip, core, sections):
    return [(replica, lax.rem(section + d, sections), chip * 2 + core) for d in range(1, sections)]


def plane_peers(replica, section, chip, core, replicas):
    found = []
    for dr in range(replicas):
        for dz in range(2):
            for dc in range(2):
                if dr or dz or dc:
                    there = lax.rem(replica + dr, replicas)
                    tensor = lax.rem(chip + dz, 2) * 2 + lax.rem(core + dc, 2)
                    found.append(((there, section, tensor), there * 4 + tensor))
    return found


def piece_sum(box):
    total = box[0].astype(jnp.float32)
    for i in range(1, box.shape[0]):
        total = total + box[i].astype(jnp.float32)
    return total


def cut(value, pieces):
    _, height, width = pieces.shape
    across = value.shape[1] // width
    for i in range(pieces.shape[0]):
        y, x = i // across * height, i % across * width
        pieces[i] = value[y : y + height, x : x + width].astype(pieces.dtype)


def join(spread, whole):
    height, width = spread.shape[-2:]
    across = whole.shape[-1] // width
    for i in range(spread.shape[0]):
        y, x = i // across * height, i % across * width
        whole[..., y : y + height, x : x + width] = spread[i]


def dma_pairs(counts):
    return [pltpu.SemaphoreType.DMA((n,)) for n in counts for _ in range(2)]


def decayed(params, moments, seconds, gradient):
    new_moments = beta_one * moments + (1.0 - beta_one) * gradient
    new_seconds = beta_two * seconds + (1.0 - beta_two) * gradient * gradient
    new_params = params - learn_rate * (
        new_moments / first_fix / (jnp.sqrt(new_seconds / second_fix) + adam_eps)
        + decay_rate * params
    )
    return new_params, new_moments, new_seconds


def run_layers(features, tokens_per, section, counted, codes, z, square, gram, coef, mixing, hb, rate, a_s, w_s, a_all):
    layers, _, tokens, wide = z.shape
    rank = wide // 2
    root = 1.0 / math.sqrt(features)
    row = lax.broadcasted_iota(jnp.int32, (tokens, 1), 0)
    taken = row < counted * tokens_per

    def picked(kind, layer):
        first = z[layer, kind][:, :rank]
        if layer == 0:
            return first.astype(jnp.float32)
        before = z[layer - 1, kind]
        code = codes[layer]
        other = jnp.where(code == 1, before[:, rank:], before[:, :rank])
        return jnp.where(code == 0, first, other).astype(jnp.float32)

    norm = square[...]
    state = jnp.concatenate([picked(1, l) for l in range(layers)], axis=1)
    a_all[...] = jnp.zeros_like(a_all)
    slopes, inner, rhos = [], [], []
    for l in range(layers):
        at = slice(l * rank, (l + 1) * rank)
        hb[l] = state
        rho = lax.rsqrt(jnp.maximum(norm, 0.0) * (1.0 / features) + norm_eps)
        product = picked(0, l)
        if l:
            product = product + dot_t(a_all[...], gram[l, :rank])
        u = product * (rho * root)
        sigma = jax.nn.sigmoid(u)
        active = (u * sigma * (1.0 / math.sqrt(rank))).astype(jnp.bfloat16)
        a_s[l] = active
        a_all[:, at] = active
        added = dot_n(active, gram[l, rank:])
        wide_a = active.astype(jnp.float32)
        norm = norm + jnp.sum(wide_a * (2.0 * state[:, at] + added[:, at]), axis=1, keepdims=True)
        state = state + added
        slopes.append(sigma * (1.0 + u * (1.0 - sigma)) * (1.0 / math.sqrt(rank)))
        inner.append(u)
        rhos.append(rho)
    back = jnp.concatenate(
        [jnp.where(taken, picked(2, l), 0.0) for l in range(layers)], axis=1
    )
    gamma = jnp.zeros((tokens, 1), jnp.float32)
    for l in reversed(range(layers)):
        at = slice(l * rank, (l + 1) * rank)
        e = back[:, at] * slopes[l]
        rho = rhos[l]
        w = (e * (rho * root)).astype(jnp.bfloat16)
        w_s[l] = w
        rate[l] = gamma
        c = rho * rho * jnp.sum(e * inner[l], axis=1, keepdims=True) * (1.0 / features)
        gamma = gamma + c
        if l:
            back = back + dot_n(w, gram[l, :rank]) - c * hb[l]
    own_w = w_s[section].astype(jnp.float32)
    own_a = a_s[section].astype(jnp.float32)
    own_rate = rate[section]
    nothing = jnp.zeros((tokens, rank), jnp.float32)
    left = jnp.concatenate(
        [
            jnp.concatenate([own_w, -own_rate * own_a], axis=1),
            jnp.concatenate([nothing, jnp.where(taken, own_a, 0.0)], axis=1),
        ],
        axis=0,
    )
    coef[...] = left.T.astype(jnp.bfloat16)
    own_left = own_a.T.astype(jnp.bfloat16)
    own_down = own_w.T.astype(jnp.bfloat16)
    before = jnp.concatenate([jnp.where(l < section, a_s[l], jnp.zeros_like(a_s[l])) for l in range(layers)], axis=1)
    beyond = jnp.concatenate([jnp.where(l > section, w_s[l], jnp.zeros_like(w_s[l])) for l in range(layers)], axis=1)
    scaled = jnp.concatenate(
        [
            (jnp.where(l <= section, own_rate, rate[l]) * a_s[l].astype(jnp.float32)).astype(jnp.bfloat16)
            for l in range(layers)
        ],
        axis=1,
    )
    mixing[:rank] = (dot_n(own_down, before) + dot_n(own_left, beyond)).astype(jnp.bfloat16)
    mixing[rank:] = (-dot_n(own_left, scaled)).astype(jnp.bfloat16)


def publish(replicas, sections, share, out, shift_send, shift_recv, far_sems, core_sems):
    replica, section, chip, core = place()
    columns = share.shape[1]
    before = lax.rem(section + sections - 1, sections)
    other = 1 - chip
    up, down, across = (lax.rem(replica + d, replicas) for d in (1, replicas - 1, 2))
    tensor = chip * 2 + core
    sibling = (replica, section, chip * 2 + 1 - core)
    partner = (replica, section, other * 2 + core)
    above, below = (up, section, tensor), (down, section, tensor)
    rank = share.shape[0] // 2

    def columns_of(r, z):
        return pl.ds(pl.multiple_of((r * 4 + z * 2 + core) * columns, 128), columns)

    def block(window, r, z):
        return out.at[window, :, columns_of(r, z)]

    started = {}
    def send(number, piece, device):
        copy = remote(piece, piece, far_sems, number, device)
        copy.start()
        started[number] = copy

    swaps = []

    def swap(window, r, z):
        copy = remote(block(window, r, z), block(window, r, z), core_sems, len(swaps), sibling)
        copy.start()
        swaps.append(copy)

    def upper(r):
        return out.at[1, pl.ds(0, rank), columns_of(r, chip)]

    def lower(r):
        return out.at[1, pl.ds(rank, rank), columns_of(r, chip)]

    own = columns_of(replica, chip)
    shift = pltpu.make_async_remote_copy(
        src_ref=share, dst_ref=out.at[1, :, own], send_sem=shift_send, recv_sem=shift_recv,
        device_id=(replica, before, tensor), device_id_type=MESH,
    )
    shift.start()
    out[0, :, own] = share[...]
    send(0, block(0, replica, chip), partner)
    send(1, block(0, replica, chip), above)
    send(3, block(0, replica, chip), below)
    swap(0, replica, chip)
    shift.wait()
    send(7, block(1, replica, chip), above)
    send(8, block(1, replica, chip), below)
    send(11, block(1, replica, chip), partner)
    swap(1, replica, chip)
    started[0].wait_recv()
    send(2, block(0, replica, other), above)
    send(4, block(0, replica, other), below)
    swap(0, replica, other)
    started[1].wait_recv()
    send(5, block(0, down, chip), above)
    swap(0, down, chip)
    started[3].wait_recv()
    swap(0, up, chip)
    started[7].wait_recv()
    send(9, upper(down), above)
    send(12, block(1, down, chip), partner)
    swap(1, down, chip)
    started[8].wait_recv()
    send(10, lower(up), below)
    send(13, block(1, up, chip), partner)
    swap(1, up, chip)
    started[4].wait_recv()
    send(6, block(0, up, other), below)
    swap(0, up, other)
    started[2].wait_recv()
    swap(0, down, other)
    started[11].wait_recv()
    swap(1, replica, other)
    started[9].wait_recv()
    send(14, upper(across), partner)
    started[10].wait_recv()
    send(15, lower(across), partner)
    swap(1, across, chip)
    started[5].wait_recv()
    swap(0, across, chip)
    started[6].wait_recv()
    swap(0, across, other)
    started[12].wait_recv()
    swap(1, down, other)
    started[13].wait_recv()
    swap(1, up, other)
    started[14].wait_recv()
    started[15].wait_recv()
    swap(1, across, other)
    for copy in started.values():
        copy.wait_send()
    for copy in swaps:
        copy.wait()


COUNTS = dict(rows=7, z=7, gram=15, piece=7, plane=7, core=8, downs=7, mix=15, mixed=15, half=8, chip=14, far=16, swap=16)


def step_kernel(
    replicas, sections, tokens_per,
    bounds, counts, hidden_hbm, last_hbm, downs_hbm, ups_hbm,
    master_down, master_up, moment_down, moment_up, second_down, second_up,
    gradient, placed_down, placed_up,
    out, hidden, last, weights, mine, z, acc, zs, rows, down_rows, gram, pieces, box, spread,
    coef, mixing, hb, rate, a_s, w_s, a_all, mix_pieces, mix_box, mix_spread,
    parts, half, chips, inbox, late, share, local, shift_send, shift_recv, *sems,
):
    sem = {name: sems[2 * i : 2 * i + 2] for i, name in enumerate(COUNTS)}
    replica, section, chip, core = place()
    tensor = chip * 2 + core
    me = replica * 4 + tensor
    rank, columns = master_down.shape
    wide = 2 * rank
    tokens, features = hidden.shape
    along = section_peers(replica, section, chip, core, sections)
    peers = plane_peers(replica, section, chip, core, replicas)
    sibling = (replica, section, chip * 2 + 1 - core)

    loads = [
        pltpu.make_async_copy(downs_hbm, weights.at[pl.ds(0, wide)], local.at[0]),
        pltpu.make_async_copy(ups_hbm, weights.at[pl.ds(wide, wide)], local.at[1]),
        pltpu.make_async_copy(hidden_hbm, hidden, local.at[2]),
        pltpu.make_async_copy(last_hbm, last, local.at[3]),
    ]
    for copy in loads:
        copy.start()
    mine[:rank] = master_down[...].astype(mine.dtype)
    mine[rank:] = master_up[...].astype(mine.dtype)
    greet(along + [device for device, _ in peers])

    row_copies = []
    for i, device in enumerate(along):
        row_copies.append(remote(mine.at[pl.ds(rank, rank)], rows.at[section], sem["rows"], i, device))
        row_copies[-1].start()
    rows[section] = mine[rank:]

    for copy in loads:
        copy.wait()
    acc[...] = jnp.zeros_like(acc)
    step = 1024

    @pl.loop(0, features // step)
    def _(i):
        at = pl.ds(pl.multiple_of(i * step, step), step)
        chunk = hidden[:, at]
        acc[:, : 2 * wide] += dot_t(chunk, weights[:, at])
        acc[:, 2 * wide : 3 * wide] += dot_t(last[:, at], weights[wide:, at])
        squares = chunk.astype(jnp.float32)
        squares = squares * squares
        folded = squares[:, :128]
        for j in range(1, step // 128):
            folded = folded + squares[:, j * 128 : (j + 1) * 128]
        acc[:, 3 * wide :] += folded

    for kind in range(3):
        z[kind] = acc[:, kind * wide : (kind + 1) * wide].astype(z.dtype)
    zs[section] = z[...]

    for copy in row_copies:
        copy.wait()
    cut(dot_t(mine[...], rows[...].reshape(sections * rank, columns)), pieces)
    copies = []
    for i, (device, number) in enumerate(peers):
        copies.append(remote(pieces.at[number], box.at[me], sem["gram"], i, device))
        copies[-1].start()
    z_copies = []
    for i, device in enumerate(along):
        z_copies.append(remote(z, zs.at[section], sem["z"], i, device))
        z_copies[-1].start()
    box[me] = pieces[me]
    for copy in copies:
        copy.wait()
    spread[me, section] = piece_sum(box).astype(spread.dtype)
    copies = []
    for i, device in enumerate(along):
        copies.append(remote(spread.at[me, section], spread.at[me, section], sem["piece"], i, device))
        copies[-1].start()
    for copy in copies:
        copy.wait()
    same = [device for i, (device, number) in enumerate(peers) if i % 2 == 1]
    copies = []
    for i, device in enumerate(same):
        copies.append(remote(spread.at[me], spread.at[me], sem["plane"], i, device))
        copies[-1].start()
    swaps = [remote(spread.at[me], spread.at[me], sem["core"], 7, sibling)]
    swaps[0].start()
    for i, copy in enumerate(copies):
        copy.wait_recv()
        dr, dz = (i + 1) // 2, (i + 1) % 2
        source = lax.rem(replica + replicas - dr, replicas) * 4 + lax.rem(chip + dz, 2) * 2 + core
        swaps.append(remote(spread.at[source], spread.at[source], sem["core"], i, sibling))
        swaps[-1].start()
    for copy in copies:
        copy.wait_send()
    for copy in z_copies:
        copy.wait()
    down_copies = []
    for i, device in enumerate(along):
        down_copies.append(remote(mine.at[pl.ds(0, rank)], down_rows.at[section], sem["downs"], i, device))
        down_copies[-1].start()
    down_rows[section] = mine[:rank]
    for copy in swaps:
        copy.wait()
    join(spread, gram)

    codes = [0]
    for l in range(1, sections):
        here = (bounds[replica, l] == l) & (bounds[replica, l + 1] > l)
        codes.append(jnp.where(here, 0, jnp.where(bounds[replica, l - 1] == l, 2, 1)))
    square = jnp.sum(acc[:, 3 * wide :], axis=1, keepdims=True)
    run_layers(
        features, tokens_per, section, counts[replica], codes, zs, square, gram, coef, mixing, hb, rate, a_s, w_s, a_all
    )

    cut(mixing[...], mix_pieces)
    mix_copies = []
    for i, (device, number) in enumerate(peers):
        mix_copies.append(remote(mix_pieces.at[number], mix_box.at[me], sem["mix"], i, device))
        mix_copies[-1].start()
    mix_box[me] = mix_pieces[me]
    order = [(2, 1), (2, 0), (1, 1), (1, 0), (3, 1), (3, 0), (0, 1), (0, 0)]
    partner = (replica, section, lax.rem(chip + 1, 2) * 2 + core)
    first, second = pl.ds(0, rank), pl.ds(rank, rank)

    def ring(dr):
        return (lax.rem(replica + dr, replicas), section, tensor)

    def block_gradient(dr, dz, c):
        number = lax.rem(replica + dr, replicas) * 4 + lax.rem(chip + dz, 2) * 2 + c
        at = pl.ds(pl.multiple_of(number * columns, 128), columns)
        return dot_n(coef[:, :tokens], hidden[:, at]) + dot_n(coef[:, tokens:], last[:, at])

    halves = []
    sends = {}

    def send(number, source, target, device):
        sends[number] = remote(source, target, sem["chip"], number, device)
        sends[number].start()

    for i in range(len(order) + 1):
        if i < len(order):
            parts[i] = block_gradient(*order[i], 1 - core).astype(parts.dtype)
            halves.append(remote(parts.at[i], half.at[i], sem["half"], i, sibling))
            halves[-1].start()
        if i:
            dr, dz = order[i - 1]
            added = block_gradient(dr, dz, core)
            halves[i - 1].wait()
            chips[i - 1] = (added + half[i - 1].astype(jnp.float32)).astype(chips.dtype)
            if dr:
                send(i - 1, chips.at[i - 1, first], inbox.at[i - 1, first], ring(dr))
            if dz:
                send(6 + dr, chips.at[i - 1, second], inbox.at[i - 1, second], partner)
    at = {distance: i for i, distance in enumerate(order)}

    for dr in (2, 1, 3):
        sends[6 + dr].wait_recv()
        i = at[dr, 1]
        parts[i, second] = (chips[at[dr, 0], second].astype(jnp.float32) + inbox[i, second].astype(jnp.float32)).astype(
            parts.dtype
        )
        send(9 + dr, parts.at[i, second], late.at[dr], ring(dr))
    for dz in (1, 0):
        total = chips[at[0, dz], first].astype(jnp.float32)
        for dr in (2, 1, 3):
            sends[at[dr, dz]].wait_recv()
            total = total + inbox[at[dr, dz], first].astype(jnp.float32)
        if dz:
            parts[at[0, 1], first] = total.astype(parts.dtype)
            send(13, parts.at[at[0, 1], first], late.at[0], partner)
        else:
            kept = total
    for copy in mix_copies:
        copy.wait()
    mix_spread[me] = piece_sum(mix_box).astype(mix_spread.dtype)
    mix_copies = []
    for i, (device, number) in enumerate(peers):
        mix_copies.append(remote(mix_spread.at[me], mix_spread.at[me], sem["mixed"], i, device))
        mix_copies[-1].start()
    for copy in mix_copies:
        copy.wait()
    join(mix_spread, mixing)
    for copy in down_copies:
        copy.wait()
    layer_of = lax.broadcasted_iota(jnp.int32, (rank, sections * rank), 1) // rank
    crossing = mixing[:rank]
    nothing = jnp.zeros_like(crossing)
    ups_all = rows[...].reshape(sections * rank, columns)
    downs_all = down_rows[...].reshape(sections * rank, columns)
    gradient[:rank] = dot_n(jnp.where(layer_of < section, crossing, nothing), ups_all)
    gradient[rank:] = dot_n(mixing[rank:], ups_all) + dot_n(
        jnp.where(layer_of > section, crossing, nothing), downs_all
    )
    sends[6].wait_recv()
    total = chips[at[0, 0], second].astype(jnp.float32) + inbox[at[0, 1], second].astype(jnp.float32)
    for dr in (2, 1, 3):
        sends[9 + dr].wait_recv()
        total = total + late[dr].astype(jnp.float32)
    gradient[rank:] += total
    sends[13].wait_recv()
    gradient[:rank] += kept + late[0].astype(jnp.float32)
    for copy in sends.values():
        copy.wait_send()
    share[:rank] = decayed(master_down[...], moment_down[...], second_down[...], gradient[:rank])[0].astype(share.dtype)
    share[rank:] = decayed(master_up[...], moment_up[...], second_up[...], gradient[rank:])[0].astype(share.dtype)
    publish(replicas, sections, share, out, shift_send, shift_recv, sem["far"], sem["swap"])
    begin, end = bounds[replica, section], bounds[replica, section + 1]
    held, both, own = end > begin, end > begin + 1, begin == section

    @pl.loop(0, features // step)
    def _(i):
        at = pl.ds(pl.multiple_of(i * step, step), step)
        for placed, rows_of in ((placed_down, first), (placed_up, second)):
            this, following = out[0, rows_of, at], out[1, rows_of, at]
            none = jnp.zeros_like(this)
            placed[0, :, at] = jnp.where(held, jnp.where(own, this, following), none)
            placed[1, :, at] = jnp.where(both, following, none)


def run_step(bounds, counts, hidden, last, downs, ups, owned, tokens_per):
    replicas, sections = lax.axis_size("replica"), lax.axis_size("section")
    rank, columns = owned[0].shape
    wide, layers = 2 * rank, sections
    tokens, features = hidden.shape
    size = replicas * 4
    height, width = 16, wide * layers * rank // size // 16
    b16, f32 = jnp.bfloat16, jnp.float32
    smem, hbm, vmem = (pl.BlockSpec(memory_space=m) for m in (pltpu.SMEM, pl.ANY, pltpu.VMEM))
    piece = pltpu.VMEM((size, height, width), b16)
    block = pltpu.VMEM((size // 2, wide, columns), b16)
    return pl.pallas_call(
        functools.partial(step_kernel, replicas, sections, tokens_per),
        out_shape=(
            jax.ShapeDtypeStruct((wide, columns), f32),
            jax.ShapeDtypeStruct((2, rank, features), b16),
            jax.ShapeDtypeStruct((2, rank, features), b16),
        ),
        in_specs=[smem, smem] + [hbm] * 4 + [vmem] * 6,
        out_specs=(vmem,) * 3,
        scratch_shapes=[
            pltpu.VMEM((2, wide, features), b16),
            pltpu.VMEM((tokens, features), b16),
            pltpu.VMEM((tokens, features), b16),
            pltpu.VMEM((2 * wide, features), b16),
            pltpu.VMEM((wide, columns), b16),
            pltpu.VMEM((3, tokens, wide), b16),
            pltpu.VMEM((tokens, 3 * wide + 128), f32),
            pltpu.VMEM((layers, 3, tokens, wide), b16),
            pltpu.VMEM((layers, rank, columns), b16),
            pltpu.VMEM((layers, rank, columns), b16),
            pltpu.VMEM((layers, wide, layers * rank), b16),
            piece,
            piece,
            pltpu.VMEM((size, sections, height, width), b16),
            pltpu.VMEM((wide, 2 * tokens), b16),
            pltpu.VMEM((wide, layers * rank), b16),
            pltpu.VMEM((layers, tokens, layers * rank), f32),
            pltpu.VMEM((layers, tokens, 1), f32),
            pltpu.VMEM((layers, tokens, rank), b16),
            pltpu.VMEM((layers, tokens, rank), b16),
            pltpu.VMEM((tokens, layers * rank), b16),
            piece,
            piece,
            piece,
            block,
            block,
            block,
            block,
            pltpu.VMEM((replicas, rank, columns), b16),
            pltpu.VMEM((wide, columns), b16),
            pltpu.SemaphoreType.DMA((4,)),
            pltpu.SemaphoreType.DMA,
            pltpu.SemaphoreType.DMA,
        ]
        + dma_pairs(COUNTS.values()),
        compiler_params=pltpu.CompilerParams(collective_id=1, has_side_effects=True, vmem_limit_bytes=42 * 2**20),
        name="step",
    )(bounds, counts, hidden, last, downs, ups, *owned)


def on_device(
    inputs, cotangent, micro_counts, bounds, holder_down, holder_up,
    master_down, master_up, moment_down, moment_up, second_down, second_up,
):
    micros, per, features = inputs.shape[1:]
    slots, rank = holder_down.shape[2:4]
    tokens = micros * per
    owned = [array[0] for array in (master_down, master_up, moment_down, moment_up, second_down, second_up)]
    gradient, placed_down, placed_up = run_step(
        bounds,
        micro_counts,
        inputs[0].reshape(tokens, features),
        cotangent[0].reshape(tokens, features),
        holder_down[0, 0].reshape(slots * rank, features),
        holder_up[0, 0].reshape(slots * rank, features),
        owned,
        per,
    )
    new_down = decayed(owned[0], owned[2], owned[4], gradient[:rank])
    new_up = decayed(owned[1], owned[3], owned[5], gradient[rank:])
    news = [array[None] for pair in zip(new_down, new_up) for array in pair]
    return (placed_down[None, None], placed_up[None, None], *news)


def solution(mesh):
    owned = P("section", None, ("replica", "tensor"))
    held = P("replica", "section", None, None, None)
    tokens = P("replica", None, "tensor", None)
    return jax.shard_map(
        on_device,
        mesh=mesh,
        in_specs=(tokens, tokens, P(), P(), held, held) + (owned,) * 6,
        out_specs=(held, held) + (owned,) * 6,
        check_vma=False,
    )
```

```python
import functools
import math

import jax
import jax.numpy as jnp
from jax import lax
from jax.experimental import pallas as pl
from jax.experimental.pallas import tpu as pltpu
from jax.sharding import PartitionSpec as P

norm_eps = 1e-06
learn_rate = 0.01
beta_one = 0.9
beta_two = 0.95
decay_rate = 0.1
adam_eps = 1e-08
first_fix = 0.9999734386011124
second_fix = 0.9940794707796659


def dot_t(left, right):
    return lax.dot_general(
        left, right, (((1,), (1,)), ((), ())), preferred_element_type=jnp.float32
    )


def dot_n(left, right):
    return jnp.dot(left, right, preferred_element_type=jnp.float32)


MESH = pl.DeviceIdType.MESH


def place():
    tensor = lax.axis_index("tensor")
    return lax.axis_index("replica"), lax.axis_index("section"), tensor // 2, tensor % 2


def remote(source, target, sems, at, device):
    return pltpu.make_async_remote_copy(
        src_ref=source, dst_ref=target, send_sem=sems[0].at[at], recv_sem=sems[1].at[at],
        device_id=device, device_id_type=MESH,
    )


def section_peers(replica, section, chip, core, sections):
    return [(replica, lax.rem(section + d, sections), chip * 2 + core) for d in range(1, sections)]


def plane_peers(replica, section, chip, core, replicas):
    found = []
    for dr in range(replicas):
        for dz in range(2):
            for dc in range(2):
                if dr or dz or dc:
                    there = lax.rem(replica + dr, replicas)
                    tensor = lax.rem(chip + dz, 2) * 2 + lax.rem(core + dc, 2)
                    found.append(((there, section, tensor), there * 4 + tensor))
    return found


def piece_sum(box):
    total = box[0].astype(jnp.float32)
    for i in range(1, box.shape[0]):
        total = total + box[i].astype(jnp.float32)
    return total


def cut(value, pieces):
    _, height, width = pieces.shape
    across = value.shape[1] // width
    for i in range(pieces.shape[0]):
        y, x = i // across * height, i % across * width
        pieces[i] = value[y : y + height, x : x + width].astype(pieces.dtype)


def join(spread, whole):
    height, width = spread.shape[-2:]
    across = whole.shape[-1] // width
    for i in range(spread.shape[0]):
        y, x = i // across * height, i % across * width
        whole[..., y : y + height, x : x + width] = spread[i]


def dma_pairs(counts):
    return [pltpu.SemaphoreType.DMA((n,)) for n in counts for _ in range(2)]


def decayed(params, moments, seconds, gradient):
    new_moments = beta_one * moments + (1.0 - beta_one) * gradient
    new_seconds = beta_two * seconds + (1.0 - beta_two) * gradient * gradient
    new_params = params - learn_rate * (
        new_moments / first_fix / (jnp.sqrt(new_seconds / second_fix) + adam_eps)
        + decay_rate * params
    )
    return new_params, new_moments, new_seconds


def run_layers(features, tokens_per, section, counted, z, square, gram, coef, mixing, hb, rate, a_s, w_s, a_all):
    layers, packed, wide = z.shape
    rank, tokens = wide // 2, packed * 2 // 3
    root = 1.0 / math.sqrt(features)
    row = lax.broadcasted_iota(jnp.int32, (tokens, 1), 0)
    taken = row < counted * tokens_per

    def picked(kind, layer):
        if kind < 2:
            found = z[layer, :tokens, kind * rank : (kind + 1) * rank]
        else:
            found = jnp.concatenate([z[layer, tokens:, :rank], z[layer, tokens:, rank:]], axis=0)
        return found.astype(jnp.float32)

    norm = square[...]
    state = jnp.concatenate([picked(1, l) for l in range(layers)], axis=1)
    a_all[...] = jnp.zeros_like(a_all)
    slopes, inner, rhos = [], [], []
    for l in range(layers):
        at = slice(l * rank, (l + 1) * rank)
        hb[l] = state
        rho = lax.rsqrt(jnp.maximum(norm, 0.0) * (1.0 / features) + norm_eps)
        product = picked(0, l)
        if l:
            product = product + dot_t(a_all[...], gram[l, :rank])
        u = product * (rho * root)
        sigma = jax.nn.sigmoid(u)
        active = (u * sigma * (1.0 / math.sqrt(rank))).astype(jnp.bfloat16)
        a_s[l] = active
        a_all[:, at] = active
        added = dot_n(active, gram[l, rank:])
        wide_a = active.astype(jnp.float32)
        norm = norm + jnp.sum(wide_a * (2.0 * state[:, at] + added[:, at]), axis=1, keepdims=True)
        state = state + added
        slopes.append(sigma * (1.0 + u * (1.0 - sigma)) * (1.0 / math.sqrt(rank)))
        inner.append(u)
        rhos.append(rho)
    back = jnp.concatenate(
        [jnp.where(taken, picked(2, l), 0.0) for l in range(layers)], axis=1
    )
    gamma = jnp.zeros((tokens, 1), jnp.float32)
    for l in reversed(range(layers)):
        at = slice(l * rank, (l + 1) * rank)
        e = back[:, at] * slopes[l]
        rho = rhos[l]
        w = (e * (rho * root)).astype(jnp.bfloat16)
        w_s[l] = w
        rate[l] = gamma
        c = rho * rho * jnp.sum(e * inner[l], axis=1, keepdims=True) * (1.0 / features)
        gamma = gamma + c
        if l:
            back = back + dot_n(w, gram[l, :rank]) - c * hb[l]
    own_w = w_s[section].astype(jnp.float32)
    own_a = a_s[section].astype(jnp.float32)
    own_rate = rate[section]
    nothing = jnp.zeros((tokens, rank), jnp.float32)
    left = jnp.concatenate(
        [
            jnp.concatenate([own_w, -own_rate * own_a], axis=1),
            jnp.concatenate([nothing, jnp.where(taken, own_a, 0.0)], axis=1),
        ],
        axis=0,
    )
    coef[...] = left.T.astype(jnp.bfloat16)
    own_left = own_a.T.astype(jnp.bfloat16)
    own_down = own_w.T.astype(jnp.bfloat16)
    before = jnp.concatenate([jnp.where(l < section, a_s[l], jnp.zeros_like(a_s[l])) for l in range(layers)], axis=1)
    beyond = jnp.concatenate([jnp.where(l > section, w_s[l], jnp.zeros_like(w_s[l])) for l in range(layers)], axis=1)
    scaled = jnp.concatenate(
        [
            (jnp.where(l <= section, own_rate, rate[l]) * a_s[l].astype(jnp.float32)).astype(jnp.bfloat16)
            for l in range(layers)
        ],
        axis=1,
    )
    mixing[:rank] = (dot_n(own_down, before) + dot_n(own_left, beyond)).astype(jnp.bfloat16)
    mixing[rank:] = (-dot_n(own_left, scaled)).astype(jnp.bfloat16)


def publish(replicas, sections, share, out, shift_send, shift_recv, far_sems, core_sems):
    replica, section, chip, core = place()
    columns = share.shape[1]
    before = lax.rem(section + sections - 1, sections)
    other = 1 - chip
    up, down, across = (lax.rem(replica + d, replicas) for d in (1, replicas - 1, 2))
    tensor = chip * 2 + core
    sibling = (replica, section, chip * 2 + 1 - core)
    partner = (replica, section, other * 2 + core)
    above, below = (up, section, tensor), (down, section, tensor)
    rank = share.shape[0] // 2

    def columns_of(r, z):
        return pl.ds(pl.multiple_of((r * 4 + z * 2 + core) * columns, 128), columns)

    def block(window, r, z):
        return out.at[window, :, columns_of(r, z)]

    started = {}
    def send(number, piece, device):
        copy = remote(piece, piece, far_sems, number, device)
        copy.start()
        started[number] = copy

    def landed(*numbers):
        for number in numbers:
            started[number].wait_recv()

    swaps = []

    def swap(window, r, z):
        copy = remote(block(window, r, z), block(window, r, z), core_sems, len(swaps), sibling)
        copy.start()
        swaps.append(copy)

    def rows_of(start, count, r, z):
        return out.at[0, pl.ds(start, count), columns_of(r, z)]

    def lower(r, z):
        return rows_of(0, rank, r, z)

    def upper(r, z):
        return rows_of(rank, rank, r, z)

    own = columns_of(replica, chip)
    shift = pltpu.make_async_remote_copy(
        src_ref=share, dst_ref=out.at[1, :, own], send_sem=shift_send, recv_sem=shift_recv,
        device_id=(replica, before, tensor), device_id_type=MESH,
    )
    shift.start()
    out[0, :, own] = share[...]
    send(0, lower(replica, chip), partner)
    send(1, block(0, replica, chip), above)
    send(2, block(0, replica, chip), below)
    send(3, upper(replica, chip), partner)
    swap(0, replica, chip)
    landed(0)
    send(4, lower(replica, other), above)
    send(5, lower(replica, other), below)
    landed(1)
    send(6, lower(down, chip), above)
    send(7, rows_of(rank, rank // 2, down, chip), above)
    send(8, upper(down, chip), partner)
    landed(2)
    send(9, rows_of(rank + rank // 2, rank // 2, up, chip), below)
    send(10, upper(up, chip), partner)
    shift.wait()
    send(13, block(1, replica, chip), above)
    send(14, block(1, replica, chip), below)
    send(15, block(1, replica, chip), partner)
    swap(0, down, chip)
    swap(0, up, chip)
    swap(1, replica, chip)
    landed(5)
    send(11, lower(up, other), below)
    landed(3)
    swap(0, replica, other)
    landed(7, 9)
    send(12, upper(across, chip), partner)
    landed(15)
    send(16, block(1, replica, other), above)
    send(17, block(1, replica, other), below)
    swap(1, replica, other)
    landed(13)
    send(18, block(1, down, chip), above)
    swap(1, down, chip)
    landed(14)
    swap(1, up, chip)
    landed(6)
    swap(0, across, chip)
    landed(4, 8)
    swap(0, down, other)
    landed(10)
    swap(0, up, other)
    landed(17)
    send(19, block(1, up, other), below)
    swap(1, up, other)
    landed(11, 12)
    swap(0, across, other)
    landed(16)
    swap(1, down, other)
    landed(18)
    swap(1, across, chip)
    landed(19)
    swap(1, across, other)
    for copy in started.values():
        copy.wait_send()
    for copy in swaps:
        copy.wait()


COUNTS = dict(rows=7, zshift=1, z=7, gram=15, piece=7, plane=7, core=8, downs=7, mix=15, mixed=15, half=8, chip=14, far=20, swap=16)


def step_kernel(
    replicas, sections, tokens_per,
    bounds_hbm, counts_hbm, hidden_hbm, last_hbm, downs_hbm, ups_hbm, *refs,
):
    owned_hbm, refs = refs[:6], refs[6:]
    step_body(
        replicas, sections, tokens_per, bounds_hbm, counts_hbm, hidden_hbm, last_hbm, downs_hbm, ups_hbm, owned_hbm, *refs
    )


def step_body(
    replicas, sections, tokens_per, bounds_hbm, counts_hbm, hidden_hbm, last_hbm, downs_hbm, ups_hbm, owned_hbm,
    gradient, placed_down, placed_up,
    bounds, counts, owned, out, both, weights, mine, z, z_before, acc, zs, rows, down_rows, gram, pieces, box, spread,
    coef, mixing, hb, rate, a_s, w_s, a_all, mix_pieces, mix_box, mix_spread,
    parts, half, chips, inbox, late, share, local, shift_send, shift_recv, *sems,
):
    sem = {name: sems[2 * i : 2 * i + 2] for i, name in enumerate(COUNTS)}
    replica, section, chip, core = place()
    tensor = chip * 2 + core
    me = replica * 4 + tensor
    _, rank, columns = owned.shape
    master_down, master_up, moment_down, moment_up, second_down, second_up = (owned.at[i] for i in range(6))
    wide = 2 * rank
    tokens, features = both.shape[0] // 2, both.shape[1]
    hidden, last = both.at[pl.ds(0, tokens)], both.at[pl.ds(tokens, tokens)]
    along = section_peers(replica, section, chip, core, sections)
    peers = plane_peers(replica, section, chip, core, replicas)
    sibling = (replica, section, chip * 2 + 1 - core)

    loads = [
        pltpu.make_async_copy(downs_hbm, weights.at[pl.ds(0, wide)], local.at[0]),
        pltpu.make_async_copy(ups_hbm, weights.at[pl.ds(wide, wide)], local.at[1]),
        pltpu.make_async_copy(hidden_hbm, hidden, local.at[2]),
        pltpu.make_async_copy(last_hbm, last, local.at[3]),
    ]
    barrier = pltpu.get_barrier_semaphore()
    everyone = along + [device for device, _ in peers]
    for device in everyone:
        pl.semaphore_signal(barrier, inc=1, device_id=device, device_id_type=MESH)
    firsts = [pltpu.make_async_copy(owned_hbm[i], owned.at[i], local.at[4 + i]) for i in range(6)]
    firsts.append(pltpu.make_async_copy(bounds_hbm, bounds, local.at[10]))
    firsts.append(pltpu.make_async_copy(counts_hbm, counts, local.at[11]))
    for copy in firsts + loads:
        copy.start()
    for copy in firsts:
        copy.wait()
    mine[:rank] = master_down[...].astype(mine.dtype)
    mine[rank:] = master_up[...].astype(mine.dtype)
    pl.semaphore_wait(barrier, len(everyone))

    row_copies = []
    for i, device in enumerate(along):
        row_copies.append(remote(mine.at[pl.ds(rank, rank)], rows.at[section], sem["rows"], i, device))
        row_copies[-1].start()
    rows[section] = mine[rank:]

    for copy in loads:
        copy.wait()
    acc[...] = jnp.zeros_like(acc)
    step = 1024

    @pl.loop(0, features // step)
    def _(i):
        at = pl.ds(pl.multiple_of(i * step, step), step)
        chunk = hidden[:, at]
        acc[:, : 2 * wide] += dot_t(chunk, weights[:, at])
        acc[:, 2 * wide : 3 * wide] += dot_t(last[:, at], weights[wide:, at])
        squares = chunk.astype(jnp.float32)
        squares = squares * squares
        folded = squares[:, :128]
        for j in range(1, step // 128):
            folded = folded + squares[:, j * 128 : (j + 1) * 128]
        acc[:, 3 * wide :] += folded

    for kind in range(3):
        z[kind] = acc[:, kind * wide : (kind + 1) * wide].astype(z.dtype)

    for copy in row_copies:
        copy.wait()
    z_shift = remote(z, z_before, sem["zshift"], 0, along[0])
    z_shift.start()
    cut(dot_t(mine[...], rows[...].reshape(sections * rank, columns)), pieces)
    copies = []
    for i, (device, number) in enumerate(peers):
        copies.append(remote(pieces.at[number], box.at[me], sem["gram"], i, device))
        copies[-1].start()
    box[me] = pieces[me]
    for copy in copies:
        copy.wait()
    spread[me, section] = piece_sum(box).astype(spread.dtype)
    copies = []
    for i, device in enumerate(along):
        copies.append(remote(spread.at[me, section], spread.at[me, section], sem["piece"], i, device))
        copies[-1].start()
    z_shift.wait()
    here = (bounds[replica, section] == section) & (bounds[replica, section + 1] > section)
    alone = bounds[replica, jnp.maximum(section - 1, 0)] == section
    own = []
    for kind in range(3):
        moved = jnp.where(alone, z_before[kind][:, :rank], z_before[kind][:, rank:])
        own.append(jnp.where(here, z[kind][:, :rank], moved))
    zs[section, :tokens] = jnp.concatenate(own[:2], axis=1)
    zs[section, tokens:] = jnp.concatenate([own[2][: tokens // 2], own[2][tokens // 2 :]], axis=1)
    for copy in copies:
        copy.wait()
    same = [device for i, (device, number) in enumerate(peers) if i % 2 == 1]
    copies = []
    for i, device in enumerate(same):
        copies.append(remote(spread.at[me], spread.at[me], sem["plane"], i, device))
        copies[-1].start()
    swaps = [remote(spread.at[me], spread.at[me], sem["core"], 7, sibling)]
    swaps[0].start()
    z_copies = []
    for i, device in enumerate(along):
        z_copies.append(remote(zs.at[section], zs.at[section], sem["z"], i, device))
        z_copies[-1].start()
    for i, copy in enumerate(copies):
        copy.wait_recv()
        dr, dz = (i + 1) // 2, (i + 1) % 2
        source = lax.rem(replica + replicas - dr, replicas) * 4 + lax.rem(chip + dz, 2) * 2 + core
        swaps.append(remote(spread.at[source], spread.at[source], sem["core"], i, sibling))
        swaps[-1].start()
    for copy in copies:
        copy.wait_send()
    for copy in z_copies:
        copy.wait()
    down_copies = []
    for i, device in enumerate(along):
        down_copies.append(remote(mine.at[pl.ds(0, rank)], down_rows.at[section], sem["downs"], i, device))
        down_copies[-1].start()
    down_rows[section] = mine[:rank]
    for copy in swaps:
        copy.wait()
    join(spread, gram)

    square = jnp.sum(acc[:, 3 * wide :], axis=1, keepdims=True)
    run_layers(
        features, tokens_per, section, counts[replica], zs, square, gram, coef, mixing, hb, rate, a_s, w_s, a_all
    )

    cut(mixing[...], mix_pieces)
    mix_copies = []
    for i, (device, number) in enumerate(peers):
        mix_copies.append(remote(mix_pieces.at[number], mix_box.at[me], sem["mix"], i, device))
        mix_copies[-1].start()
    mix_box[me] = mix_pieces[me]
    order = [(2, 1), (2, 0), (1, 1), (1, 0), (3, 1), (3, 0), (0, 1), (0, 0)]
    partner = (replica, section, lax.rem(chip + 1, 2) * 2 + core)
    first, second = pl.ds(0, rank), pl.ds(rank, rank)

    def ring(dr):
        return (lax.rem(replica + dr, replicas), section, tensor)

    def block_gradient(dr, dz, c):
        number = lax.rem(replica + dr, replicas) * 4 + lax.rem(chip + dz, 2) * 2 + c
        at = pl.ds(pl.multiple_of(number * columns, 128), columns)
        return dot_n(coef[...], both[:, at])

    halves = []
    sends = {}

    def send(number, source, target, device):
        sends[number] = remote(source, target, sem["chip"], number, device)
        sends[number].start()

    for i in range(len(order) + 1):
        if i < len(order):
            parts[i] = block_gradient(*order[i], 1 - core).astype(parts.dtype)
            halves.append(remote(parts.at[i], half.at[i], sem["half"], i, sibling))
            halves[-1].start()
        if i:
            dr, dz = order[i - 1]
            added = block_gradient(dr, dz, core)
            halves[i - 1].wait()
            chips[i - 1] = (added + half[i - 1].astype(jnp.float32)).astype(chips.dtype)
            if dr:
                send(i - 1, chips.at[i - 1, first], inbox.at[i - 1, first], ring(dr))
            if dz:
                send(6 + dr, chips.at[i - 1, second], inbox.at[i - 1, second], partner)
    at = {distance: i for i, distance in enumerate(order)}

    for dr in (2, 1, 3):
        sends[6 + dr].wait_recv()
        i = at[dr, 1]
        parts[i, second] = (chips[at[dr, 0], second].astype(jnp.float32) + inbox[i, second].astype(jnp.float32)).astype(
            parts.dtype
        )
        send(9 + dr, parts.at[i, second], late.at[dr], ring(dr))
    for dz in (1, 0):
        total = chips[at[0, dz], first].astype(jnp.float32)
        for dr in (2, 1, 3):
            sends[at[dr, dz]].wait_recv()
            total = total + inbox[at[dr, dz], first].astype(jnp.float32)
        if dz:
            parts[at[0, 1], first] = total.astype(parts.dtype)
            send(13, parts.at[at[0, 1], first], late.at[0], partner)
        else:
            kept = total
    for copy in mix_copies:
        copy.wait()
    mix_spread[me] = piece_sum(mix_box).astype(mix_spread.dtype)
    mix_copies = []
    for i, (device, number) in enumerate(peers):
        mix_copies.append(remote(mix_spread.at[me], mix_spread.at[me], sem["mixed"], i, device))
        mix_copies[-1].start()
    for copy in mix_copies:
        copy.wait()
    join(mix_spread, mixing)
    for copy in down_copies:
        copy.wait()
    layer_of = lax.broadcasted_iota(jnp.int32, (rank, sections * rank), 1) // rank
    crossing = mixing[:rank]
    nothing = jnp.zeros_like(crossing)
    ups_all = rows[...].reshape(sections * rank, columns)
    downs_all = down_rows[...].reshape(sections * rank, columns)
    gradient[:rank] = dot_n(jnp.where(layer_of < section, crossing, nothing), ups_all)
    gradient[rank:] = dot_n(mixing[rank:], ups_all) + dot_n(
        jnp.where(layer_of > section, crossing, nothing), downs_all
    )
    sends[6].wait_recv()
    total = chips[at[0, 0], second].astype(jnp.float32) + inbox[at[0, 1], second].astype(jnp.float32)
    for dr in (2, 1, 3):
        sends[9 + dr].wait_recv()
        total = total + late[dr].astype(jnp.float32)
    gradient[rank:] += total
    sends[13].wait_recv()
    gradient[:rank] += kept + late[0].astype(jnp.float32)
    for copy in sends.values():
        copy.wait_send()
    share[:rank] = decayed(master_down[...], moment_down[...], second_down[...], gradient[:rank])[0].astype(share.dtype)
    share[rank:] = decayed(master_up[...], moment_up[...], second_up[...], gradient[rank:])[0].astype(share.dtype)
    publish(replicas, sections, share, out, shift_send, shift_recv, sem["far"], sem["swap"])
    begin, end = bounds[replica, section], bounds[replica, section + 1]
    held, both, own = end > begin, end > begin + 1, begin == section

    @pl.loop(0, features // step)
    def _(i):
        at = pl.ds(pl.multiple_of(i * step, step), step)
        for placed, rows_of in ((placed_down, first), (placed_up, second)):
            this, following = out[0, rows_of, at], out[1, rows_of, at]
            none = jnp.zeros_like(this)
            placed[0, :, at] = jnp.where(held, jnp.where(own, this, following), none)
            placed[1, :, at] = jnp.where(both, following, none)


def run_step(bounds, counts, hidden, last, downs, ups, owned, tokens_per):
    replicas, sections = lax.axis_size("replica"), lax.axis_size("section")
    rank, columns = owned[0].shape
    wide, layers = 2 * rank, sections
    tokens, features = hidden.shape
    size = replicas * 4
    height, width = 16, wide * layers * rank // size // 16
    b16, f32 = jnp.bfloat16, jnp.float32
    hbm, vmem = (pl.BlockSpec(memory_space=m) for m in (pltpu.HBM, pltpu.VMEM))
    piece = pltpu.VMEM((size, height, width), b16)
    block = pltpu.VMEM((size // 2, wide, columns), b16)
    return pl.pallas_call(
        functools.partial(step_kernel, replicas, sections, tokens_per),
        out_shape=(
            jax.ShapeDtypeStruct((wide, columns), f32),
            jax.ShapeDtypeStruct((2, rank, features), b16),
            jax.ShapeDtypeStruct((2, rank, features), b16),
        ),
        in_specs=[hbm] * 12,
        out_specs=(vmem,) * 3,
        scratch_shapes=[
            pltpu.SMEM(bounds.shape, jnp.int32),
            pltpu.SMEM(counts.shape, jnp.int32),
            pltpu.VMEM((6, rank, columns), f32),
            pltpu.VMEM((2, wide, features), b16),
            pltpu.VMEM((2 * tokens, features), b16),
            pltpu.VMEM((2 * wide, features), b16),
            pltpu.VMEM((wide, columns), b16),
            pltpu.VMEM((3, tokens, wide), b16),
            pltpu.VMEM((3, tokens, wide), b16),
            pltpu.VMEM((tokens, 3 * wide + 128), f32),
            pltpu.VMEM((layers, tokens * 3 // 2, wide), b16),
            pltpu.VMEM((layers, rank, columns), b16),
            pltpu.VMEM((layers, rank, columns), b16),
            pltpu.VMEM((layers, wide, layers * rank), b16),
            piece,
            piece,
            pltpu.VMEM((size, sections, height, width), b16),
            pltpu.VMEM((wide, 2 * tokens), b16),
            pltpu.VMEM((wide, layers * rank), b16),
            pltpu.VMEM((layers, tokens, layers * rank), f32),
            pltpu.VMEM((layers, tokens, 1), f32),
            pltpu.VMEM((layers, tokens, rank), b16),
            pltpu.VMEM((layers, tokens, rank), b16),
            pltpu.VMEM((tokens, layers * rank), b16),
            piece,
            piece,
            piece,
            block,
            block,
            block,
            block,
            pltpu.VMEM((replicas, rank, columns), b16),
            pltpu.VMEM((wide, columns), b16),
            pltpu.SemaphoreType.DMA((12,)),
            pltpu.SemaphoreType.DMA,
            pltpu.SemaphoreType.DMA,
        ]
        + dma_pairs(COUNTS.values()),
        compiler_params=pltpu.CompilerParams(collective_id=1, has_side_effects=True, vmem_limit_bytes=42 * 2**20),
        name="step",
    )(*[pltpu.with_memory_space_constraint(array, pltpu.HBM) for array in (bounds, counts, hidden, last, downs, ups, *owned)])


def on_device(
    inputs, cotangent, micro_counts, bounds, holder_down, holder_up,
    master_down, master_up, moment_down, moment_up, second_down, second_up,
):
    micros, per, features = inputs.shape[1:]
    slots, rank = holder_down.shape[2:4]
    tokens = micros * per
    owned = [array[0] for array in (master_down, master_up, moment_down, moment_up, second_down, second_up)]
    gradient, placed_down, placed_up = run_step(
        bounds,
        micro_counts,
        inputs[0].reshape(tokens, features),
        cotangent[0].reshape(tokens, features),
        holder_down[0, 0].reshape(slots * rank, features),
        holder_up[0, 0].reshape(slots * rank, features),
        owned,
        per,
    )
    new_down = decayed(owned[0], owned[2], owned[4], gradient[:rank])
    new_up = decayed(owned[1], owned[3], owned[5], gradient[rank:])
    news = [array[None] for pair in zip(new_down, new_up) for array in pair]
    return (placed_down[None, None], placed_up[None, None], *news)


def solution(mesh):
    owned = P("section", None, ("replica", "tensor"))
    held = P("replica", "section", None, None, None)
    tokens = P("replica", None, "tensor", None)
    return jax.shard_map(
        on_device,
        mesh=mesh,
        in_specs=(tokens, tokens, P(), P(), held, held) + (owned,) * 6,
        out_specs=(held, held) + (owned,) * 6,
        check_vma=False,
    )
```

```python
import functools
import math

import jax
import jax.numpy as jnp
from jax import lax
from jax.experimental import pallas as pl
from jax.experimental.pallas import tpu as pltpu
from jax.sharding import PartitionSpec as P

norm_eps = 1e-06
learn_rate = 0.01
beta_one = 0.9
beta_two = 0.95
decay_rate = 0.1
adam_eps = 1e-08
first_fix = 0.9999734386011124
second_fix = 0.9940794707796659


def dot_t(left, right):
    return lax.dot_general(
        left, right, (((1,), (1,)), ((), ())), preferred_element_type=jnp.float32
    )


def dot_n(left, right):
    return jnp.dot(left, right, preferred_element_type=jnp.float32)


MESH = pl.DeviceIdType.MESH


def place():
    tensor = lax.axis_index("tensor")
    return lax.axis_index("replica"), lax.axis_index("section"), tensor // 2, tensor % 2


def remote(source, target, sems, at, device):
    return pltpu.make_async_remote_copy(
        src_ref=source, dst_ref=target, send_sem=sems[0].at[at], recv_sem=sems[1].at[at],
        device_id=device, device_id_type=MESH,
    )


def section_peers(replica, section, chip, core, sections):
    return [(replica, lax.rem(section + d, sections), chip * 2 + core) for d in range(1, sections)]


def plane_peers(replica, section, chip, core, replicas):
    found = []
    for dr in range(replicas):
        for dz in range(2):
            for dc in range(2):
                if dr or dz or dc:
                    there = lax.rem(replica + dr, replicas)
                    tensor = lax.rem(chip + dz, 2) * 2 + lax.rem(core + dc, 2)
                    found.append(((there, section, tensor), there * 4 + tensor))
    return found


def piece_sum(box):
    total = box[0].astype(jnp.float32)
    for i in range(1, box.shape[0]):
        total = total + box[i].astype(jnp.float32)
    return total


def cut(value, pieces):
    _, height, width = pieces.shape
    across = value.shape[1] // width
    for i in range(pieces.shape[0]):
        y, x = i // across * height, i % across * width
        pieces[i] = value[y : y + height, x : x + width].astype(pieces.dtype)


def join(spread, whole):
    height, width = spread.shape[-2:]
    across = whole.shape[-1] // width
    for i in range(spread.shape[0]):
        y, x = i // across * height, i % across * width
        whole[..., y : y + height, x : x + width] = spread[i]


def dma_pairs(counts):
    return [pltpu.SemaphoreType.DMA((n,)) for n in counts for _ in range(2)]


def decayed(params, moments, seconds, gradient):
    new_moments = beta_one * moments + (1.0 - beta_one) * gradient
    new_seconds = beta_two * seconds + (1.0 - beta_two) * gradient * gradient
    new_params = params - learn_rate * (
        new_moments / first_fix / (jnp.sqrt(new_seconds / second_fix) + adam_eps)
        + decay_rate * params
    )
    return new_params, new_moments, new_seconds


def run_layers(features, tokens_per, section, counted, z, square, gram, coef, mixing, hb, rate, a_s, w_s, a_all):
    layers, packed, wide = z.shape
    rank, tokens = wide // 2, packed * 2 // 3
    root = 1.0 / math.sqrt(features)
    row = lax.broadcasted_iota(jnp.int32, (tokens, 1), 0)
    taken = row < counted * tokens_per

    def picked(kind, layer):
        if kind < 2:
            found = z[layer, :tokens, kind * rank : (kind + 1) * rank]
        else:
            found = jnp.concatenate([z[layer, tokens:, :rank], z[layer, tokens:, rank:]], axis=0)
        return found.astype(jnp.float32)

    norm = square[...]
    state = jnp.concatenate([picked(1, l) for l in range(layers)], axis=1)
    a_all[...] = jnp.zeros_like(a_all)
    slopes, inner, rhos = [], [], []
    for l in range(layers):
        at = slice(l * rank, (l + 1) * rank)
        hb[l] = state
        rho = lax.rsqrt(jnp.maximum(norm, 0.0) * (1.0 / features) + norm_eps)
        product = picked(0, l)
        if l:
            product = product + dot_t(a_all[...], gram[l, :rank])
        u = product * (rho * root)
        sigma = jax.nn.sigmoid(u)
        active = (u * sigma * (1.0 / math.sqrt(rank))).astype(jnp.bfloat16)
        a_s[l] = active
        a_all[:, at] = active
        added = dot_n(active, gram[l, rank:])
        wide_a = active.astype(jnp.float32)
        norm = norm + jnp.sum(wide_a * (2.0 * state[:, at] + added[:, at]), axis=1, keepdims=True)
        state = state + added
        slopes.append(sigma * (1.0 + u * (1.0 - sigma)) * (1.0 / math.sqrt(rank)))
        inner.append(u)
        rhos.append(rho)
    back = jnp.concatenate(
        [jnp.where(taken, picked(2, l), 0.0) for l in range(layers)], axis=1
    )
    gamma = jnp.zeros((tokens, 1), jnp.float32)
    for l in reversed(range(layers)):
        at = slice(l * rank, (l + 1) * rank)
        e = back[:, at] * slopes[l]
        rho = rhos[l]
        w = (e * (rho * root)).astype(jnp.bfloat16)
        w_s[l] = w
        rate[l] = gamma
        c = rho * rho * jnp.sum(e * inner[l], axis=1, keepdims=True) * (1.0 / features)
        gamma = gamma + c
        if l:
            back = back + dot_n(w, gram[l, :rank]) - c * hb[l]
    own_w = w_s[section].astype(jnp.float32)
    own_a = a_s[section].astype(jnp.float32)
    own_rate = rate[section]
    nothing = jnp.zeros((tokens, rank), jnp.float32)
    left = jnp.concatenate(
        [
            jnp.concatenate([own_w, -own_rate * own_a], axis=1),
            jnp.concatenate([nothing, jnp.where(taken, own_a, 0.0)], axis=1),
        ],
        axis=0,
    )
    coef[...] = left.T.astype(jnp.bfloat16)
    own_left = own_a.T.astype(jnp.bfloat16)
    own_down = own_w.T.astype(jnp.bfloat16)
    before = jnp.concatenate([jnp.where(l < section, a_s[l], jnp.zeros_like(a_s[l])) for l in range(layers)], axis=1)
    beyond = jnp.concatenate([jnp.where(l > section, w_s[l], jnp.zeros_like(w_s[l])) for l in range(layers)], axis=1)
    scaled = jnp.concatenate(
        [
            (jnp.where(l <= section, own_rate, rate[l]) * a_s[l].astype(jnp.float32)).astype(jnp.bfloat16)
            for l in range(layers)
        ],
        axis=1,
    )
    mixing[:rank] = (dot_n(own_down, before) + dot_n(own_left, beyond)).astype(jnp.bfloat16)
    mixing[rank:] = (-dot_n(own_left, scaled)).astype(jnp.bfloat16)


def publish(replicas, sections, share, out, far_sems, core_sems):
    replica, section, chip, core = place()
    columns = share.shape[1]
    before = lax.rem(section + sections - 1, sections)
    other = 1 - chip
    up, down, across = (lax.rem(replica + d, replicas) for d in (1, replicas - 1, 2))
    tensor = chip * 2 + core
    sibling = (replica, section, chip * 2 + 1 - core)
    partner = (replica, section, other * 2 + core)
    above, below = (up, section, tensor), (down, section, tensor)
    rank = share.shape[0] // 2

    def columns_of(r, z):
        return pl.ds(pl.multiple_of((r * 4 + z * 2 + core) * columns, 128), columns)

    def block(window, r, z):
        return out.at[window, :, columns_of(r, z)]

    started = {}
    def send(number, piece, device):
        copy = remote(piece, piece, far_sems, number, device)
        copy.start()
        started[number] = copy

    def landed(*numbers):
        for number in numbers:
            started[number].wait_recv()

    swaps = []

    def swap(window, r, z):
        copy = remote(block(window, r, z), block(window, r, z), core_sems, len(swaps), sibling)
        copy.start()
        swaps.append(copy)

    def half(which, r):
        return out.at[0, pl.ds(which * rank, rank), columns_of(r, chip)]

    own = columns_of(replica, chip)
    for number, device in ((3, (replica, before, tensor)), (4, (replica, before, other * 2 + core))):
        started[number] = remote(share, out.at[1, :, own], far_sems, number, device)
        started[number].start()
    out[0, :, own] = share[...]
    send(0, block(0, replica, chip), above)
    send(1, block(0, replica, chip), below)
    send(2, block(0, replica, chip), partner)
    swap(0, replica, chip)
    landed(0)
    send(5, half(0, down), above)
    send(6, block(0, down, chip), partner)
    landed(1)
    send(7, half(1, up), below)
    send(8, block(0, up, chip), partner)
    landed(3)
    send(9, block(1, replica, chip), above)
    send(10, block(1, replica, chip), below)
    landed(4)
    send(11, block(1, replica, other), above)
    send(12, block(1, replica, other), below)
    swap(0, down, chip)
    swap(0, up, chip)
    swap(1, replica, chip)
    swap(1, replica, other)
    landed(2)
    swap(0, replica, other)
    landed(5)
    send(13, half(0, across), partner)
    landed(7)
    send(14, half(1, across), partner)
    swap(0, across, chip)
    landed(9)
    send(15, block(1, down, chip), above)
    swap(1, down, chip)
    landed(10)
    swap(1, up, chip)
    landed(12)
    send(16, block(1, up, other), below)
    swap(1, up, other)
    landed(11)
    swap(1, down, other)
    landed(6)
    swap(0, down, other)
    landed(8)
    swap(0, up, other)
    landed(15)
    swap(1, across, chip)
    landed(13, 14)
    swap(0, across, other)
    landed(16)
    swap(1, across, other)
    for copy in started.values():
        copy.wait_send()
    for copy in swaps:
        copy.wait()


COUNTS = dict(rows=7, zshift=1, z=7, gram=15, piece=7, plane=7, core=8, downs=7, mix=15, mixed=15, half=8, chip=14, far=17, swap=16)


def step_kernel(
    replicas, sections, tokens_per,
    bounds_hbm, counts_hbm, hidden_hbm, last_hbm, downs_hbm, ups_hbm, *refs,
):
    owned_hbm, refs = refs[:6], refs[6:]
    step_body(
        replicas, sections, tokens_per, bounds_hbm, counts_hbm, hidden_hbm, last_hbm, downs_hbm, ups_hbm, owned_hbm, *refs
    )


def step_body(
    replicas, sections, tokens_per, bounds_hbm, counts_hbm, hidden_hbm, last_hbm, downs_hbm, ups_hbm, owned_hbm,
    gradient, placed_down, placed_up,
    bounds, counts, owned, out, both, weights, mine, z, z_before, acc, zs, rows, down_rows, gram, pieces, box, spread,
    coef, mixing, hb, rate, a_s, w_s, a_all, mix_pieces, mix_box, mix_spread,
    parts, half, chips, inbox, late, share, local, *sems,
):
    sem = {name: sems[2 * i : 2 * i + 2] for i, name in enumerate(COUNTS)}
    replica, section, chip, core = place()
    tensor = chip * 2 + core
    me = replica * 4 + tensor
    _, rank, columns = owned.shape
    master_down, master_up, moment_down, moment_up, second_down, second_up = (owned.at[i] for i in range(6))
    wide = 2 * rank
    tokens, features = both.shape[0] // 2, both.shape[1]
    hidden, last = both.at[pl.ds(0, tokens)], both.at[pl.ds(tokens, tokens)]
    along = section_peers(replica, section, chip, core, sections)
    peers = plane_peers(replica, section, chip, core, replicas)
    sibling = (replica, section, chip * 2 + 1 - core)

    loads = [
        pltpu.make_async_copy(downs_hbm, weights.at[pl.ds(0, wide)], local.at[0]),
        pltpu.make_async_copy(ups_hbm, weights.at[pl.ds(wide, wide)], local.at[1]),
        pltpu.make_async_copy(hidden_hbm, hidden, local.at[2]),
        pltpu.make_async_copy(last_hbm, last, local.at[3]),
    ]
    barrier = pltpu.get_barrier_semaphore()
    everyone = along + [device for device, _ in peers]
    for d in (1, sections - 1):
        everyone.append((replica, lax.rem(section + d, sections), (1 - chip) * 2 + core))
    for device in everyone:
        pl.semaphore_signal(barrier, inc=1, device_id=device, device_id_type=MESH)
    firsts = [pltpu.make_async_copy(owned_hbm[i], owned.at[i], local.at[4 + i]) for i in range(6)]
    firsts.append(pltpu.make_async_copy(bounds_hbm, bounds, local.at[10]))
    firsts.append(pltpu.make_async_copy(counts_hbm, counts, local.at[11]))
    for copy in firsts + loads:
        copy.start()
    for copy in firsts:
        copy.wait()
    mine[:rank] = master_down[...].astype(mine.dtype)
    mine[rank:] = master_up[...].astype(mine.dtype)
    pl.semaphore_wait(barrier, len(everyone))

    row_copies = []
    for i, device in enumerate(along):
        row_copies.append(remote(mine.at[pl.ds(rank, rank)], rows.at[section], sem["rows"], i, device))
        row_copies[-1].start()
    rows[section] = mine[rank:]

    for copy in loads:
        copy.wait()
    acc[...] = jnp.zeros_like(acc)
    step = 1024

    @pl.loop(0, features // step)
    def _(i):
        at = pl.ds(pl.multiple_of(i * step, step), step)
        chunk = hidden[:, at]
        acc[:, : 2 * wide] += dot_t(chunk, weights[:, at])
        acc[:, 2 * wide : 3 * wide] += dot_t(last[:, at], weights[wide:, at])
        squares = chunk.astype(jnp.float32)
        squares = squares * squares
        folded = squares[:, :128]
        for j in range(1, step // 128):
            folded = folded + squares[:, j * 128 : (j + 1) * 128]
        acc[:, 3 * wide :] += folded

    for kind in range(3):
        z[kind] = acc[:, kind * wide : (kind + 1) * wide].astype(z.dtype)

    for copy in row_copies:
        copy.wait()
    z_shift = remote(z, z_before, sem["zshift"], 0, along[0])
    z_shift.start()
    cut(dot_t(mine[...], rows[...].reshape(sections * rank, columns)), pieces)
    copies = []
    for i, (device, number) in enumerate(peers):
        copies.append(remote(pieces.at[number], box.at[me], sem["gram"], i, device))
        copies[-1].start()
    box[me] = pieces[me]
    for copy in copies:
        copy.wait()
    spread[me, section] = piece_sum(box).astype(spread.dtype)
    copies = []
    for i, device in enumerate(along):
        copies.append(remote(spread.at[me, section], spread.at[me, section], sem["piece"], i, device))
        copies[-1].start()
    z_shift.wait()
    here = (bounds[replica, section] == section) & (bounds[replica, section + 1] > section)
    alone = bounds[replica, jnp.maximum(section - 1, 0)] == section
    own = []
    for kind in range(3):
        moved = jnp.where(alone, z_before[kind][:, :rank], z_before[kind][:, rank:])
        own.append(jnp.where(here, z[kind][:, :rank], moved))
    zs[section, :tokens] = jnp.concatenate(own[:2], axis=1)
    zs[section, tokens:] = jnp.concatenate([own[2][: tokens // 2], own[2][tokens // 2 :]], axis=1)
    for copy in copies:
        copy.wait()
    partner = (replica, section, (1 - chip) * 2 + core)
    theirs = replica * 4 + (1 - chip) * 2 + core
    copies, swaps = [], []

    def spread_to(number, device):
        copies.append(remote(spread.at[number], spread.at[number], sem["plane"], len(copies), device))
        copies[-1].start()

    def spread_swap(number):
        swaps.append(remote(spread.at[number], spread.at[number], sem["core"], len(swaps), sibling))
        swaps[-1].start()

    spread_to(me, partner)
    distances = (2, 1, 3)
    for dr in distances:
        spread_to(me, (lax.rem(replica + dr, replicas), section, tensor))
    z_copies = []
    for i, device in enumerate(along):
        z_copies.append(remote(zs.at[section], zs.at[section], sem["z"], i, device))
        z_copies[-1].start()
    spread_swap(me)
    copies[0].wait_recv()
    for dr in distances:
        spread_to(theirs, (lax.rem(replica + dr, replicas), section, tensor))
    spread_swap(theirs)
    for i, z_at in ((1, chip), (4, 1 - chip)):
        for j, dr in enumerate(distances):
            copies[i + j].wait_recv()
            spread_swap(lax.rem(replica + replicas - dr, replicas) * 4 + z_at * 2 + core)
    for copy in copies:
        copy.wait_send()
    for copy in z_copies:
        copy.wait()
    down_copies = []
    for i, device in enumerate(along):
        down_copies.append(remote(mine.at[pl.ds(0, rank)], down_rows.at[section], sem["downs"], i, device))
        down_copies[-1].start()
    down_rows[section] = mine[:rank]
    for copy in swaps:
        copy.wait()
    join(spread, gram)

    square = jnp.sum(acc[:, 3 * wide :], axis=1, keepdims=True)
    run_layers(
        features, tokens_per, section, counts[replica], zs, square, gram, coef, mixing, hb, rate, a_s, w_s, a_all
    )

    cut(mixing[...], mix_pieces)
    mix_copies = []
    for i, (device, number) in enumerate(peers):
        mix_copies.append(remote(mix_pieces.at[number], mix_box.at[me], sem["mix"], i, device))
        mix_copies[-1].start()
    mix_box[me] = mix_pieces[me]
    order = [(2, 1), (2, 0), (1, 1), (1, 0), (3, 1), (3, 0), (0, 1), (0, 0)]
    first, second = pl.ds(0, rank), pl.ds(rank, rank)

    def ring(dr):
        return (lax.rem(replica + dr, replicas), section, tensor)

    def block_gradient(dr, dz, c):
        number = lax.rem(replica + dr, replicas) * 4 + lax.rem(chip + dz, 2) * 2 + c
        at = pl.ds(pl.multiple_of(number * columns, 128), columns)
        return dot_n(coef[...], both[:, at])

    halves = []
    sends = {}

    def send(number, source, target, device):
        sends[number] = remote(source, target, sem["chip"], number, device)
        sends[number].start()

    for i in range(len(order) + 1):
        if i < len(order):
            parts[i] = block_gradient(*order[i], 1 - core).astype(parts.dtype)
            halves.append(remote(parts.at[i], half.at[i], sem["half"], i, sibling))
            halves[-1].start()
        if i:
            dr, dz = order[i - 1]
            added = block_gradient(dr, dz, core)
            halves[i - 1].wait()
            chips[i - 1] = (added + half[i - 1].astype(jnp.float32)).astype(chips.dtype)
            if dr:
                send(i - 1, chips.at[i - 1, first], inbox.at[i - 1, first], ring(dr))
            if dz:
                send(6 + dr, chips.at[i - 1, second], inbox.at[i - 1, second], partner)
    at = {distance: i for i, distance in enumerate(order)}

    for dr in (2, 1, 3):
        sends[6 + dr].wait_recv()
        i = at[dr, 1]
        parts[i, second] = (chips[at[dr, 0], second].astype(jnp.float32) + inbox[i, second].astype(jnp.float32)).astype(
            parts.dtype
        )
        send(9 + dr, parts.at[i, second], late.at[dr], ring(dr))
    for dz in (1, 0):
        total = chips[at[0, dz], first].astype(jnp.float32)
        for dr in (2, 1, 3):
            sends[at[dr, dz]].wait_recv()
            total = total + inbox[at[dr, dz], first].astype(jnp.float32)
        if dz:
            parts[at[0, 1], first] = total.astype(parts.dtype)
            send(13, parts.at[at[0, 1], first], late.at[0], partner)
        else:
            kept = total
    for copy in mix_copies:
        copy.wait()
    mix_spread[me] = piece_sum(mix_box).astype(mix_spread.dtype)
    mix_copies = []
    for i, (device, number) in enumerate(peers):
        mix_copies.append(remote(mix_spread.at[me], mix_spread.at[me], sem["mixed"], i, device))
        mix_copies[-1].start()
    for copy in mix_copies:
        copy.wait()
    join(mix_spread, mixing)
    for copy in down_copies:
        copy.wait()
    layer_of = lax.broadcasted_iota(jnp.int32, (rank, sections * rank), 1) // rank
    crossing = mixing[:rank]
    nothing = jnp.zeros_like(crossing)
    ups_all = rows[...].reshape(sections * rank, columns)
    downs_all = down_rows[...].reshape(sections * rank, columns)
    gradient[:rank] = dot_n(jnp.where(layer_of < section, crossing, nothing), ups_all)
    gradient[rank:] = dot_n(mixing[rank:], ups_all) + dot_n(
        jnp.where(layer_of > section, crossing, nothing), downs_all
    )
    sends[6].wait_recv()
    total = chips[at[0, 0], second].astype(jnp.float32) + inbox[at[0, 1], second].astype(jnp.float32)
    for dr in (2, 1, 3):
        sends[9 + dr].wait_recv()
        total = total + late[dr].astype(jnp.float32)
    gradient[rank:] += total
    sends[13].wait_recv()
    gradient[:rank] += kept + late[0].astype(jnp.float32)
    for copy in sends.values():
        copy.wait_send()
    share[:rank] = decayed(master_down[...], moment_down[...], second_down[...], gradient[:rank])[0].astype(share.dtype)
    share[rank:] = decayed(master_up[...], moment_up[...], second_up[...], gradient[rank:])[0].astype(share.dtype)
    publish(replicas, sections, share, out, sem["far"], sem["swap"])
    begin, end = bounds[replica, section], bounds[replica, section + 1]
    held, both, own = end > begin, end > begin + 1, begin == section

    @pl.loop(0, features // step)
    def _(i):
        at = pl.ds(pl.multiple_of(i * step, step), step)
        for placed, rows_of in ((placed_down, first), (placed_up, second)):
            this, following = out[0, rows_of, at], out[1, rows_of, at]
            none = jnp.zeros_like(this)
            placed[0, :, at] = jnp.where(held, jnp.where(own, this, following), none)
            placed[1, :, at] = jnp.where(both, following, none)


def run_step(bounds, counts, hidden, last, downs, ups, owned, tokens_per):
    replicas, sections = lax.axis_size("replica"), lax.axis_size("section")
    rank, columns = owned[0].shape
    wide, layers = 2 * rank, sections
    tokens, features = hidden.shape
    size = replicas * 4
    height, width = 16, wide * layers * rank // size // 16
    b16, f32 = jnp.bfloat16, jnp.float32
    hbm, vmem = (pl.BlockSpec(memory_space=m) for m in (pltpu.HBM, pltpu.VMEM))
    piece = pltpu.VMEM((size, height, width), b16)
    block = pltpu.VMEM((size // 2, wide, columns), b16)
    return pl.pallas_call(
        functools.partial(step_kernel, replicas, sections, tokens_per),
        out_shape=(
            jax.ShapeDtypeStruct((wide, columns), f32),
            jax.ShapeDtypeStruct((2, rank, features), b16),
            jax.ShapeDtypeStruct((2, rank, features), b16),
        ),
        in_specs=[hbm] * 12,
        out_specs=(vmem,) * 3,
        scratch_shapes=[
            pltpu.SMEM(bounds.shape, jnp.int32),
            pltpu.SMEM(counts.shape, jnp.int32),
            pltpu.VMEM((6, rank, columns), f32),
            pltpu.VMEM((2, wide, features), b16),
            pltpu.VMEM((2 * tokens, features), b16),
            pltpu.VMEM((2 * wide, features), b16),
            pltpu.VMEM((wide, columns), b16),
            pltpu.VMEM((3, tokens, wide), b16),
            pltpu.VMEM((3, tokens, wide), b16),
            pltpu.VMEM((tokens, 3 * wide + 128), f32),
            pltpu.VMEM((layers, tokens * 3 // 2, wide), b16),
            pltpu.VMEM((layers, rank, columns), b16),
            pltpu.VMEM((layers, rank, columns), b16),
            pltpu.VMEM((layers, wide, layers * rank), b16),
            piece,
            piece,
            pltpu.VMEM((size, sections, height, width), b16),
            pltpu.VMEM((wide, 2 * tokens), b16),
            pltpu.VMEM((wide, layers * rank), b16),
            pltpu.VMEM((layers, tokens, layers * rank), f32),
            pltpu.VMEM((layers, tokens, 1), f32),
            pltpu.VMEM((layers, tokens, rank), b16),
            pltpu.VMEM((layers, tokens, rank), b16),
            pltpu.VMEM((tokens, layers * rank), b16),
            piece,
            piece,
            piece,
            block,
            block,
            block,
            block,
            pltpu.VMEM((replicas, rank, columns), b16),
            pltpu.VMEM((wide, columns), b16),
            pltpu.SemaphoreType.DMA((12,)),
        ]
        + dma_pairs(COUNTS.values()),
        compiler_params=pltpu.CompilerParams(collective_id=1, has_side_effects=True, vmem_limit_bytes=42 * 2**20),
        name="step",
    )(*[pltpu.with_memory_space_constraint(array, pltpu.HBM) for array in (bounds, counts, hidden, last, downs, ups, *owned)])


def on_device(
    inputs, cotangent, micro_counts, bounds, holder_down, holder_up,
    master_down, master_up, moment_down, moment_up, second_down, second_up,
):
    micros, per, features = inputs.shape[1:]
    slots, rank = holder_down.shape[2:4]
    tokens = micros * per
    owned = [array[0] for array in (master_down, master_up, moment_down, moment_up, second_down, second_up)]
    gradient, placed_down, placed_up = run_step(
        bounds,
        micro_counts,
        inputs[0].reshape(tokens, features),
        cotangent[0].reshape(tokens, features),
        holder_down[0, 0].reshape(slots * rank, features),
        holder_up[0, 0].reshape(slots * rank, features),
        owned,
        per,
    )
    new_down = decayed(owned[0], owned[2], owned[4], gradient[:rank])
    new_up = decayed(owned[1], owned[3], owned[5], gradient[rank:])
    news = [array[None] for pair in zip(new_down, new_up) for array in pair]
    return (placed_down[None, None], placed_up[None, None], *news)


def solution(mesh):
    owned = P("section", None, ("replica", "tensor"))
    held = P("replica", "section", None, None, None)
    tokens = P("replica", None, "tensor", None)
    return jax.shard_map(
        on_device,
        mesh=mesh,
        in_specs=(tokens, tokens, P(), P(), held, held) + (owned,) * 6,
        out_specs=(held, held) + (owned,) * 6,
        check_vma=False,
    )
```

```python
import functools
import math

import jax
import jax.numpy as jnp
from jax import lax
from jax.experimental import pallas as pl
from jax.experimental.pallas import tpu as pltpu
from jax.sharding import PartitionSpec as P

norm_eps = 1e-06
learn_rate = 0.01
beta_one = 0.9
beta_two = 0.95
decay_rate = 0.1
adam_eps = 1e-08
first_fix = 0.9999734386011124
second_fix = 0.9940794707796659


def dot_t(left, right):
    return lax.dot_general(
        left, right, (((1,), (1,)), ((), ())), preferred_element_type=jnp.float32
    )


def dot_n(left, right):
    return jnp.dot(left, right, preferred_element_type=jnp.float32)


MESH = pl.DeviceIdType.MESH


def place():
    tensor = lax.axis_index("tensor")
    return lax.axis_index("replica"), lax.axis_index("section"), tensor // 2, tensor % 2


def remote(source, target, sems, at, device):
    return pltpu.make_async_remote_copy(
        src_ref=source, dst_ref=target, send_sem=sems[0].at[at], recv_sem=sems[1].at[at],
        device_id=device, device_id_type=MESH,
    )


def section_peers(replica, section, chip, core, sections):
    return [(replica, lax.rem(section + d, sections), chip * 2 + core) for d in range(1, sections)]


def plane_peers(replica, section, chip, core, replicas):
    found = []
    for dr in range(replicas):
        for dz in range(2):
            for dc in range(2):
                if dr or dz or dc:
                    there = lax.rem(replica + dr, replicas)
                    tensor = lax.rem(chip + dz, 2) * 2 + lax.rem(core + dc, 2)
                    found.append(((there, section, tensor), there * 4 + tensor))
    return found


def piece_sum(box):
    total = box[0].astype(jnp.float32)
    for i in range(1, box.shape[0]):
        total = total + box[i].astype(jnp.float32)
    return total


def cut(value, pieces):
    _, height, width = pieces.shape
    across = value.shape[1] // width
    for i in range(pieces.shape[0]):
        y, x = i // across * height, i % across * width
        pieces[i] = value[y : y + height, x : x + width].astype(pieces.dtype)


def join(spread, whole):
    height, width = spread.shape[-2:]
    across = whole.shape[-1] // width
    for i in range(spread.shape[0]):
        y, x = i // across * height, i % across * width
        whole[..., y : y + height, x : x + width] = spread[i]


def dma_pairs(counts):
    return [pltpu.SemaphoreType.DMA((n,)) for n in counts for _ in range(2)]


def decayed(params, moments, seconds, gradient):
    new_moments = beta_one * moments + (1.0 - beta_one) * gradient
    new_seconds = beta_two * seconds + (1.0 - beta_two) * gradient * gradient
    new_params = params - learn_rate * (
        new_moments / first_fix / (jnp.sqrt(new_seconds / second_fix) + adam_eps)
        + decay_rate * params
    )
    return new_params, new_moments, new_seconds


def run_layers(features, tokens_per, section, counted, z, square, gram, coef, mixing, hb, rate, a_s, w_s, a_all):
    layers, packed, wide = z.shape
    rank, tokens = wide // 2, packed * 2 // 3
    root = 1.0 / math.sqrt(features)
    row = lax.broadcasted_iota(jnp.int32, (tokens, 1), 0)
    taken = row < counted * tokens_per

    def picked(kind, layer):
        if kind < 2:
            found = z[layer, :tokens, kind * rank : (kind + 1) * rank]
        else:
            found = jnp.concatenate([z[layer, tokens:, :rank], z[layer, tokens:, rank:]], axis=0)
        return found.astype(jnp.float32)

    norm = square[...]
    state = jnp.concatenate([picked(1, l) for l in range(layers)], axis=1)
    a_all[...] = jnp.zeros_like(a_all)
    slopes, inner, rhos = [], [], []
    for l in range(layers):
        at = slice(l * rank, (l + 1) * rank)
        hb[l] = state
        rho = lax.rsqrt(jnp.maximum(norm, 0.0) * (1.0 / features) + norm_eps)
        product = picked(0, l)
        if l:
            product = product + dot_t(a_all[...], gram[l, :rank])
        u = product * (rho * root)
        sigma = jax.nn.sigmoid(u)
        active = (u * sigma * (1.0 / math.sqrt(rank))).astype(jnp.bfloat16)
        a_s[l] = active
        a_all[:, at] = active
        added = dot_n(active, gram[l, rank:])
        wide_a = active.astype(jnp.float32)
        norm = norm + jnp.sum(wide_a * (2.0 * state[:, at] + added[:, at]), axis=1, keepdims=True)
        state = state + added
        slopes.append(sigma * (1.0 + u * (1.0 - sigma)) * (1.0 / math.sqrt(rank)))
        inner.append(u)
        rhos.append(rho)
    back = jnp.concatenate(
        [jnp.where(taken, picked(2, l), 0.0) for l in range(layers)], axis=1
    )
    gamma = jnp.zeros((tokens, 1), jnp.float32)
    for l in reversed(range(layers)):
        at = slice(l * rank, (l + 1) * rank)
        e = back[:, at] * slopes[l]
        rho = rhos[l]
        w = (e * (rho * root)).astype(jnp.bfloat16)
        w_s[l] = w
        rate[l] = gamma
        c = rho * rho * jnp.sum(e * inner[l], axis=1, keepdims=True) * (1.0 / features)
        gamma = gamma + c
        if l:
            back = back + dot_n(w, gram[l, :rank]) - c * hb[l]
    own_w = w_s[section].astype(jnp.float32)
    own_a = a_s[section].astype(jnp.float32)
    own_rate = rate[section]
    nothing = jnp.zeros((tokens, rank), jnp.float32)
    left = jnp.concatenate(
        [
            jnp.concatenate([own_w, -own_rate * own_a], axis=1),
            jnp.concatenate([nothing, jnp.where(taken, own_a, 0.0)], axis=1),
        ],
        axis=0,
    )
    coef[...] = left.T.astype(jnp.bfloat16)
    own_left = own_a.T.astype(jnp.bfloat16)
    own_down = own_w.T.astype(jnp.bfloat16)
    before = jnp.concatenate([jnp.where(l < section, a_s[l], jnp.zeros_like(a_s[l])) for l in range(layers)], axis=1)
    beyond = jnp.concatenate([jnp.where(l > section, w_s[l], jnp.zeros_like(w_s[l])) for l in range(layers)], axis=1)
    scaled = jnp.concatenate(
        [
            (jnp.where(l <= section, own_rate, rate[l]) * a_s[l].astype(jnp.float32)).astype(jnp.bfloat16)
            for l in range(layers)
        ],
        axis=1,
    )
    mixing[:rank] = (dot_n(own_down, before) + dot_n(own_left, beyond)).astype(jnp.bfloat16)
    mixing[rank:] = (-dot_n(own_left, scaled)).astype(jnp.bfloat16)


def publish(replicas, sections, share, out, far_sems, core_sems):
    replica, section, chip, core = place()
    columns = share.shape[1]
    before = lax.rem(section + sections - 1, sections)
    other = 1 - chip
    up, down, across = (lax.rem(replica + d, replicas) for d in (1, replicas - 1, 2))
    tensor = chip * 2 + core
    sibling = (replica, section, chip * 2 + 1 - core)
    partner = (replica, section, other * 2 + core)
    above, below = (up, section, tensor), (down, section, tensor)
    rank = share.shape[0] // 2

    def columns_of(r, z):
        return pl.ds(pl.multiple_of((r * 4 + z * 2 + core) * columns, 128), columns)

    def block(window, r, z):
        return out.at[window, :, columns_of(r, z)]

    started = {}
    def send(number, piece, device):
        copy = remote(piece, piece, far_sems, number, device)
        copy.start()
        started[number] = copy

    def landed(*numbers):
        for number in numbers:
            started[number].wait_recv()

    swaps = []

    def swap(window, r, z):
        copy = remote(block(window, r, z), block(window, r, z), core_sems, len(swaps), sibling)
        copy.start()
        swaps.append(copy)

    def half(which, r):
        return out.at[0, pl.ds(which * rank, rank), columns_of(r, chip)]

    own = columns_of(replica, chip)
    for number, device in ((3, (replica, before, tensor)), (4, (replica, before, other * 2 + core))):
        started[number] = remote(share, out.at[1, :, own], far_sems, number, device)
        pl.when(section > 0)(started[number].start)

    @pl.when(section == sections - 1)
    def _():
        out[1, :, own] = share[...]
        out[1, :, columns_of(replica, other)] = share[...]

    out[0, :, own] = share[...]
    send(0, block(0, replica, chip), above)
    send(1, block(0, replica, chip), below)
    swap(0, replica, chip)
    pl.when(section < sections - 1)(started[3].wait_recv)
    send(9, block(1, replica, chip), above)
    send(10, block(1, replica, chip), below)
    pl.when(section < sections - 1)(started[4].wait_recv)
    send(11, block(1, replica, other), above)
    send(12, block(1, replica, other), below)
    send(2, block(0, replica, chip), partner)
    landed(0)
    send(5, half(0, down), above)
    send(6, block(0, down, chip), partner)
    landed(1)
    send(7, half(1, up), below)
    send(8, block(0, up, chip), partner)
    swap(0, down, chip)
    swap(0, up, chip)
    swap(1, replica, chip)
    swap(1, replica, other)
    landed(2)
    swap(0, replica, other)
    landed(5)
    send(13, half(0, across), partner)
    landed(7)
    send(14, half(1, across), partner)
    swap(0, across, chip)
    landed(9)
    send(15, block(1, down, chip), above)
    swap(1, down, chip)
    landed(10)
    swap(1, up, chip)
    landed(12)
    send(16, block(1, up, other), below)
    swap(1, up, other)
    landed(11)
    swap(1, down, other)
    landed(6)
    swap(0, down, other)
    landed(8)
    swap(0, up, other)
    landed(15)
    swap(1, across, chip)
    landed(13, 14)
    swap(0, across, other)
    landed(16)
    swap(1, across, other)
    for number, copy in started.items():
        if number in (3, 4):
            pl.when(section > 0)(copy.wait_send)
        else:
            copy.wait_send()
    for copy in swaps:
        copy.wait()


COUNTS = dict(rows=7, zshift=1, z=7, gram=15, piece=7, plane=7, core=8, downs=7, mix=15, mixed=15, half=8, chip=14, far=17, swap=16)


def step_kernel(
    replicas, sections, tokens_per,
    bounds_hbm, counts_hbm, hidden_hbm, last_hbm, downs_hbm, ups_hbm, *refs,
):
    owned_hbm, refs = refs[:6], refs[6:]
    step_body(
        replicas, sections, tokens_per, bounds_hbm, counts_hbm, hidden_hbm, last_hbm, downs_hbm, ups_hbm, owned_hbm, *refs
    )


def step_body(
    replicas, sections, tokens_per, bounds_hbm, counts_hbm, hidden_hbm, last_hbm, downs_hbm, ups_hbm, owned_hbm,
    gradient, placed_down, placed_up,
    bounds, counts, owned, out, both, weights, mine, z, z_before, acc, zs, rows, down_rows, gram, pieces, box, spread,
    coef, mixing, hb, rate, a_s, w_s, a_all, mix_pieces, mix_box, mix_spread,
    parts, half, chips, inbox, late, share, local, *sems,
):
    sem = {name: sems[2 * i : 2 * i + 2] for i, name in enumerate(COUNTS)}
    replica, section, chip, core = place()
    tensor = chip * 2 + core
    me = replica * 4 + tensor
    _, rank, columns = owned.shape
    master_down, master_up, moment_down, moment_up, second_down, second_up = (owned.at[i] for i in range(6))
    wide = 2 * rank
    tokens, features = both.shape[0] // 2, both.shape[1]
    hidden, last = both.at[pl.ds(0, tokens)], both.at[pl.ds(tokens, tokens)]
    along = section_peers(replica, section, chip, core, sections)
    peers = plane_peers(replica, section, chip, core, replicas)
    sibling = (replica, section, chip * 2 + 1 - core)

    loads = [
        pltpu.make_async_copy(downs_hbm, weights.at[pl.ds(0, wide)], local.at[0]),
        pltpu.make_async_copy(ups_hbm, weights.at[pl.ds(wide, wide)], local.at[1]),
        pltpu.make_async_copy(hidden_hbm, hidden, local.at[2]),
        pltpu.make_async_copy(last_hbm, last, local.at[3]),
    ]
    barrier = pltpu.get_barrier_semaphore()
    everyone = along + [device for device, _ in peers]
    for d in (1, sections - 1):
        everyone.append((replica, lax.rem(section + d, sections), (1 - chip) * 2 + core))
    for device in everyone:
        pl.semaphore_signal(barrier, inc=1, device_id=device, device_id_type=MESH)
    firsts = [pltpu.make_async_copy(owned_hbm[i], owned.at[i], local.at[4 + i]) for i in range(6)]
    firsts.append(pltpu.make_async_copy(bounds_hbm, bounds, local.at[10]))
    firsts.append(pltpu.make_async_copy(counts_hbm, counts, local.at[11]))
    for copy in firsts + loads:
        copy.start()
    for copy in firsts:
        copy.wait()
    mine[:rank] = master_down[...].astype(mine.dtype)
    mine[rank:] = master_up[...].astype(mine.dtype)
    pl.semaphore_wait(barrier, len(everyone))

    row_copies = []
    for i, device in enumerate(along):
        row_copies.append(remote(mine.at[pl.ds(rank, rank)], rows.at[section], sem["rows"], i, device))
        row_copies[-1].start()
    rows[section] = mine[rank:]

    for copy in loads:
        copy.wait()
    acc[...] = jnp.zeros_like(acc)
    step = 1024

    @pl.loop(0, features // step)
    def _(i):
        at = pl.ds(pl.multiple_of(i * step, step), step)
        chunk = hidden[:, at]
        acc[:, : 2 * wide] += dot_t(chunk, weights[:, at])
        acc[:, 2 * wide : 3 * wide] += dot_t(last[:, at], weights[wide:, at])
        squares = chunk.astype(jnp.float32)
        squares = squares * squares
        folded = squares[:, :128]
        for j in range(1, step // 128):
            folded = folded + squares[:, j * 128 : (j + 1) * 128]
        acc[:, 3 * wide :] += folded

    for kind in range(3):
        z[kind] = acc[:, kind * wide : (kind + 1) * wide].astype(z.dtype)

    for copy in row_copies:
        copy.wait()
    z_shift = remote(z, z_before, sem["zshift"], 0, along[0])
    z_shift.start()
    cut(dot_t(mine[...], rows[...].reshape(sections * rank, columns)), pieces)
    copies = []
    for i, (device, number) in enumerate(peers):
        copies.append(remote(pieces.at[number], box.at[me], sem["gram"], i, device))
        copies[-1].start()
    box[me] = pieces[me]
    for copy in copies:
        copy.wait()
    spread[me, section] = piece_sum(box).astype(spread.dtype)
    copies = []
    for i, device in enumerate(along):
        copies.append(remote(spread.at[me, section], spread.at[me, section], sem["piece"], i, device))
        copies[-1].start()
    z_shift.wait()
    here = (bounds[replica, section] == section) & (bounds[replica, section + 1] > section)
    alone = bounds[replica, jnp.maximum(section - 1, 0)] == section
    own = []
    for kind in range(3):
        moved = jnp.where(alone, z_before[kind][:, :rank], z_before[kind][:, rank:])
        own.append(jnp.where(here, z[kind][:, :rank], moved))
    zs[section, :tokens] = jnp.concatenate(own[:2], axis=1)
    zs[section, tokens:] = jnp.concatenate([own[2][: tokens // 2], own[2][tokens // 2 :]], axis=1)
    for copy in copies:
        copy.wait()
    partner = (replica, section, (1 - chip) * 2 + core)
    theirs = replica * 4 + (1 - chip) * 2 + core
    copies, swaps = [], []

    def spread_to(number, device):
        copies.append(remote(spread.at[number], spread.at[number], sem["plane"], len(copies), device))
        copies[-1].start()

    def spread_swap(number):
        swaps.append(remote(spread.at[number], spread.at[number], sem["core"], len(swaps), sibling))
        swaps[-1].start()

    spread_to(me, partner)
    distances = (2, 1, 3)
    for dr in distances:
        spread_to(me, (lax.rem(replica + dr, replicas), section, tensor))
    z_copies = []
    for i, device in enumerate(along):
        z_copies.append(remote(zs.at[section], zs.at[section], sem["z"], i, device))
        z_copies[-1].start()
    spread_swap(me)
    copies[0].wait_recv()
    for dr in distances:
        spread_to(theirs, (lax.rem(replica + dr, replicas), section, tensor))
    spread_swap(theirs)
    for i, z_at in ((1, chip), (4, 1 - chip)):
        for j, dr in enumerate(distances):
            copies[i + j].wait_recv()
            spread_swap(lax.rem(replica + replicas - dr, replicas) * 4 + z_at * 2 + core)
    for copy in copies:
        copy.wait_send()
    for copy in z_copies:
        copy.wait()
    down_copies = []
    for i, device in enumerate(along):
        down_copies.append(remote(mine.at[pl.ds(0, rank)], down_rows.at[section], sem["downs"], i, device))
        down_copies[-1].start()
    down_rows[section] = mine[:rank]
    for copy in swaps:
        copy.wait()
    join(spread, gram)

    square = jnp.sum(acc[:, 3 * wide :], axis=1, keepdims=True)
    run_layers(
        features, tokens_per, section, counts[replica], zs, square, gram, coef, mixing, hb, rate, a_s, w_s, a_all
    )

    cut(mixing[...], mix_pieces)
    mix_copies = []
    for i, (device, number) in enumerate(peers):
        mix_copies.append(remote(mix_pieces.at[number], mix_box.at[me], sem["mix"], i, device))
        mix_copies[-1].start()
    mix_box[me] = mix_pieces[me]
    order = [(2, 1), (2, 0), (1, 1), (1, 0), (3, 1), (3, 0), (0, 1), (0, 0)]
    first, second = pl.ds(0, rank), pl.ds(rank, rank)

    def ring(dr):
        return (lax.rem(replica + dr, replicas), section, tensor)

    def block_gradient(dr, dz, c):
        number = lax.rem(replica + dr, replicas) * 4 + lax.rem(chip + dz, 2) * 2 + c
        at = pl.ds(pl.multiple_of(number * columns, 128), columns)
        return dot_n(coef[...], both[:, at])

    halves = []
    sends = {}

    def send(number, source, target, device):
        sends[number] = remote(source, target, sem["chip"], number, device)
        sends[number].start()

    for i in range(len(order) + 1):
        if i < len(order):
            parts[i] = block_gradient(*order[i], 1 - core).astype(parts.dtype)
            halves.append(remote(parts.at[i], half.at[i], sem["half"], i, sibling))
            halves[-1].start()
        if i:
            dr, dz = order[i - 1]
            added = block_gradient(dr, dz, core)
            halves[i - 1].wait()
            chips[i - 1] = (added + half[i - 1].astype(jnp.float32)).astype(chips.dtype)
            if dr:
                send(i - 1, chips.at[i - 1, first], inbox.at[i - 1, first], ring(dr))
            if dz:
                send(6 + dr, chips.at[i - 1, second], inbox.at[i - 1, second], partner)
    at = {distance: i for i, distance in enumerate(order)}

    for dr in (2, 1, 3):
        sends[6 + dr].wait_recv()
        i = at[dr, 1]
        parts[i, second] = (chips[at[dr, 0], second].astype(jnp.float32) + inbox[i, second].astype(jnp.float32)).astype(
            parts.dtype
        )
        send(9 + dr, parts.at[i, second], late.at[dr], ring(dr))
    for dz in (1, 0):
        total = chips[at[0, dz], first].astype(jnp.float32)
        for dr in (2, 1, 3):
            sends[at[dr, dz]].wait_recv()
            total = total + inbox[at[dr, dz], first].astype(jnp.float32)
        if dz:
            parts[at[0, 1], first] = total.astype(parts.dtype)
            send(13, parts.at[at[0, 1], first], late.at[0], partner)
        else:
            kept = total
    for copy in mix_copies:
        copy.wait()
    mix_spread[me] = piece_sum(mix_box).astype(mix_spread.dtype)
    mix_copies = []
    for i, (device, number) in enumerate(peers):
        mix_copies.append(remote(mix_spread.at[me], mix_spread.at[me], sem["mixed"], i, device))
        mix_copies[-1].start()
    for copy in mix_copies:
        copy.wait()
    join(mix_spread, mixing)
    for copy in down_copies:
        copy.wait()
    layer_of = lax.broadcasted_iota(jnp.int32, (rank, sections * rank), 1) // rank
    crossing = mixing[:rank]
    nothing = jnp.zeros_like(crossing)
    ups_all = rows[...].reshape(sections * rank, columns)
    downs_all = down_rows[...].reshape(sections * rank, columns)
    gradient[:rank] = dot_n(jnp.where(layer_of < section, crossing, nothing), ups_all)
    gradient[rank:] = dot_n(mixing[rank:], ups_all) + dot_n(
        jnp.where(layer_of > section, crossing, nothing), downs_all
    )
    sends[6].wait_recv()
    total = chips[at[0, 0], second].astype(jnp.float32) + inbox[at[0, 1], second].astype(jnp.float32)
    for dr in (2, 1, 3):
        sends[9 + dr].wait_recv()
        total = total + late[dr].astype(jnp.float32)
    gradient[rank:] += total
    sends[13].wait_recv()
    gradient[:rank] += kept + late[0].astype(jnp.float32)
    for copy in sends.values():
        copy.wait_send()
    share[:rank] = decayed(master_down[...], moment_down[...], second_down[...], gradient[:rank])[0].astype(share.dtype)
    share[rank:] = decayed(master_up[...], moment_up[...], second_up[...], gradient[rank:])[0].astype(share.dtype)
    publish(replicas, sections, share, out, sem["far"], sem["swap"])
    begin, end = bounds[replica, section], bounds[replica, section + 1]
    held, both, own = end > begin, end > begin + 1, begin == section

    @pl.loop(0, features // step)
    def _(i):
        at = pl.ds(pl.multiple_of(i * step, step), step)
        for placed, rows_of in ((placed_down, first), (placed_up, second)):
            this, following = out[0, rows_of, at], out[1, rows_of, at]
            none = jnp.zeros_like(this)
            placed[0, :, at] = jnp.where(held, jnp.where(own, this, following), none)
            placed[1, :, at] = jnp.where(both, following, none)


def run_step(bounds, counts, hidden, last, downs, ups, owned, tokens_per):
    replicas, sections = lax.axis_size("replica"), lax.axis_size("section")
    rank, columns = owned[0].shape
    wide, layers = 2 * rank, sections
    tokens, features = hidden.shape
    size = replicas * 4
    height, width = 16, wide * layers * rank // size // 16
    b16, f32 = jnp.bfloat16, jnp.float32
    hbm, vmem = (pl.BlockSpec(memory_space=m) for m in (pltpu.HBM, pltpu.VMEM))
    piece = pltpu.VMEM((size, height, width), b16)
    block = pltpu.VMEM((size // 2, wide, columns), b16)
    return pl.pallas_call(
        functools.partial(step_kernel, replicas, sections, tokens_per),
        out_shape=(
            jax.ShapeDtypeStruct((wide, columns), f32),
            jax.ShapeDtypeStruct((2, rank, features), b16),
            jax.ShapeDtypeStruct((2, rank, features), b16),
        ),
        in_specs=[hbm] * 12,
        out_specs=(vmem,) * 3,
        scratch_shapes=[
            pltpu.SMEM(bounds.shape, jnp.int32),
            pltpu.SMEM(counts.shape, jnp.int32),
            pltpu.VMEM((6, rank, columns), f32),
            pltpu.VMEM((2, wide, features), b16),
            pltpu.VMEM((2 * tokens, features), b16),
            pltpu.VMEM((2 * wide, features), b16),
            pltpu.VMEM((wide, columns), b16),
            pltpu.VMEM((3, tokens, wide), b16),
            pltpu.VMEM((3, tokens, wide), b16),
            pltpu.VMEM((tokens, 3 * wide + 128), f32),
            pltpu.VMEM((layers, tokens * 3 // 2, wide), b16),
            pltpu.VMEM((layers, rank, columns), b16),
            pltpu.VMEM((layers, rank, columns), b16),
            pltpu.VMEM((layers, wide, layers * rank), b16),
            piece,
            piece,
            pltpu.VMEM((size, sections, height, width), b16),
            pltpu.VMEM((wide, 2 * tokens), b16),
            pltpu.VMEM((wide, layers * rank), b16),
            pltpu.VMEM((layers, tokens, layers * rank), f32),
            pltpu.VMEM((layers, tokens, 1), f32),
            pltpu.VMEM((layers, tokens, rank), b16),
            pltpu.VMEM((layers, tokens, rank), b16),
            pltpu.VMEM((tokens, layers * rank), b16),
            piece,
            piece,
            piece,
            block,
            block,
            block,
            block,
            pltpu.VMEM((replicas, rank, columns), b16),
            pltpu.VMEM((wide, columns), b16),
            pltpu.SemaphoreType.DMA((12,)),
        ]
        + dma_pairs(COUNTS.values()),
        compiler_params=pltpu.CompilerParams(collective_id=1, has_side_effects=True, vmem_limit_bytes=42 * 2**20),
        name="step",
    )(*[pltpu.with_memory_space_constraint(array, pltpu.HBM) for array in (bounds, counts, hidden, last, downs, ups, *owned)])


def on_device(
    inputs, cotangent, micro_counts, bounds, holder_down, holder_up,
    master_down, master_up, moment_down, moment_up, second_down, second_up,
):
    micros, per, features = inputs.shape[1:]
    slots, rank = holder_down.shape[2:4]
    tokens = micros * per
    owned = [array[0] for array in (master_down, master_up, moment_down, moment_up, second_down, second_up)]
    gradient, placed_down, placed_up = run_step(
        bounds,
        micro_counts,
        inputs[0].reshape(tokens, features),
        cotangent[0].reshape(tokens, features),
        holder_down[0, 0].reshape(slots * rank, features),
        holder_up[0, 0].reshape(slots * rank, features),
        owned,
        per,
    )
    new_down = decayed(owned[0], owned[2], owned[4], gradient[:rank])
    new_up = decayed(owned[1], owned[3], owned[5], gradient[rank:])
    news = [array[None] for pair in zip(new_down, new_up) for array in pair]
    return (placed_down[None, None], placed_up[None, None], *news)


def solution(mesh):
    owned = P("section", None, ("replica", "tensor"))
    held = P("replica", "section", None, None, None)
    tokens = P("replica", None, "tensor", None)
    return jax.shard_map(
        on_device,
        mesh=mesh,
        in_specs=(tokens, tokens, P(), P(), held, held) + (owned,) * 6,
        out_specs=(held, held) + (owned,) * 6,
        check_vma=False,
    )
```

```python
import functools
import math

import jax
import jax.numpy as jnp
from jax import lax
from jax.experimental import pallas as pl
from jax.experimental.pallas import tpu as pltpu
from jax.sharding import PartitionSpec as P

norm_eps = 1e-06
learn_rate = 0.01
beta_one = 0.9
beta_two = 0.95
decay_rate = 0.1
adam_eps = 1e-08
first_fix = 0.9999734386011124
second_fix = 0.9940794707796659


def dot_t(left, right):
    return lax.dot_general(
        left, right, (((1,), (1,)), ((), ())), preferred_element_type=jnp.float32
    )


def dot_n(left, right):
    return jnp.dot(left, right, preferred_element_type=jnp.float32)


MESH = pl.DeviceIdType.MESH


def place():
    tensor = lax.axis_index("tensor")
    return lax.axis_index("replica"), lax.axis_index("section"), tensor // 2, tensor % 2


def remote(source, target, sems, at, device):
    return pltpu.make_async_remote_copy(
        src_ref=source, dst_ref=target, send_sem=sems[0].at[at], recv_sem=sems[1].at[at],
        device_id=device, device_id_type=MESH,
    )


def section_peers(replica, section, chip, core, sections):
    return [(replica, lax.rem(section + d, sections), chip * 2 + core) for d in range(1, sections)]


def plane_peers(replica, section, chip, core, replicas):
    found = []
    for dr in range(replicas):
        for dz in range(2):
            for dc in range(2):
                if dr or dz or dc:
                    there = lax.rem(replica + dr, replicas)
                    tensor = lax.rem(chip + dz, 2) * 2 + lax.rem(core + dc, 2)
                    found.append(((there, section, tensor), there * 4 + tensor))
    return found


def piece_sum(box):
    total = box[0].astype(jnp.float32)
    for i in range(1, box.shape[0]):
        total = total + box[i].astype(jnp.float32)
    return total


def cut(value, pieces):
    _, height, width = pieces.shape
    across = value.shape[1] // width
    for i in range(pieces.shape[0]):
        y, x = i // across * height, i % across * width
        pieces[i] = value[y : y + height, x : x + width].astype(pieces.dtype)


def join(spread, whole):
    height, width = spread.shape[-2:]
    across = whole.shape[-1] // width
    for i in range(spread.shape[0]):
        y, x = i // across * height, i % across * width
        whole[..., y : y + height, x : x + width] = spread[i]


def dma_pairs(counts):
    return [pltpu.SemaphoreType.DMA((n,)) for n in counts for _ in range(2)]


def decayed(params, moments, seconds, gradient):
    new_moments = beta_one * moments + (1.0 - beta_one) * gradient
    new_seconds = beta_two * seconds + (1.0 - beta_two) * gradient * gradient
    new_params = params - learn_rate * (
        new_moments / first_fix / (jnp.sqrt(new_seconds / second_fix) + adam_eps)
        + decay_rate * params
    )
    return new_params, new_moments, new_seconds


def run_layers(features, tokens_per, section, counted, z, square, gram, coef, mixing, hb, rate, a_s, w_s, a_all):
    layers, packed, wide = z.shape
    rank, tokens = wide // 2, packed * 2 // 3
    root = 1.0 / math.sqrt(features)
    row = lax.broadcasted_iota(jnp.int32, (tokens, 1), 0)
    taken = row < counted * tokens_per

    def picked(kind, layer):
        if kind < 2:
            found = z[layer, :tokens, kind * rank : (kind + 1) * rank]
        else:
            found = jnp.concatenate([z[layer, tokens:, :rank], z[layer, tokens:, rank:]], axis=0)
        return found.astype(jnp.float32)

    norm = square[...]
    state = jnp.concatenate([picked(1, l) for l in range(layers)], axis=1)
    a_all[...] = jnp.zeros_like(a_all)
    slopes, inner, rhos = [], [], []
    for l in range(layers):
        at = slice(l * rank, (l + 1) * rank)
        hb[l] = state
        rho = lax.rsqrt(jnp.maximum(norm, 0.0) * (1.0 / features) + norm_eps)
        product = picked(0, l)
        if l:
            product = product + dot_t(a_all[...], gram[l, :rank])
        u = product * (rho * root)
        sigma = jax.nn.sigmoid(u)
        active = (u * sigma * (1.0 / math.sqrt(rank))).astype(jnp.bfloat16)
        a_s[l] = active
        a_all[:, at] = active
        added = dot_n(active, gram[l, rank:])
        wide_a = active.astype(jnp.float32)
        norm = norm + jnp.sum(wide_a * (2.0 * state[:, at] + added[:, at]), axis=1, keepdims=True)
        state = state + added
        slopes.append(sigma * (1.0 + u * (1.0 - sigma)) * (1.0 / math.sqrt(rank)))
        inner.append(u)
        rhos.append(rho)
    back = jnp.concatenate(
        [jnp.where(taken, picked(2, l), 0.0) for l in range(layers)], axis=1
    )
    gamma = jnp.zeros((tokens, 1), jnp.float32)
    for l in reversed(range(layers)):
        at = slice(l * rank, (l + 1) * rank)
        e = back[:, at] * slopes[l]
        rho = rhos[l]
        w = (e * (rho * root)).astype(jnp.bfloat16)
        w_s[l] = w
        rate[l] = gamma
        c = rho * rho * jnp.sum(e * inner[l], axis=1, keepdims=True) * (1.0 / features)
        gamma = gamma + c
        if l:
            back = back + dot_n(w, gram[l, :rank]) - c * hb[l]
    own_w = w_s[section].astype(jnp.float32)
    own_a = a_s[section].astype(jnp.float32)
    own_rate = rate[section]
    nothing = jnp.zeros((tokens, rank), jnp.float32)
    left = jnp.concatenate(
        [
            jnp.concatenate([own_w, -own_rate * own_a], axis=1),
            jnp.concatenate([nothing, jnp.where(taken, own_a, 0.0)], axis=1),
        ],
        axis=0,
    )
    coef[...] = left.T.astype(jnp.bfloat16)
    own_left = own_a.T.astype(jnp.bfloat16)
    own_down = own_w.T.astype(jnp.bfloat16)
    before = jnp.concatenate([jnp.where(l < section, a_s[l], jnp.zeros_like(a_s[l])) for l in range(layers)], axis=1)
    beyond = jnp.concatenate([jnp.where(l > section, w_s[l], jnp.zeros_like(w_s[l])) for l in range(layers)], axis=1)
    scaled = jnp.concatenate(
        [
            (jnp.where(l <= section, own_rate, rate[l]) * a_s[l].astype(jnp.float32)).astype(jnp.bfloat16)
            for l in range(layers)
        ],
        axis=1,
    )
    mixing[:rank] = (dot_n(own_down, before) + dot_n(own_left, beyond)).astype(jnp.bfloat16)
    mixing[rank:] = (-dot_n(own_left, scaled)).astype(jnp.bfloat16)


def publish(replicas, sections, share, out, far_sems, core_sems):
    replica, section, chip, core = place()
    columns = share.shape[1]
    before = lax.rem(section + sections - 1, sections)
    other = 1 - chip
    up, down, across = (lax.rem(replica + d, replicas) for d in (1, replicas - 1, 2))
    tensor = chip * 2 + core
    sibling = (replica, section, chip * 2 + 1 - core)
    partner = (replica, section, other * 2 + core)
    above, below = (up, section, tensor), (down, section, tensor)
    rank = share.shape[0] // 2

    def columns_of(r, z):
        return pl.ds(pl.multiple_of((r * 4 + z * 2 + core) * columns, 128), columns)

    def block(window, r, z):
        return out.at[window, :, columns_of(r, z)]

    started = {}
    def send(number, piece, device):
        copy = remote(piece, piece, far_sems, number, device)
        copy.start()
        started[number] = copy

    def landed(*numbers):
        for number in numbers:
            started[number].wait_recv()

    swaps = []

    def swap(window, r, z):
        copy = remote(block(window, r, z), block(window, r, z), core_sems, len(swaps), sibling)
        copy.start()
        swaps.append(copy)

    def half(which, r):
        return out.at[0, pl.ds(which * rank, rank), columns_of(r, chip)]

    own = columns_of(replica, chip)
    for number, device in ((3, (replica, before, tensor)), (4, (replica, before, other * 2 + core))):
        started[number] = remote(share, out.at[1, :, own], far_sems, number, device)
        pl.when(section > 0)(started[number].start)

    @pl.when(section == sections - 1)
    def _():
        out[1, :, own] = share[...]
        out[1, :, columns_of(replica, other)] = share[...]

    out[0, :, own] = share[...]
    send(0, block(0, replica, chip), above)
    send(1, block(0, replica, chip), below)
    swap(0, replica, chip)
    pl.when(section < sections - 1)(started[3].wait_recv)
    send(9, block(1, replica, chip), above)
    send(10, block(1, replica, chip), below)
    send(2, block(0, replica, chip), partner)
    landed(0)
    send(5, half(0, down), above)
    send(6, block(0, down, chip), partner)
    landed(1)
    send(7, half(1, up), below)
    send(8, block(0, up, chip), partner)
    pl.when(section < sections - 1)(started[4].wait_recv)
    send(11, block(1, replica, other), above)
    send(12, block(1, replica, other), below)
    swap(0, down, chip)
    swap(0, up, chip)
    swap(1, replica, chip)
    swap(1, replica, other)
    landed(2)
    swap(0, replica, other)
    landed(5)
    send(13, half(0, across), partner)
    landed(7)
    send(14, half(1, across), partner)
    swap(0, across, chip)
    landed(9)
    send(15, block(1, down, chip), above)
    swap(1, down, chip)
    landed(10)
    swap(1, up, chip)
    landed(12)
    send(16, block(1, up, other), below)
    swap(1, up, other)
    landed(11)
    swap(1, down, other)
    landed(6)
    swap(0, down, other)
    landed(8)
    swap(0, up, other)
    landed(15)
    swap(1, across, chip)
    landed(13, 14)
    swap(0, across, other)
    landed(16)
    swap(1, across, other)
    for number, copy in started.items():
        if number in (3, 4):
            pl.when(section > 0)(copy.wait_send)
        else:
            copy.wait_send()
    for copy in swaps:
        copy.wait()


COUNTS = dict(rows=7, zshift=1, z=7, gram=15, piece=7, plane=7, core=8, downs=7, mix=15, mixed=15, half=8, chip=14, far=17, swap=16)


def step_kernel(
    replicas, sections, tokens_per,
    bounds_hbm, counts_hbm, hidden_hbm, last_hbm, downs_hbm, ups_hbm, *refs,
):
    owned_hbm, refs = refs[:6], refs[6:]
    step_body(
        replicas, sections, tokens_per, bounds_hbm, counts_hbm, hidden_hbm, last_hbm, downs_hbm, ups_hbm, owned_hbm, *refs
    )


def step_body(
    replicas, sections, tokens_per, bounds_hbm, counts_hbm, hidden_hbm, last_hbm, downs_hbm, ups_hbm, owned_hbm,
    gradient, placed_down, placed_up,
    bounds, counts, owned, out, both, weights, mine, z, z_before, acc, zs, rows, down_rows, gram, pieces, box, spread,
    coef, mixing, hb, rate, a_s, w_s, a_all, mix_pieces, mix_box, mix_spread,
    parts, half, chips, inbox, late, share, local, *sems,
):
    sem = {name: sems[2 * i : 2 * i + 2] for i, name in enumerate(COUNTS)}
    replica, section, chip, core = place()
    tensor = chip * 2 + core
    me = replica * 4 + tensor
    _, rank, columns = owned.shape
    master_down, master_up, moment_down, moment_up, second_down, second_up = (owned.at[i] for i in range(6))
    wide = 2 * rank
    tokens, features = both.shape[0] // 2, both.shape[1]
    hidden, last = both.at[pl.ds(0, tokens)], both.at[pl.ds(tokens, tokens)]
    along = section_peers(replica, section, chip, core, sections)
    peers = plane_peers(replica, section, chip, core, replicas)
    sibling = (replica, section, chip * 2 + 1 - core)

    loads = [
        pltpu.make_async_copy(downs_hbm, weights.at[pl.ds(0, wide)], local.at[0]),
        pltpu.make_async_copy(ups_hbm, weights.at[pl.ds(wide, wide)], local.at[1]),
        pltpu.make_async_copy(hidden_hbm, hidden, local.at[2]),
        pltpu.make_async_copy(last_hbm, last, local.at[3]),
    ]
    barrier = pltpu.get_barrier_semaphore()
    everyone = along + [device for device, _ in peers]
    for d in (1, sections - 1):
        everyone.append((replica, lax.rem(section + d, sections), (1 - chip) * 2 + core))
    for device in everyone:
        pl.semaphore_signal(barrier, inc=1, device_id=device, device_id_type=MESH)
    firsts = [pltpu.make_async_copy(owned_hbm[i], owned.at[i], local.at[4 + i]) for i in range(6)]
    firsts.append(pltpu.make_async_copy(bounds_hbm, bounds, local.at[10]))
    firsts.append(pltpu.make_async_copy(counts_hbm, counts, local.at[11]))
    for copy in firsts + loads:
        copy.start()
    for copy in firsts:
        copy.wait()
    mine[:rank] = master_down[...].astype(mine.dtype)
    mine[rank:] = master_up[...].astype(mine.dtype)
    pl.semaphore_wait(barrier, len(everyone))

    row_copies = []
    for i, device in enumerate(along):
        row_copies.append(remote(mine.at[pl.ds(rank, rank)], rows.at[section], sem["rows"], i, device))
        row_copies[-1].start()
    rows[section] = mine[rank:]

    for copy in loads:
        copy.wait()
    acc[...] = jnp.zeros_like(acc)
    step = 1024

    @pl.loop(0, features // step)
    def _(i):
        at = pl.ds(pl.multiple_of(i * step, step), step)
        chunk = hidden[:, at]
        acc[:, : 2 * wide] += dot_t(chunk, weights[:, at])
        acc[:, 2 * wide : 3 * wide] += dot_t(last[:, at], weights[wide:, at])
        squares = chunk.astype(jnp.float32)
        squares = squares * squares
        folded = squares[:, :128]
        for j in range(1, step // 128):
            folded = folded + squares[:, j * 128 : (j + 1) * 128]
        acc[:, 3 * wide :] += folded

    for kind in range(3):
        z[kind] = acc[:, kind * wide : (kind + 1) * wide].astype(z.dtype)
    z_shift = remote(z, z_before, sem["zshift"], 0, along[0])
    z_shift.start()

    for copy in row_copies:
        copy.wait()
    cut(dot_t(mine[...], rows[...].reshape(sections * rank, columns)), pieces)
    copies = []
    for i, (device, number) in enumerate(peers):
        copies.append(remote(pieces.at[number], box.at[me], sem["gram"], i, device))
        copies[-1].start()
    box[me] = pieces[me]
    z_shift.wait()
    here = (bounds[replica, section] == section) & (bounds[replica, section + 1] > section)
    alone = bounds[replica, jnp.maximum(section - 1, 0)] == section
    own = []
    for kind in range(3):
        moved = jnp.where(alone, z_before[kind][:, :rank], z_before[kind][:, rank:])
        own.append(jnp.where(here, z[kind][:, :rank], moved))
    zs[section, :tokens] = jnp.concatenate(own[:2], axis=1)
    zs[section, tokens:] = jnp.concatenate([own[2][: tokens // 2], own[2][tokens // 2 :]], axis=1)
    z_copies = []
    for i, device in enumerate(along):
        z_copies.append(remote(zs.at[section], zs.at[section], sem["z"], i, device))
        z_copies[-1].start()
    for copy in copies:
        copy.wait()
    spread[me, section] = piece_sum(box).astype(spread.dtype)
    copies = []
    for i, device in enumerate(along):
        copies.append(remote(spread.at[me, section], spread.at[me, section], sem["piece"], i, device))
        copies[-1].start()
    for copy in copies:
        copy.wait()
    partner = (replica, section, (1 - chip) * 2 + core)
    theirs = replica * 4 + (1 - chip) * 2 + core
    copies, swaps = [], []

    def spread_to(number, device):
        copies.append(remote(spread.at[number], spread.at[number], sem["plane"], len(copies), device))
        copies[-1].start()

    def spread_swap(number):
        swaps.append(remote(spread.at[number], spread.at[number], sem["core"], len(swaps), sibling))
        swaps[-1].start()

    spread_to(me, partner)
    distances = (2, 1, 3)
    for dr in distances:
        spread_to(me, (lax.rem(replica + dr, replicas), section, tensor))
    spread_swap(me)
    copies[0].wait_recv()
    for dr in distances:
        spread_to(theirs, (lax.rem(replica + dr, replicas), section, tensor))
    spread_swap(theirs)
    for i, z_at in ((1, chip), (4, 1 - chip)):
        for j, dr in enumerate(distances):
            copies[i + j].wait_recv()
            spread_swap(lax.rem(replica + replicas - dr, replicas) * 4 + z_at * 2 + core)
    for copy in copies:
        copy.wait_send()
    for copy in z_copies:
        copy.wait()
    down_copies = []
    for i, device in enumerate(along):
        down_copies.append(remote(mine.at[pl.ds(0, rank)], down_rows.at[section], sem["downs"], i, device))
        down_copies[-1].start()
    down_rows[section] = mine[:rank]
    for copy in swaps:
        copy.wait()
    join(spread, gram)

    square = jnp.sum(acc[:, 3 * wide :], axis=1, keepdims=True)
    run_layers(
        features, tokens_per, section, counts[replica], zs, square, gram, coef, mixing, hb, rate, a_s, w_s, a_all
    )

    cut(mixing[...], mix_pieces)
    mix_copies = []
    for i, (device, number) in enumerate(peers):
        mix_copies.append(remote(mix_pieces.at[number], mix_box.at[me], sem["mix"], i, device))
        mix_copies[-1].start()
    mix_box[me] = mix_pieces[me]
    order = [(2, 1), (2, 0), (1, 1), (1, 0), (3, 1), (3, 0), (0, 1), (0, 0)]
    first, second = pl.ds(0, rank), pl.ds(rank, rank)

    def ring(dr):
        return (lax.rem(replica + dr, replicas), section, tensor)

    def block_gradient(dr, dz, c):
        number = lax.rem(replica + dr, replicas) * 4 + lax.rem(chip + dz, 2) * 2 + c
        at = pl.ds(pl.multiple_of(number * columns, 128), columns)
        return dot_n(coef[...], both[:, at])

    halves = []
    sends = {}

    def send(number, source, target, device):
        sends[number] = remote(source, target, sem["chip"], number, device)
        sends[number].start()

    for i in range(len(order) + 1):
        if i < len(order):
            parts[i] = block_gradient(*order[i], 1 - core).astype(parts.dtype)
            halves.append(remote(parts.at[i], half.at[i], sem["half"], i, sibling))
            halves[-1].start()
        if i:
            dr, dz = order[i - 1]
            added = block_gradient(dr, dz, core)
            halves[i - 1].wait()
            chips[i - 1] = (added + half[i - 1].astype(jnp.float32)).astype(chips.dtype)
            if dr:
                send(i - 1, chips.at[i - 1, first], inbox.at[i - 1, first], ring(dr))
            if dz:
                send(6 + dr, chips.at[i - 1, second], inbox.at[i - 1, second], partner)
    at = {distance: i for i, distance in enumerate(order)}

    for dr in (2, 1, 3):
        sends[6 + dr].wait_recv()
        i = at[dr, 1]
        parts[i, second] = (chips[at[dr, 0], second].astype(jnp.float32) + inbox[i, second].astype(jnp.float32)).astype(
            parts.dtype
        )
        send(9 + dr, parts.at[i, second], late.at[dr], ring(dr))
    for dz in (1, 0):
        total = chips[at[0, dz], first].astype(jnp.float32)
        for dr in (2, 1, 3):
            sends[at[dr, dz]].wait_recv()
            total = total + inbox[at[dr, dz], first].astype(jnp.float32)
        if dz:
            parts[at[0, 1], first] = total.astype(parts.dtype)
            send(13, parts.at[at[0, 1], first], late.at[0], partner)
        else:
            kept = total
    for copy in mix_copies:
        copy.wait()
    mix_spread[me] = piece_sum(mix_box).astype(mix_spread.dtype)
    mix_copies = []
    for i, (device, number) in enumerate(peers):
        mix_copies.append(remote(mix_spread.at[me], mix_spread.at[me], sem["mixed"], i, device))
        mix_copies[-1].start()
    for copy in mix_copies:
        copy.wait()
    join(mix_spread, mixing)
    for copy in down_copies:
        copy.wait()
    layer_of = lax.broadcasted_iota(jnp.int32, (rank, sections * rank), 1) // rank
    crossing = mixing[:rank]
    nothing = jnp.zeros_like(crossing)
    ups_all = rows[...].reshape(sections * rank, columns)
    downs_all = down_rows[...].reshape(sections * rank, columns)
    gradient[:rank] = dot_n(jnp.where(layer_of < section, crossing, nothing), ups_all)
    gradient[rank:] = dot_n(mixing[rank:], ups_all) + dot_n(
        jnp.where(layer_of > section, crossing, nothing), downs_all
    )
    sends[6].wait_recv()
    total = chips[at[0, 0], second].astype(jnp.float32) + inbox[at[0, 1], second].astype(jnp.float32)
    for dr in (2, 1, 3):
        sends[9 + dr].wait_recv()
        total = total + late[dr].astype(jnp.float32)
    gradient[rank:] += total
    sends[13].wait_recv()
    gradient[:rank] += kept + late[0].astype(jnp.float32)
    for copy in sends.values():
        copy.wait_send()
    share[:rank] = decayed(master_down[...], moment_down[...], second_down[...], gradient[:rank])[0].astype(share.dtype)
    share[rank:] = decayed(master_up[...], moment_up[...], second_up[...], gradient[rank:])[0].astype(share.dtype)
    publish(replicas, sections, share, out, sem["far"], sem["swap"])
    begin, end = bounds[replica, section], bounds[replica, section + 1]
    held, both, own = end > begin, end > begin + 1, begin == section

    @pl.loop(0, features // step)
    def _(i):
        at = pl.ds(pl.multiple_of(i * step, step), step)
        for placed, rows_of in ((placed_down, first), (placed_up, second)):
            this, following = out[0, rows_of, at], out[1, rows_of, at]
            none = jnp.zeros_like(this)
            placed[0, :, at] = jnp.where(held, jnp.where(own, this, following), none)
            placed[1, :, at] = jnp.where(both, following, none)


def run_step(bounds, counts, hidden, last, downs, ups, owned, tokens_per):
    replicas, sections = lax.axis_size("replica"), lax.axis_size("section")
    rank, columns = owned[0].shape
    wide, layers = 2 * rank, sections
    tokens, features = hidden.shape
    size = replicas * 4
    height, width = 16, wide * layers * rank // size // 16
    b16, f32 = jnp.bfloat16, jnp.float32
    hbm, vmem = (pl.BlockSpec(memory_space=m) for m in (pltpu.HBM, pltpu.VMEM))
    piece = pltpu.VMEM((size, height, width), b16)
    block = pltpu.VMEM((size // 2, wide, columns), b16)
    return pl.pallas_call(
        functools.partial(step_kernel, replicas, sections, tokens_per),
        out_shape=(
            jax.ShapeDtypeStruct((wide, columns), f32),
            jax.ShapeDtypeStruct((2, rank, features), b16),
            jax.ShapeDtypeStruct((2, rank, features), b16),
        ),
        in_specs=[hbm] * 12,
        out_specs=(vmem,) * 3,
        scratch_shapes=[
            pltpu.SMEM(bounds.shape, jnp.int32),
            pltpu.SMEM(counts.shape, jnp.int32),
            pltpu.VMEM((6, rank, columns), f32),
            pltpu.VMEM((2, wide, features), b16),
            pltpu.VMEM((2 * tokens, features), b16),
            pltpu.VMEM((2 * wide, features), b16),
            pltpu.VMEM((wide, columns), b16),
            pltpu.VMEM((3, tokens, wide), b16),
            pltpu.VMEM((3, tokens, wide), b16),
            pltpu.VMEM((tokens, 3 * wide + 128), f32),
            pltpu.VMEM((layers, tokens * 3 // 2, wide), b16),
            pltpu.VMEM((layers, rank, columns), b16),
            pltpu.VMEM((layers, rank, columns), b16),
            pltpu.VMEM((layers, wide, layers * rank), b16),
            piece,
            piece,
            pltpu.VMEM((size, sections, height, width), b16),
            pltpu.VMEM((wide, 2 * tokens), b16),
            pltpu.VMEM((wide, layers * rank), b16),
            pltpu.VMEM((layers, tokens, layers * rank), f32),
            pltpu.VMEM((layers, tokens, 1), f32),
            pltpu.VMEM((layers, tokens, rank), b16),
            pltpu.VMEM((layers, tokens, rank), b16),
            pltpu.VMEM((tokens, layers * rank), b16),
            piece,
            piece,
            piece,
            block,
            block,
            block,
            block,
            pltpu.VMEM((replicas, rank, columns), b16),
            pltpu.VMEM((wide, columns), b16),
            pltpu.SemaphoreType.DMA((12,)),
        ]
        + dma_pairs(COUNTS.values()),
        compiler_params=pltpu.CompilerParams(collective_id=1, has_side_effects=True, vmem_limit_bytes=42 * 2**20),
        name="step",
    )(*[pltpu.with_memory_space_constraint(array, pltpu.HBM) for array in (bounds, counts, hidden, last, downs, ups, *owned)])


def finish_kernel(placed_down, placed_up, gradient, *refs):
    owned, (new_down, new_up), news = refs[:6], refs[6:8], refs[8:14]
    held, sems = refs[14:]
    copies = [
        pltpu.make_async_copy(placed_down, new_down, sems.at[0]),
        pltpu.make_async_copy(placed_up, new_up, sems.at[1]),
    ]
    for copy in copies:
        copy.start()
    rank = owned[0].shape[0]
    for kind in range(2):
        rows = slice(kind * rank, (kind + 1) * rank)
        values = decayed(owned[kind][...], owned[2 + kind][...], owned[4 + kind][...], gradient[rows])
        for i, value in enumerate(values):
            number = 2 * i + kind
            held[number] = value
            copies.append(pltpu.make_async_copy(held.at[number], news[number], sems.at[2 + number]))
            copies[-1].start()
    for copy in copies:
        copy.wait()


def finish(placed_down, placed_up, gradient, owned):
    hbm, vmem = (pl.BlockSpec(memory_space=m) for m in (pl.ANY, pltpu.VMEM))
    like = [jax.ShapeDtypeStruct(array.shape, array.dtype) for array in (placed_down, placed_up, *owned)]
    return pl.pallas_call(
        finish_kernel,
        out_shape=like,
        in_specs=[vmem] * 9,
        out_specs=[hbm] * 8,
        scratch_shapes=[pltpu.VMEM((6,) + owned[0].shape, jnp.float32), pltpu.SemaphoreType.DMA((8,))],
        compiler_params=pltpu.CompilerParams(vmem_limit_bytes=16 * 2**20),
        name="finish",
    )(placed_down, placed_up, gradient, *owned)


def on_device(
    inputs, cotangent, micro_counts, bounds, holder_down, holder_up,
    master_down, master_up, moment_down, moment_up, second_down, second_up,
):
    micros, per, features = inputs.shape[1:]
    slots, rank = holder_down.shape[2:4]
    tokens = micros * per
    owned = [array[0] for array in (master_down, master_up, moment_down, moment_up, second_down, second_up)]
    gradient, placed_down, placed_up = run_step(
        bounds,
        micro_counts,
        inputs[0].reshape(tokens, features),
        cotangent[0].reshape(tokens, features),
        holder_down[0, 0].reshape(slots * rank, features),
        holder_up[0, 0].reshape(slots * rank, features),
        owned,
        per,
    )
    new_down, new_up, *news = finish(placed_down, placed_up, gradient, owned)
    return (new_down[None, None], new_up[None, None], *[array[None] for array in news])


def solution(mesh):
    owned = P("section", None, ("replica", "tensor"))
    held = P("replica", "section", None, None, None)
    tokens = P("replica", None, "tensor", None)
    return jax.shard_map(
        on_device,
        mesh=mesh,
        in_specs=(tokens, tokens, P(), P(), held, held) + (owned,) * 6,
        out_specs=(held, held) + (owned,) * 6,
        check_vma=False,
    )
```

```python
import functools
import math

import jax
import jax.numpy as jnp
from jax import lax
from jax.experimental import pallas as pl
from jax.experimental.pallas import tpu as pltpu
from jax.sharding import PartitionSpec as P

norm_eps = 1e-06
learn_rate = 0.01
beta_one = 0.9
beta_two = 0.95
decay_rate = 0.1
adam_eps = 1e-08
first_fix = 0.9999734386011124
second_fix = 0.9940794707796659


def dot_t(left, right):
    return lax.dot_general(
        left, right, (((1,), (1,)), ((), ())), preferred_element_type=jnp.float32
    )


def dot_n(left, right):
    return jnp.dot(left, right, preferred_element_type=jnp.float32)


MESH = pl.DeviceIdType.MESH


def place():
    tensor = lax.axis_index("tensor")
    return lax.axis_index("replica"), lax.axis_index("section"), tensor // 2, tensor % 2


def remote(source, target, sems, at, device):
    return pltpu.make_async_remote_copy(
        src_ref=source, dst_ref=target, send_sem=sems[0].at[at], recv_sem=sems[1].at[at],
        device_id=device, device_id_type=MESH,
    )


def section_peers(replica, section, chip, core, sections):
    return [(replica, lax.rem(section + d, sections), chip * 2 + core) for d in range(1, sections)]


def plane_peers(replica, section, chip, core, replicas):
    found = []
    for dr in range(replicas):
        for dz in range(2):
            for dc in range(2):
                if dr or dz or dc:
                    there = lax.rem(replica + dr, replicas)
                    tensor = lax.rem(chip + dz, 2) * 2 + lax.rem(core + dc, 2)
                    found.append(((there, section, tensor), there * 4 + tensor))
    return found


def piece_sum(box):
    total = box[0].astype(jnp.float32)
    for i in range(1, box.shape[0]):
        total = total + box[i].astype(jnp.float32)
    return total


def cut(value, pieces):
    _, height, width = pieces.shape
    across = value.shape[1] // width
    for i in range(pieces.shape[0]):
        y, x = i // across * height, i % across * width
        pieces[i] = value[y : y + height, x : x + width].astype(pieces.dtype)


def join(spread, whole):
    height, width = spread.shape[-2:]
    across = whole.shape[-1] // width
    for i in range(spread.shape[0]):
        y, x = i // across * height, i % across * width
        whole[..., y : y + height, x : x + width] = spread[i]


def dma_pairs(counts):
    return [pltpu.SemaphoreType.DMA((n,)) for n in counts for _ in range(2)]


def decayed(params, moments, seconds, gradient):
    new_moments = beta_one * moments + (1.0 - beta_one) * gradient
    new_seconds = beta_two * seconds + (1.0 - beta_two) * gradient * gradient
    new_params = params - learn_rate * (
        new_moments / first_fix / (jnp.sqrt(new_seconds / second_fix) + adam_eps)
        + decay_rate * params
    )
    return new_params, new_moments, new_seconds


def run_layers(features, tokens_per, section, counted, z, square, gram, coef, mixing, hb, rate, a_s, w_s, a_all):
    layers, packed, wide = z.shape
    rank, tokens = wide // 2, packed * 2 // 3
    root = 1.0 / math.sqrt(features)
    row = lax.broadcasted_iota(jnp.int32, (tokens, 1), 0)
    taken = row < counted * tokens_per

    def picked(kind, layer):
        if kind < 2:
            found = z[layer, :tokens, kind * rank : (kind + 1) * rank]
        else:
            found = jnp.concatenate([z[layer, tokens:, :rank], z[layer, tokens:, rank:]], axis=0)
        return found.astype(jnp.float32)

    norm = square[...]
    state = jnp.concatenate([picked(1, l) for l in range(layers)], axis=1)
    a_all[...] = jnp.zeros_like(a_all)
    slopes, inner, rhos = [], [], []
    for l in range(layers):
        at = slice(l * rank, (l + 1) * rank)
        hb[l] = state
        rho = lax.rsqrt(jnp.maximum(norm, 0.0) * (1.0 / features) + norm_eps)
        product = picked(0, l)
        if l:
            product = product + dot_t(a_all[...], gram[l, :rank])
        u = product * (rho * root)
        sigma = jax.nn.sigmoid(u)
        active = (u * sigma * (1.0 / math.sqrt(rank))).astype(jnp.bfloat16)
        a_s[l] = active
        a_all[:, at] = active
        added = dot_n(active, gram[l, rank:])
        wide_a = active.astype(jnp.float32)
        norm = norm + jnp.sum(wide_a * (2.0 * state[:, at] + added[:, at]), axis=1, keepdims=True)
        state = state + added
        slopes.append(sigma * (1.0 + u * (1.0 - sigma)) * (1.0 / math.sqrt(rank)))
        inner.append(u)
        rhos.append(rho)
    back = jnp.concatenate(
        [jnp.where(taken, picked(2, l), 0.0) for l in range(layers)], axis=1
    )
    gamma = jnp.zeros((tokens, 1), jnp.float32)
    for l in reversed(range(layers)):
        at = slice(l * rank, (l + 1) * rank)
        e = back[:, at] * slopes[l]
        rho = rhos[l]
        w = (e * (rho * root)).astype(jnp.bfloat16)
        w_s[l] = w
        rate[l] = gamma
        c = rho * rho * jnp.sum(e * inner[l], axis=1, keepdims=True) * (1.0 / features)
        gamma = gamma + c
        if l:
            back = back + dot_n(w, gram[l, :rank]) - c * hb[l]
    own_w = w_s[section].astype(jnp.float32)
    own_a = a_s[section].astype(jnp.float32)
    own_rate = rate[section]
    nothing = jnp.zeros((tokens, rank), jnp.float32)
    left = jnp.concatenate(
        [
            jnp.concatenate([own_w, -own_rate * own_a], axis=1),
            jnp.concatenate([nothing, jnp.where(taken, own_a, 0.0)], axis=1),
        ],
        axis=0,
    )
    coef[...] = left.T.astype(jnp.bfloat16)
    own_left = own_a.T.astype(jnp.bfloat16)
    own_down = own_w.T.astype(jnp.bfloat16)
    before = jnp.concatenate([jnp.where(l < section, a_s[l], jnp.zeros_like(a_s[l])) for l in range(layers)], axis=1)
    beyond = jnp.concatenate([jnp.where(l > section, w_s[l], jnp.zeros_like(w_s[l])) for l in range(layers)], axis=1)
    scaled = jnp.concatenate(
        [
            (jnp.where(l <= section, own_rate, rate[l]) * a_s[l].astype(jnp.float32)).astype(jnp.bfloat16)
            for l in range(layers)
        ],
        axis=1,
    )
    mixing[:rank] = (dot_n(own_down, before) + dot_n(own_left, beyond)).astype(jnp.bfloat16)
    mixing[rank:] = (-dot_n(own_left, scaled)).astype(jnp.bfloat16)


def publish(replicas, sections, share, out, far_sems, core_sems):
    replica, section, chip, core = place()
    columns = share.shape[1]
    before = lax.rem(section + sections - 1, sections)
    other = 1 - chip
    up, down, across = (lax.rem(replica + d, replicas) for d in (1, replicas - 1, 2))
    tensor = chip * 2 + core
    sibling = (replica, section, chip * 2 + 1 - core)
    partner = (replica, section, other * 2 + core)
    above, below = (up, section, tensor), (down, section, tensor)
    rank = share.shape[0] // 2

    def columns_of(r, z):
        return pl.ds(pl.multiple_of((r * 4 + z * 2 + core) * columns, 128), columns)

    def block(window, r, z):
        return out.at[window, :, columns_of(r, z)]

    started = {}
    def send(number, piece, device):
        copy = remote(piece, piece, far_sems, number, device)
        copy.start()
        started[number] = copy

    def landed(*numbers):
        for number in numbers:
            started[number].wait_recv()

    swaps = []

    def swap(window, r, z):
        copy = remote(block(window, r, z), block(window, r, z), core_sems, len(swaps), sibling)
        copy.start()
        swaps.append(copy)

    few = rank // 2

    def some(start, stop, r, z):
        return out.at[0, pl.ds(start, stop - start), columns_of(r, z)]

    def half(which, r):
        return some(which * rank, (which + 1) * rank, r, chip)

    def rest(r):
        return some(few, 2 * rank, r, chip)

    def early(r):
        return some(0, few, r, other)

    own = columns_of(replica, chip)
    for number, device in ((3, (replica, before, tensor)), (4, (replica, before, other * 2 + core))):
        started[number] = remote(share, out.at[1, :, own], far_sems, number, device)
        pl.when(section > 0)(started[number].start)

    @pl.when(section == sections - 1)
    def _():
        out[1, :, own] = share[...]
        out[1, :, columns_of(replica, other)] = share[...]

    out[0, :, own] = share[...]
    send(0, block(0, replica, chip), above)
    send(1, block(0, replica, chip), below)
    swap(0, replica, chip)
    pl.when(section < sections - 1)(started[3].wait_recv)
    send(9, block(1, replica, chip), above)
    send(10, block(1, replica, chip), below)
    send(2, block(0, replica, chip), partner)
    landed(0)
    send(5, half(0, down), above)
    send(6, rest(down), partner)
    landed(1)
    send(7, half(1, up), below)
    send(8, rest(up), partner)
    pl.when(section < sections - 1)(started[4].wait_recv)
    send(11, block(1, replica, other), above)
    send(12, block(1, replica, other), below)
    swap(0, down, chip)
    swap(0, up, chip)
    swap(1, replica, chip)
    swap(1, replica, other)
    landed(2)
    send(17, early(replica), above)
    send(18, early(replica), below)
    swap(0, replica, other)
    landed(5)
    send(13, some(few, rank, across, chip), partner)
    landed(7)
    send(14, half(1, across), partner)
    swap(0, across, chip)
    landed(9)
    send(15, block(1, down, chip), above)
    swap(1, down, chip)
    landed(10)
    swap(1, up, chip)
    landed(12)
    send(16, block(1, up, other), below)
    swap(1, up, other)
    landed(11)
    swap(1, down, other)
    landed(18)
    send(19, early(up), below)
    landed(6, 17)
    swap(0, down, other)
    landed(8)
    swap(0, up, other)
    landed(15)
    swap(1, across, chip)
    landed(13, 14, 19)
    swap(0, across, other)
    landed(16)
    swap(1, across, other)
    for number, copy in started.items():
        if number in (3, 4):
            pl.when(section > 0)(copy.wait_send)
        else:
            copy.wait_send()
    for copy in swaps:
        copy.wait()


COUNTS = dict(rows=7, zshift=1, z=7, gram=15, piece=7, plane=7, core=8, downs=7, mix=15, mixed=15, half=8, chip=14, far=20, swap=16)


def step_kernel(
    replicas, sections, tokens_per,
    bounds_hbm, counts_hbm, hidden_hbm, last_hbm, downs_hbm, ups_hbm, *refs,
):
    owned_hbm, refs = refs[:6], refs[6:]
    step_body(
        replicas, sections, tokens_per, bounds_hbm, counts_hbm, hidden_hbm, last_hbm, downs_hbm, ups_hbm, owned_hbm, *refs
    )


def step_body(
    replicas, sections, tokens_per, bounds_hbm, counts_hbm, hidden_hbm, last_hbm, downs_hbm, ups_hbm, owned_hbm,
    gradient, placed_down, placed_up,
    bounds, counts, owned, out, both, weights, mine, z, z_before, acc, zs, rows, down_rows, gram, pieces, box, spread,
    coef, mixing, hb, rate, a_s, w_s, a_all, mix_pieces, mix_box, mix_spread,
    parts, half, chips, inbox, late, share, local, *sems,
):
    sem = {name: sems[2 * i : 2 * i + 2] for i, name in enumerate(COUNTS)}
    replica, section, chip, core = place()
    tensor = chip * 2 + core
    me = replica * 4 + tensor
    _, rank, columns = owned.shape
    master_down, master_up, moment_down, moment_up, second_down, second_up = (owned.at[i] for i in range(6))
    wide = 2 * rank
    tokens, features = both.shape[0] // 2, both.shape[1]
    hidden, last = both.at[pl.ds(0, tokens)], both.at[pl.ds(tokens, tokens)]
    along = section_peers(replica, section, chip, core, sections)
    peers = plane_peers(replica, section, chip, core, replicas)
    sibling = (replica, section, chip * 2 + 1 - core)

    loads = [
        pltpu.make_async_copy(downs_hbm, weights.at[pl.ds(0, wide)], local.at[0]),
        pltpu.make_async_copy(ups_hbm, weights.at[pl.ds(wide, wide)], local.at[1]),
        pltpu.make_async_copy(hidden_hbm, hidden, local.at[2]),
        pltpu.make_async_copy(last_hbm, last, local.at[3]),
    ]
    barrier = pltpu.get_barrier_semaphore()
    everyone = along + [device for device, _ in peers]
    for d in (1, sections - 1):
        everyone.append((replica, lax.rem(section + d, sections), (1 - chip) * 2 + core))
    for device in everyone:
        pl.semaphore_signal(barrier, inc=1, device_id=device, device_id_type=MESH)
    firsts = [pltpu.make_async_copy(owned_hbm[i], owned.at[i], local.at[4 + i]) for i in range(6)]
    firsts.append(pltpu.make_async_copy(bounds_hbm, bounds, local.at[10]))
    firsts.append(pltpu.make_async_copy(counts_hbm, counts, local.at[11]))
    for copy in firsts + loads:
        copy.start()
    for copy in firsts:
        copy.wait()
    mine[:rank] = master_down[...].astype(mine.dtype)
    mine[rank:] = master_up[...].astype(mine.dtype)
    pl.semaphore_wait(barrier, len(everyone))

    row_copies = []
    for i, device in enumerate(along):
        row_copies.append(remote(mine.at[pl.ds(rank, rank)], rows.at[section], sem["rows"], i, device))
        row_copies[-1].start()
    rows[section] = mine[rank:]

    for copy in loads:
        copy.wait()
    acc[...] = jnp.zeros_like(acc)
    step = 1024

    @pl.loop(0, features // step)
    def _(i):
        at = pl.ds(pl.multiple_of(i * step, step), step)
        chunk = hidden[:, at]
        acc[:, : 2 * wide] += dot_t(chunk, weights[:, at])
        acc[:, 2 * wide : 3 * wide] += dot_t(last[:, at], weights[wide:, at])
        squares = chunk.astype(jnp.float32)
        squares = squares * squares
        folded = squares[:, :128]
        for j in range(1, step // 128):
            folded = folded + squares[:, j * 128 : (j + 1) * 128]
        acc[:, 3 * wide :] += folded

    for kind in range(3):
        z[kind] = acc[:, kind * wide : (kind + 1) * wide].astype(z.dtype)
    z_shift = remote(z, z_before, sem["zshift"], 0, along[0])
    z_shift.start()

    for copy in row_copies:
        copy.wait()
    cut(dot_t(mine[...], rows[...].reshape(sections * rank, columns)), pieces)
    copies = []
    for i, (device, number) in enumerate(peers):
        copies.append(remote(pieces.at[number], box.at[me], sem["gram"], i, device))
        copies[-1].start()
    box[me] = pieces[me]
    z_shift.wait()
    here = (bounds[replica, section] == section) & (bounds[replica, section + 1] > section)
    alone = bounds[replica, jnp.maximum(section - 1, 0)] == section
    own = []
    for kind in range(3):
        moved = jnp.where(alone, z_before[kind][:, :rank], z_before[kind][:, rank:])
        own.append(jnp.where(here, z[kind][:, :rank], moved))
    zs[section, :tokens] = jnp.concatenate(own[:2], axis=1)
    zs[section, tokens:] = jnp.concatenate([own[2][: tokens // 2], own[2][tokens // 2 :]], axis=1)
    z_copies = []
    for i, device in enumerate(along):
        z_copies.append(remote(zs.at[section], zs.at[section], sem["z"], i, device))
        z_copies[-1].start()
    for copy in copies:
        copy.wait()
    spread[me, section] = piece_sum(box).astype(spread.dtype)
    copies = []
    for i, device in enumerate(along):
        copies.append(remote(spread.at[me, section], spread.at[me, section], sem["piece"], i, device))
        copies[-1].start()
    for copy in copies:
        copy.wait()
    partner = (replica, section, (1 - chip) * 2 + core)
    theirs = replica * 4 + (1 - chip) * 2 + core
    copies, swaps = [], []

    def spread_to(number, device):
        copies.append(remote(spread.at[number], spread.at[number], sem["plane"], len(copies), device))
        copies[-1].start()

    def spread_swap(number):
        swaps.append(remote(spread.at[number], spread.at[number], sem["core"], len(swaps), sibling))
        swaps[-1].start()

    spread_to(me, partner)
    distances = (2, 1, 3)
    for dr in distances:
        spread_to(me, (lax.rem(replica + dr, replicas), section, tensor))
    spread_swap(me)
    copies[0].wait_recv()
    for dr in distances:
        spread_to(theirs, (lax.rem(replica + dr, replicas), section, tensor))
    spread_swap(theirs)
    for i, z_at in ((1, chip), (4, 1 - chip)):
        for j, dr in enumerate(distances):
            copies[i + j].wait_recv()
            spread_swap(lax.rem(replica + replicas - dr, replicas) * 4 + z_at * 2 + core)
    for copy in copies:
        copy.wait_send()
    for copy in z_copies:
        copy.wait()
    down_copies = []
    for i, device in enumerate(along):
        down_copies.append(remote(mine.at[pl.ds(0, rank)], down_rows.at[section], sem["downs"], i, device))
        down_copies[-1].start()
    down_rows[section] = mine[:rank]
    for copy in swaps:
        copy.wait()
    join(spread, gram)

    square = jnp.sum(acc[:, 3 * wide :], axis=1, keepdims=True)
    run_layers(
        features, tokens_per, section, counts[replica], zs, square, gram, coef, mixing, hb, rate, a_s, w_s, a_all
    )

    cut(mixing[...], mix_pieces)
    mix_copies = []
    for i, (device, number) in enumerate(peers):
        mix_copies.append(remote(mix_pieces.at[number], mix_box.at[me], sem["mix"], i, device))
        mix_copies[-1].start()
    mix_box[me] = mix_pieces[me]
    order = [(2, 1), (2, 0), (1, 1), (1, 0), (3, 1), (3, 0), (0, 1), (0, 0)]
    first, second = pl.ds(0, rank), pl.ds(rank, rank)

    def ring(dr):
        return (lax.rem(replica + dr, replicas), section, tensor)

    def block_gradient(dr, dz, c):
        number = lax.rem(replica + dr, replicas) * 4 + lax.rem(chip + dz, 2) * 2 + c
        at = pl.ds(pl.multiple_of(number * columns, 128), columns)
        return dot_n(coef[...], both[:, at])

    halves = []
    sends = {}

    def send(number, source, target, device):
        sends[number] = remote(source, target, sem["chip"], number, device)
        sends[number].start()

    for i in range(len(order) + 1):
        if i < len(order):
            parts[i] = block_gradient(*order[i], 1 - core).astype(parts.dtype)
            halves.append(remote(parts.at[i], half.at[i], sem["half"], i, sibling))
            halves[-1].start()
        if i:
            dr, dz = order[i - 1]
            added = block_gradient(dr, dz, core)
            halves[i - 1].wait()
            chips[i - 1] = (added + half[i - 1].astype(jnp.float32)).astype(chips.dtype)
            if dr:
                send(i - 1, chips.at[i - 1, first], inbox.at[i - 1, first], ring(dr))
            if dz:
                send(6 + dr, chips.at[i - 1, second], inbox.at[i - 1, second], partner)
    at = {distance: i for i, distance in enumerate(order)}

    for dr in (2, 1, 3):
        sends[6 + dr].wait_recv()
        i = at[dr, 1]
        parts[i, second] = (chips[at[dr, 0], second].astype(jnp.float32) + inbox[i, second].astype(jnp.float32)).astype(
            parts.dtype
        )
        send(9 + dr, parts.at[i, second], late.at[dr], ring(dr))
    for dz in (1, 0):
        total = chips[at[0, dz], first].astype(jnp.float32)
        for dr in (2, 1, 3):
            sends[at[dr, dz]].wait_recv()
            total = total + inbox[at[dr, dz], first].astype(jnp.float32)
        if dz:
            parts[at[0, 1], first] = total.astype(parts.dtype)
            send(13, parts.at[at[0, 1], first], late.at[0], partner)
        else:
            kept = total
    for copy in mix_copies:
        copy.wait()
    mix_spread[me] = piece_sum(mix_box).astype(mix_spread.dtype)
    mix_copies = []
    for i, (device, number) in enumerate(peers):
        mix_copies.append(remote(mix_spread.at[me], mix_spread.at[me], sem["mixed"], i, device))
        mix_copies[-1].start()
    for copy in mix_copies:
        copy.wait()
    join(mix_spread, mixing)
    for copy in down_copies:
        copy.wait()
    layer_of = lax.broadcasted_iota(jnp.int32, (rank, sections * rank), 1) // rank
    crossing = mixing[:rank]
    nothing = jnp.zeros_like(crossing)
    ups_all = rows[...].reshape(sections * rank, columns)
    downs_all = down_rows[...].reshape(sections * rank, columns)
    gradient[:rank] = dot_n(jnp.where(layer_of < section, crossing, nothing), ups_all)
    gradient[rank:] = dot_n(mixing[rank:], ups_all) + dot_n(
        jnp.where(layer_of > section, crossing, nothing), downs_all
    )
    sends[6].wait_recv()
    total = chips[at[0, 0], second].astype(jnp.float32) + inbox[at[0, 1], second].astype(jnp.float32)
    for dr in (2, 1, 3):
        sends[9 + dr].wait_recv()
        total = total + late[dr].astype(jnp.float32)
    gradient[rank:] += total
    sends[13].wait_recv()
    gradient[:rank] += kept + late[0].astype(jnp.float32)
    for copy in sends.values():
        copy.wait_send()
    share[:rank] = decayed(master_down[...], moment_down[...], second_down[...], gradient[:rank])[0].astype(share.dtype)
    share[rank:] = decayed(master_up[...], moment_up[...], second_up[...], gradient[rank:])[0].astype(share.dtype)
    publish(replicas, sections, share, out, sem["far"], sem["swap"])
    begin, end = bounds[replica, section], bounds[replica, section + 1]
    held, both, own = end > begin, end > begin + 1, begin == section

    @pl.loop(0, features // step)
    def _(i):
        at = pl.ds(pl.multiple_of(i * step, step), step)
        for placed, rows_of in ((placed_down, first), (placed_up, second)):
            this, following = out[0, rows_of, at], out[1, rows_of, at]
            none = jnp.zeros_like(this)
            placed[0, :, at] = jnp.where(held, jnp.where(own, this, following), none)
            placed[1, :, at] = jnp.where(both, following, none)


def run_step(bounds, counts, hidden, last, downs, ups, owned, tokens_per):
    replicas, sections = lax.axis_size("replica"), lax.axis_size("section")
    rank, columns = owned[0].shape
    wide, layers = 2 * rank, sections
    tokens, features = hidden.shape
    size = replicas * 4
    height, width = 16, wide * layers * rank // size // 16
    b16, f32 = jnp.bfloat16, jnp.float32
    hbm, vmem = (pl.BlockSpec(memory_space=m) for m in (pltpu.HBM, pltpu.VMEM))
    piece = pltpu.VMEM((size, height, width), b16)
    block = pltpu.VMEM((size // 2, wide, columns), b16)
    return pl.pallas_call(
        functools.partial(step_kernel, replicas, sections, tokens_per),
        out_shape=(
            jax.ShapeDtypeStruct((wide, columns), f32),
            jax.ShapeDtypeStruct((2, rank, features), b16),
            jax.ShapeDtypeStruct((2, rank, features), b16),
        ),
        in_specs=[hbm] * 12,
        out_specs=(vmem,) * 3,
        scratch_shapes=[
            pltpu.SMEM(bounds.shape, jnp.int32),
            pltpu.SMEM(counts.shape, jnp.int32),
            pltpu.VMEM((6, rank, columns), f32),
            pltpu.VMEM((2, wide, features), b16),
            pltpu.VMEM((2 * tokens, features), b16),
            pltpu.VMEM((2 * wide, features), b16),
            pltpu.VMEM((wide, columns), b16),
            pltpu.VMEM((3, tokens, wide), b16),
            pltpu.VMEM((3, tokens, wide), b16),
            pltpu.VMEM((tokens, 3 * wide + 128), f32),
            pltpu.VMEM((layers, tokens * 3 // 2, wide), b16),
            pltpu.VMEM((layers, rank, columns), b16),
            pltpu.VMEM((layers, rank, columns), b16),
            pltpu.VMEM((layers, wide, layers * rank), b16),
            piece,
            piece,
            pltpu.VMEM((size, sections, height, width), b16),
            pltpu.VMEM((wide, 2 * tokens), b16),
            pltpu.VMEM((wide, layers * rank), b16),
            pltpu.VMEM((layers, tokens, layers * rank), f32),
            pltpu.VMEM((layers, tokens, 1), f32),
            pltpu.VMEM((layers, tokens, rank), b16),
            pltpu.VMEM((layers, tokens, rank), b16),
            pltpu.VMEM((tokens, layers * rank), b16),
            piece,
            piece,
            piece,
            block,
            block,
            block,
            block,
            pltpu.VMEM((replicas, rank, columns), b16),
            pltpu.VMEM((wide, columns), b16),
            pltpu.SemaphoreType.DMA((12,)),
        ]
        + dma_pairs(COUNTS.values()),
        compiler_params=pltpu.CompilerParams(collective_id=1, has_side_effects=True, vmem_limit_bytes=42 * 2**20),
        name="step",
    )(*[pltpu.with_memory_space_constraint(array, pltpu.HBM) for array in (bounds, counts, hidden, last, downs, ups, *owned)])


def finish_kernel(placed_down, placed_up, gradient, *refs):
    owned, (new_down, new_up), news = refs[:6], refs[6:8], refs[8:14]
    held, sems = refs[14:]
    copies = [
        pltpu.make_async_copy(placed_down, new_down, sems.at[0]),
        pltpu.make_async_copy(placed_up, new_up, sems.at[1]),
    ]
    for copy in copies:
        copy.start()
    rank = owned[0].shape[0]
    for kind in range(2):
        rows = slice(kind * rank, (kind + 1) * rank)
        values = decayed(owned[kind][...], owned[2 + kind][...], owned[4 + kind][...], gradient[rows])
        for i, value in enumerate(values):
            number = 2 * i + kind
            held[number] = value
            copies.append(pltpu.make_async_copy(held.at[number], news[number], sems.at[2 + number]))
            copies[-1].start()
    for copy in copies:
        copy.wait()


def finish(placed_down, placed_up, gradient, owned):
    hbm, vmem = (pl.BlockSpec(memory_space=m) for m in (pl.ANY, pltpu.VMEM))
    like = [jax.ShapeDtypeStruct(array.shape, array.dtype) for array in (placed_down, placed_up, *owned)]
    return pl.pallas_call(
        finish_kernel,
        out_shape=like,
        in_specs=[vmem] * 9,
        out_specs=[hbm] * 8,
        scratch_shapes=[pltpu.VMEM((6,) + owned[0].shape, jnp.float32), pltpu.SemaphoreType.DMA((8,))],
        compiler_params=pltpu.CompilerParams(vmem_limit_bytes=16 * 2**20),
        name="finish",
    )(placed_down, placed_up, gradient, *owned)


def on_device(
    inputs, cotangent, micro_counts, bounds, holder_down, holder_up,
    master_down, master_up, moment_down, moment_up, second_down, second_up,
):
    micros, per, features = inputs.shape[1:]
    slots, rank = holder_down.shape[2:4]
    tokens = micros * per
    owned = [array[0] for array in (master_down, master_up, moment_down, moment_up, second_down, second_up)]
    gradient, placed_down, placed_up = run_step(
        bounds,
        micro_counts,
        inputs[0].reshape(tokens, features),
        cotangent[0].reshape(tokens, features),
        holder_down[0, 0].reshape(slots * rank, features),
        holder_up[0, 0].reshape(slots * rank, features),
        owned,
        per,
    )
    new_down, new_up, *news = finish(placed_down, placed_up, gradient, owned)
    return (new_down[None, None], new_up[None, None], *[array[None] for array in news])


def solution(mesh):
    owned = P("section", None, ("replica", "tensor"))
    held = P("replica", "section", None, None, None)
    tokens = P("replica", None, "tensor", None)
    return jax.shard_map(
        on_device,
        mesh=mesh,
        in_specs=(tokens, tokens, P(), P(), held, held) + (owned,) * 6,
        out_specs=(held, held) + (owned,) * 6,
        check_vma=False,
    )
```

```python
import functools
import math

import jax
import jax.numpy as jnp
from jax import lax
from jax.experimental import pallas as pl
from jax.experimental.pallas import tpu as pltpu
from jax.sharding import PartitionSpec as P

norm_eps = 1e-06
learn_rate = 0.01
beta_one = 0.9
beta_two = 0.95
decay_rate = 0.1
adam_eps = 1e-08
first_fix = 0.9999734386011124
second_fix = 0.9940794707796659


def dot_t(left, right):
    return lax.dot_general(
        left, right, (((1,), (1,)), ((), ())), preferred_element_type=jnp.float32
    )


def dot_n(left, right):
    return jnp.dot(left, right, preferred_element_type=jnp.float32)


MESH = pl.DeviceIdType.MESH


def place():
    tensor = lax.axis_index("tensor")
    return lax.axis_index("replica"), lax.axis_index("section"), tensor // 2, tensor % 2


def remote(source, target, sems, at, device):
    return pltpu.make_async_remote_copy(
        src_ref=source, dst_ref=target, send_sem=sems[0].at[at], recv_sem=sems[1].at[at],
        device_id=device, device_id_type=MESH,
    )


def section_peers(replica, section, chip, core, sections):
    return [(replica, lax.rem(section + d, sections), chip * 2 + core) for d in range(1, sections)]


def plane_peers(replica, section, chip, core, replicas):
    found = []
    for dr in range(replicas):
        for dz in range(2):
            for dc in range(2):
                if dr or dz or dc:
                    there = lax.rem(replica + dr, replicas)
                    tensor = lax.rem(chip + dz, 2) * 2 + lax.rem(core + dc, 2)
                    found.append(((there, section, tensor), there * 4 + tensor))
    return found


def piece_sum(box):
    total = box[0].astype(jnp.float32)
    for i in range(1, box.shape[0]):
        total = total + box[i].astype(jnp.float32)
    return total


def cut(value, pieces):
    _, height, width = pieces.shape
    across = value.shape[1] // width
    for i in range(pieces.shape[0]):
        y, x = i // across * height, i % across * width
        pieces[i] = value[y : y + height, x : x + width].astype(pieces.dtype)


def join(spread, whole):
    height, width = spread.shape[-2:]
    across = whole.shape[-1] // width
    for i in range(spread.shape[0]):
        y, x = i // across * height, i % across * width
        whole[..., y : y + height, x : x + width] = spread[i]


def dma_pairs(counts):
    return [pltpu.SemaphoreType.DMA((n,)) for n in counts for _ in range(2)]


def decayed(params, moments, seconds, gradient):
    new_moments = beta_one * moments + (1.0 - beta_one) * gradient
    new_seconds = beta_two * seconds + (1.0 - beta_two) * gradient * gradient
    new_params = params - learn_rate * (
        new_moments / first_fix / (jnp.sqrt(new_seconds / second_fix) + adam_eps)
        + decay_rate * params
    )
    return new_params, new_moments, new_seconds


def run_layers(features, tokens_per, section, counted, z, square, gram, coef, mixing, hb, rate, a_s, w_s, a_all):
    layers, packed, wide = z.shape
    rank, tokens = wide // 2, packed * 2 // 3
    root = 1.0 / math.sqrt(features)
    row = lax.broadcasted_iota(jnp.int32, (tokens, 1), 0)
    taken = row < counted * tokens_per

    def picked(kind, layer):
        if kind < 2:
            found = z[layer, :tokens, kind * rank : (kind + 1) * rank]
        else:
            found = jnp.concatenate([z[layer, tokens:, :rank], z[layer, tokens:, rank:]], axis=0)
        return found.astype(jnp.float32)

    norm = square[...]
    state = jnp.concatenate([picked(1, l) for l in range(layers)], axis=1)
    a_all[...] = jnp.zeros_like(a_all)
    slopes, inner, rhos = [], [], []
    for l in range(layers):
        at = slice(l * rank, (l + 1) * rank)
        hb[l] = state
        rho = lax.rsqrt(jnp.maximum(norm, 0.0) * (1.0 / features) + norm_eps)
        product = picked(0, l)
        if l:
            product = product + dot_t(a_all[...], gram[l, :rank])
        u = product * (rho * root)
        sigma = jax.nn.sigmoid(u)
        active = (u * sigma * (1.0 / math.sqrt(rank))).astype(jnp.bfloat16)
        a_s[l] = active
        a_all[:, at] = active
        added = dot_n(active, gram[l, rank:])
        wide_a = active.astype(jnp.float32)
        norm = norm + jnp.sum(wide_a * (2.0 * state[:, at] + added[:, at]), axis=1, keepdims=True)
        state = state + added
        slopes.append(sigma * (1.0 + u * (1.0 - sigma)) * (1.0 / math.sqrt(rank)))
        inner.append(u)
        rhos.append(rho)
    back = jnp.concatenate(
        [jnp.where(taken, picked(2, l), 0.0) for l in range(layers)], axis=1
    )
    gamma = jnp.zeros((tokens, 1), jnp.float32)
    for l in reversed(range(layers)):
        at = slice(l * rank, (l + 1) * rank)
        e = back[:, at] * slopes[l]
        rho = rhos[l]
        w = (e * (rho * root)).astype(jnp.bfloat16)
        w_s[l] = w
        rate[l] = gamma
        c = rho * rho * jnp.sum(e * inner[l], axis=1, keepdims=True) * (1.0 / features)
        gamma = gamma + c
        if l:
            back = back + dot_n(w, gram[l, :rank]) - c * hb[l]
    own_w = w_s[section].astype(jnp.float32)
    own_a = a_s[section].astype(jnp.float32)
    own_rate = rate[section]
    nothing = jnp.zeros((tokens, rank), jnp.float32)
    left = jnp.concatenate(
        [
            jnp.concatenate([own_w, -own_rate * own_a], axis=1),
            jnp.concatenate([nothing, jnp.where(taken, own_a, 0.0)], axis=1),
        ],
        axis=0,
    )
    coef[...] = left.T.astype(jnp.bfloat16)
    own_left = own_a.T.astype(jnp.bfloat16)
    own_down = own_w.T.astype(jnp.bfloat16)
    before = jnp.concatenate([jnp.where(l < section, a_s[l], jnp.zeros_like(a_s[l])) for l in range(layers)], axis=1)
    beyond = jnp.concatenate([jnp.where(l > section, w_s[l], jnp.zeros_like(w_s[l])) for l in range(layers)], axis=1)
    scaled = jnp.concatenate(
        [
            (jnp.where(l <= section, own_rate, rate[l]) * a_s[l].astype(jnp.float32)).astype(jnp.bfloat16)
            for l in range(layers)
        ],
        axis=1,
    )
    mixing[:rank] = (dot_n(own_down, before) + dot_n(own_left, beyond)).astype(jnp.bfloat16)
    mixing[rank:] = (-dot_n(own_left, scaled)).astype(jnp.bfloat16)


def publish(replicas, sections, share, out, far_sems, core_sems):
    replica, section, chip, core = place()
    columns = share.shape[1]
    before = lax.rem(section + sections - 1, sections)
    other = 1 - chip
    up, down, across = (lax.rem(replica + d, replicas) for d in (1, replicas - 1, 2))
    tensor = chip * 2 + core
    sibling = (replica, section, chip * 2 + 1 - core)
    partner = (replica, section, other * 2 + core)
    above, below = (up, section, tensor), (down, section, tensor)
    rank = share.shape[0] // 2

    def columns_of(r, z):
        return pl.ds(pl.multiple_of((r * 4 + z * 2 + core) * columns, 128), columns)

    def block(window, r, z):
        return out.at[window, :, columns_of(r, z)]

    started = {}
    def send(number, piece, device):
        copy = remote(piece, piece, far_sems, number, device)
        copy.start()
        started[number] = copy

    def landed(*numbers):
        for number in numbers:
            started[number].wait_recv()

    swaps = []

    def swap(window, r, z):
        copy = remote(block(window, r, z), block(window, r, z), core_sems, len(swaps), sibling)
        copy.start()
        swaps.append(copy)

    few = rank // 2

    def some(start, stop, r, z):
        return out.at[0, pl.ds(start, stop - start), columns_of(r, z)]

    def half(which, r):
        return some(which * rank, (which + 1) * rank, r, chip)

    def rest(r):
        return some(few, 2 * rank, r, chip)

    def early(r):
        return some(0, few, r, other)

    own = columns_of(replica, chip)
    for number, device in ((3, (replica, before, tensor)), (4, (replica, before, other * 2 + core))):
        started[number] = remote(share, out.at[1, :, own], far_sems, number, device)
        pl.when(section > 0)(started[number].start)

    @pl.when(section == sections - 1)
    def _():
        out[1, :, own] = share[...]
        out[1, :, columns_of(replica, other)] = share[...]

    out[0, :, own] = share[...]
    send(0, block(0, replica, chip), above)
    send(1, block(0, replica, chip), below)
    swap(0, replica, chip)
    pl.when(section < sections - 1)(started[3].wait_recv)
    send(9, block(1, replica, chip), above)
    send(10, block(1, replica, chip), below)
    send(2, block(0, replica, chip), partner)
    landed(0)
    send(5, half(0, down), above)
    send(6, rest(down), partner)
    landed(1)
    send(7, half(1, up), below)
    send(8, rest(up), partner)
    pl.when(section < sections - 1)(started[4].wait_recv)
    send(11, block(1, replica, other), above)
    send(12, block(1, replica, other), below)
    swap(0, down, chip)
    swap(0, up, chip)
    swap(1, replica, chip)
    swap(1, replica, other)
    landed(2)
    send(17, early(replica), above)
    send(18, early(replica), below)
    swap(0, replica, other)
    landed(5)
    send(13, some(few, rank, across, chip), partner)
    landed(7)
    send(14, half(1, across), partner)
    swap(0, across, chip)
    landed(9)
    send(15, block(1, down, chip), above)
    swap(1, down, chip)
    landed(10)
    swap(1, up, chip)
    landed(12)
    send(16, block(1, up, other), below)
    swap(1, up, other)
    landed(11)
    swap(1, down, other)
    landed(18)
    send(19, early(up), below)
    landed(6, 17)
    swap(0, down, other)
    landed(8)
    swap(0, up, other)
    landed(15)
    swap(1, across, chip)
    landed(13, 14, 19)
    swap(0, across, other)
    landed(16)
    swap(1, across, other)
    for number, copy in started.items():
        if number in (3, 4):
            pl.when(section > 0)(copy.wait_send)
        else:
            copy.wait_send()
    for copy in swaps:
        copy.wait()


COUNTS = dict(rows=7, zshift=1, z=7, gram=15, piece=7, plane=7, core=8, downs=7, mix=15, mixed=15, half=8, chip=14, far=20, swap=16)


def step_kernel(
    replicas, sections, tokens_per,
    bounds_hbm, counts_hbm, hidden_hbm, last_hbm, downs_hbm, ups_hbm, *refs,
):
    owned_hbm, refs = refs[:6], refs[6:]
    step_body(
        replicas, sections, tokens_per, bounds_hbm, counts_hbm, hidden_hbm, last_hbm, downs_hbm, ups_hbm, owned_hbm, *refs
    )


def step_body(
    replicas, sections, tokens_per, bounds_hbm, counts_hbm, hidden_hbm, last_hbm, downs_hbm, ups_hbm, owned_hbm,
    gradient, placed_down, placed_up,
    bounds, counts, owned, out, both, weights, mine, z, z_before, acc, zs, rows, down_rows, gram, pieces, box, spread,
    coef, mixing, hb, rate, a_s, w_s, a_all, mix_pieces, mix_box, mix_spread,
    parts, half, chips, inbox, late, share, local, *sems,
):
    sem = {name: sems[2 * i : 2 * i + 2] for i, name in enumerate(COUNTS)}
    replica, section, chip, core = place()
    tensor = chip * 2 + core
    me = replica * 4 + tensor
    _, rank, columns = owned.shape
    master_down, master_up, moment_down, moment_up, second_down, second_up = (owned.at[i] for i in range(6))
    wide = 2 * rank
    tokens, features = both.shape[0] // 2, both.shape[1]
    hidden, last = both.at[pl.ds(0, tokens)], both.at[pl.ds(tokens, tokens)]
    along = section_peers(replica, section, chip, core, sections)
    peers = plane_peers(replica, section, chip, core, replicas)
    sibling = (replica, section, chip * 2 + 1 - core)

    loads = [
        pltpu.make_async_copy(downs_hbm, weights.at[pl.ds(0, wide)], local.at[0]),
        pltpu.make_async_copy(ups_hbm, weights.at[pl.ds(wide, wide)], local.at[1]),
        pltpu.make_async_copy(hidden_hbm, hidden, local.at[2]),
        pltpu.make_async_copy(last_hbm, last, local.at[3]),
    ]
    barrier = pltpu.get_barrier_semaphore()
    everyone = along + [device for device, _ in peers]
    for d in (1, sections - 1):
        everyone.append((replica, lax.rem(section + d, sections), (1 - chip) * 2 + core))
    for device in everyone:
        pl.semaphore_signal(barrier, inc=1, device_id=device, device_id_type=MESH)
    firsts = [pltpu.make_async_copy(owned_hbm[i], owned.at[i], local.at[4 + i]) for i in range(6)]
    firsts.append(pltpu.make_async_copy(bounds_hbm, bounds, local.at[10]))
    firsts.append(pltpu.make_async_copy(counts_hbm, counts, local.at[11]))
    for copy in firsts + loads:
        copy.start()
    for copy in firsts:
        copy.wait()
    mine[:rank] = master_down[...].astype(mine.dtype)
    mine[rank:] = master_up[...].astype(mine.dtype)
    pl.semaphore_wait(barrier, len(everyone))

    row_copies = []
    far_first = sorted(range(len(along)), key=lambda i: abs(i + 1 - sections // 2))
    for i in far_first:
        row_copies.append(remote(mine.at[pl.ds(rank, rank)], rows.at[section], sem["rows"], i, along[i]))
        row_copies[-1].start()
    rows[section] = mine[rank:]

    for copy in loads:
        copy.wait()
    acc[...] = jnp.zeros_like(acc)
    step = 1024

    @pl.loop(0, features // step)
    def _(i):
        at = pl.ds(pl.multiple_of(i * step, step), step)
        chunk = hidden[:, at]
        acc[:, : 2 * wide] += dot_t(chunk, weights[:, at])
        acc[:, 2 * wide : 3 * wide] += dot_t(last[:, at], weights[wide:, at])
        squares = chunk.astype(jnp.float32)
        squares = squares * squares
        folded = squares[:, :128]
        for j in range(1, step // 128):
            folded = folded + squares[:, j * 128 : (j + 1) * 128]
        acc[:, 3 * wide :] += folded

    for kind in range(3):
        z[kind] = acc[:, kind * wide : (kind + 1) * wide].astype(z.dtype)
    z_shift = remote(z, z_before, sem["zshift"], 0, along[0])
    z_shift.start()

    for copy in row_copies:
        copy.wait()
    cut(dot_t(mine[...], rows[...].reshape(sections * rank, columns)), pieces)
    copies = []
    for i, (device, number) in enumerate(peers):
        copies.append(remote(pieces.at[number], box.at[me], sem["gram"], i, device))
        copies[-1].start()
    box[me] = pieces[me]
    z_shift.wait()
    here = (bounds[replica, section] == section) & (bounds[replica, section + 1] > section)
    alone = bounds[replica, jnp.maximum(section - 1, 0)] == section
    own = []
    for kind in range(3):
        moved = jnp.where(alone, z_before[kind][:, :rank], z_before[kind][:, rank:])
        own.append(jnp.where(here, z[kind][:, :rank], moved))
    zs[section, :tokens] = jnp.concatenate(own[:2], axis=1)
    zs[section, tokens:] = jnp.concatenate([own[2][: tokens // 2], own[2][tokens // 2 :]], axis=1)
    z_copies = []
    for i, device in enumerate(along):
        z_copies.append(remote(zs.at[section], zs.at[section], sem["z"], i, device))
        z_copies[-1].start()
    for copy in copies:
        copy.wait()
    spread[me, section] = piece_sum(box).astype(spread.dtype)
    copies = []
    for i, device in enumerate(along):
        copies.append(remote(spread.at[me, section], spread.at[me, section], sem["piece"], i, device))
        copies[-1].start()
    for copy in copies:
        copy.wait()
    partner = (replica, section, (1 - chip) * 2 + core)
    theirs = replica * 4 + (1 - chip) * 2 + core
    copies, swaps = [], []

    def spread_to(number, device):
        copies.append(remote(spread.at[number], spread.at[number], sem["plane"], len(copies), device))
        copies[-1].start()

    def spread_swap(number):
        swaps.append(remote(spread.at[number], spread.at[number], sem["core"], len(swaps), sibling))
        swaps[-1].start()

    spread_to(me, partner)
    distances = (2, 1, 3)
    for dr in distances:
        spread_to(me, (lax.rem(replica + dr, replicas), section, tensor))
    spread_swap(me)
    copies[0].wait_recv()
    for dr in distances:
        spread_to(theirs, (lax.rem(replica + dr, replicas), section, tensor))
    spread_swap(theirs)
    for i, z_at in ((1, chip), (4, 1 - chip)):
        for j, dr in enumerate(distances):
            copies[i + j].wait_recv()
            spread_swap(lax.rem(replica + replicas - dr, replicas) * 4 + z_at * 2 + core)
    for copy in copies:
        copy.wait_send()
    for copy in z_copies:
        copy.wait()
    down_copies = []
    for i, device in enumerate(along):
        down_copies.append(remote(mine.at[pl.ds(0, rank)], down_rows.at[section], sem["downs"], i, device))
        down_copies[-1].start()
    down_rows[section] = mine[:rank]
    for copy in swaps:
        copy.wait()
    join(spread, gram)

    square = jnp.sum(acc[:, 3 * wide :], axis=1, keepdims=True)
    run_layers(
        features, tokens_per, section, counts[replica], zs, square, gram, coef, mixing, hb, rate, a_s, w_s, a_all
    )

    cut(mixing[...], mix_pieces)
    mix_copies = []
    for i, (device, number) in enumerate(peers):
        mix_copies.append(remote(mix_pieces.at[number], mix_box.at[me], sem["mix"], i, device))
        mix_copies[-1].start()
    mix_box[me] = mix_pieces[me]
    order = [(2, 1), (2, 0), (1, 1), (1, 0), (3, 1), (3, 0), (0, 1), (0, 0)]
    first, second = pl.ds(0, rank), pl.ds(rank, rank)

    def ring(dr):
        return (lax.rem(replica + dr, replicas), section, tensor)

    def block_gradient(dr, dz, c):
        number = lax.rem(replica + dr, replicas) * 4 + lax.rem(chip + dz, 2) * 2 + c
        at = pl.ds(pl.multiple_of(number * columns, 128), columns)
        return dot_n(coef[...], both[:, at])

    halves = []
    sends = {}

    def send(number, source, target, device):
        sends[number] = remote(source, target, sem["chip"], number, device)
        sends[number].start()

    for i in range(len(order) + 1):
        if i < len(order):
            parts[i] = block_gradient(*order[i], 1 - core).astype(parts.dtype)
            halves.append(remote(parts.at[i], half.at[i], sem["half"], i, sibling))
            halves[-1].start()
        if i:
            dr, dz = order[i - 1]
            added = block_gradient(dr, dz, core)
            halves[i - 1].wait()
            chips[i - 1] = (added + half[i - 1].astype(jnp.float32)).astype(chips.dtype)
            if dr:
                send(i - 1, chips.at[i - 1, first], inbox.at[i - 1, first], ring(dr))
            if dz:
                send(6 + dr, chips.at[i - 1, second], inbox.at[i - 1, second], partner)
    at = {distance: i for i, distance in enumerate(order)}

    for dr in (2, 1, 3):
        sends[6 + dr].wait_recv()
        i = at[dr, 1]
        parts[i, second] = (chips[at[dr, 0], second].astype(jnp.float32) + inbox[i, second].astype(jnp.float32)).astype(
            parts.dtype
        )
        send(9 + dr, parts.at[i, second], late.at[dr], ring(dr))
    for dz in (1, 0):
        total = chips[at[0, dz], first].astype(jnp.float32)
        for dr in (2, 1, 3):
            sends[at[dr, dz]].wait_recv()
            total = total + inbox[at[dr, dz], first].astype(jnp.float32)
        if dz:
            parts[at[0, 1], first] = total.astype(parts.dtype)
            send(13, parts.at[at[0, 1], first], late.at[0], partner)
        else:
            kept = total
    for copy in mix_copies:
        copy.wait()
    mix_spread[me] = piece_sum(mix_box).astype(mix_spread.dtype)
    mix_copies = []
    for i, (device, number) in enumerate(peers):
        mix_copies.append(remote(mix_spread.at[me], mix_spread.at[me], sem["mixed"], i, device))
        mix_copies[-1].start()
    for copy in mix_copies:
        copy.wait()
    join(mix_spread, mixing)
    for copy in down_copies:
        copy.wait()
    layer_of = lax.broadcasted_iota(jnp.int32, (rank, sections * rank), 1) // rank
    crossing = mixing[:rank]
    nothing = jnp.zeros_like(crossing)
    ups_all = rows[...].reshape(sections * rank, columns)
    downs_all = down_rows[...].reshape(sections * rank, columns)
    gradient[:rank] = dot_n(jnp.where(layer_of < section, crossing, nothing), ups_all)
    gradient[rank:] = dot_n(mixing[rank:], ups_all) + dot_n(
        jnp.where(layer_of > section, crossing, nothing), downs_all
    )
    sends[6].wait_recv()
    total = chips[at[0, 0], second].astype(jnp.float32) + inbox[at[0, 1], second].astype(jnp.float32)
    for dr in (2, 1, 3):
        sends[9 + dr].wait_recv()
        total = total + late[dr].astype(jnp.float32)
    gradient[rank:] += total
    sends[13].wait_recv()
    gradient[:rank] += kept + late[0].astype(jnp.float32)
    for copy in sends.values():
        copy.wait_send()
    share[:rank] = decayed(master_down[...], moment_down[...], second_down[...], gradient[:rank])[0].astype(share.dtype)
    share[rank:] = decayed(master_up[...], moment_up[...], second_up[...], gradient[rank:])[0].astype(share.dtype)
    publish(replicas, sections, share, out, sem["far"], sem["swap"])
    begin, end = bounds[replica, section], bounds[replica, section + 1]
    held, both, own = end > begin, end > begin + 1, begin == section

    @pl.loop(0, features // step)
    def _(i):
        at = pl.ds(pl.multiple_of(i * step, step), step)
        for placed, rows_of in ((placed_down, first), (placed_up, second)):
            this, following = out[0, rows_of, at], out[1, rows_of, at]
            none = jnp.zeros_like(this)
            placed[0, :, at] = jnp.where(held, jnp.where(own, this, following), none)
            placed[1, :, at] = jnp.where(both, following, none)


def run_step(bounds, counts, hidden, last, downs, ups, owned, tokens_per):
    replicas, sections = lax.axis_size("replica"), lax.axis_size("section")
    rank, columns = owned[0].shape
    wide, layers = 2 * rank, sections
    tokens, features = hidden.shape
    size = replicas * 4
    height, width = 16, wide * layers * rank // size // 16
    b16, f32 = jnp.bfloat16, jnp.float32
    hbm, vmem = (pl.BlockSpec(memory_space=m) for m in (pltpu.HBM, pltpu.VMEM))
    piece = pltpu.VMEM((size, height, width), b16)
    block = pltpu.VMEM((size // 2, wide, columns), b16)
    return pl.pallas_call(
        functools.partial(step_kernel, replicas, sections, tokens_per),
        out_shape=(
            jax.ShapeDtypeStruct((wide, columns), f32),
            jax.ShapeDtypeStruct((2, rank, features), b16),
            jax.ShapeDtypeStruct((2, rank, features), b16),
        ),
        in_specs=[hbm] * 12,
        out_specs=(vmem,) * 3,
        scratch_shapes=[
            pltpu.SMEM(bounds.shape, jnp.int32),
            pltpu.SMEM(counts.shape, jnp.int32),
            pltpu.VMEM((6, rank, columns), f32),
            pltpu.VMEM((2, wide, features), b16),
            pltpu.VMEM((2 * tokens, features), b16),
            pltpu.VMEM((2 * wide, features), b16),
            pltpu.VMEM((wide, columns), b16),
            pltpu.VMEM((3, tokens, wide), b16),
            pltpu.VMEM((3, tokens, wide), b16),
            pltpu.VMEM((tokens, 3 * wide + 128), f32),
            pltpu.VMEM((layers, tokens * 3 // 2, wide), b16),
            pltpu.VMEM((layers, rank, columns), b16),
            pltpu.VMEM((layers, rank, columns), b16),
            pltpu.VMEM((layers, wide, layers * rank), b16),
            piece,
            piece,
            pltpu.VMEM((size, sections, height, width), b16),
            pltpu.VMEM((wide, 2 * tokens), b16),
            pltpu.VMEM((wide, layers * rank), b16),
            pltpu.VMEM((layers, tokens, layers * rank), f32),
            pltpu.VMEM((layers, tokens, 1), f32),
            pltpu.VMEM((layers, tokens, rank), b16),
            pltpu.VMEM((layers, tokens, rank), b16),
            pltpu.VMEM((tokens, layers * rank), b16),
            piece,
            piece,
            piece,
            block,
            block,
            block,
            block,
            pltpu.VMEM((replicas, rank, columns), b16),
            pltpu.VMEM((wide, columns), b16),
            pltpu.SemaphoreType.DMA((12,)),
        ]
        + dma_pairs(COUNTS.values()),
        compiler_params=pltpu.CompilerParams(collective_id=1, has_side_effects=True, vmem_limit_bytes=42 * 2**20),
        name="step",
    )(*[pltpu.with_memory_space_constraint(array, pltpu.HBM) for array in (bounds, counts, hidden, last, downs, ups, *owned)])


def finish_kernel(placed_down, placed_up, gradient, *refs):
    owned, (new_down, new_up), news = refs[:6], refs[6:8], refs[8:14]
    held, sems = refs[14:]
    copies = [
        pltpu.make_async_copy(placed_down, new_down, sems.at[0]),
        pltpu.make_async_copy(placed_up, new_up, sems.at[1]),
    ]
    for copy in copies:
        copy.start()
    rank = owned[0].shape[0]
    for kind in range(2):
        rows = slice(kind * rank, (kind + 1) * rank)
        values = decayed(owned[kind][...], owned[2 + kind][...], owned[4 + kind][...], gradient[rows])
        for i, value in enumerate(values):
            number = 2 * i + kind
            held[number] = value
            copies.append(pltpu.make_async_copy(held.at[number], news[number], sems.at[2 + number]))
            copies[-1].start()
    for copy in copies:
        copy.wait()


def finish(placed_down, placed_up, gradient, owned):
    hbm, vmem = (pl.BlockSpec(memory_space=m) for m in (pl.ANY, pltpu.VMEM))
    like = [jax.ShapeDtypeStruct(array.shape, array.dtype) for array in (placed_down, placed_up, *owned)]
    return pl.pallas_call(
        finish_kernel,
        out_shape=like,
        in_specs=[vmem] * 9,
        out_specs=[hbm] * 8,
        scratch_shapes=[pltpu.VMEM((6,) + owned[0].shape, jnp.float32), pltpu.SemaphoreType.DMA((8,))],
        compiler_params=pltpu.CompilerParams(vmem_limit_bytes=16 * 2**20),
        name="finish",
    )(placed_down, placed_up, gradient, *owned)


def on_device(
    inputs, cotangent, micro_counts, bounds, holder_down, holder_up,
    master_down, master_up, moment_down, moment_up, second_down, second_up,
):
    micros, per, features = inputs.shape[1:]
    slots, rank = holder_down.shape[2:4]
    tokens = micros * per
    owned = [array[0] for array in (master_down, master_up, moment_down, moment_up, second_down, second_up)]
    gradient, placed_down, placed_up = run_step(
        bounds,
        micro_counts,
        inputs[0].reshape(tokens, features),
        cotangent[0].reshape(tokens, features),
        holder_down[0, 0].reshape(slots * rank, features),
        holder_up[0, 0].reshape(slots * rank, features),
        owned,
        per,
    )
    new_down, new_up, *news = finish(placed_down, placed_up, gradient, owned)
    return (new_down[None, None], new_up[None, None], *[array[None] for array in news])


def solution(mesh):
    owned = P("section", None, ("replica", "tensor"))
    held = P("replica", "section", None, None, None)
    tokens = P("replica", None, "tensor", None)
    return jax.shard_map(
        on_device,
        mesh=mesh,
        in_specs=(tokens, tokens, P(), P(), held, held) + (owned,) * 6,
        out_specs=(held, held) + (owned,) * 6,
        check_vma=False,
    )
```
